32 devices in a mesh: dp: 16 (over z, x, core), fsdp: 2 (over y).
Axes of the slice: x: 2, y: 2, z: 4, core: 2. Of those that a mesh axis runs over, the one named last changes fastest.
Arguments:
- inputs: bfloat16 [64, 512, 512], P(('dp', 'fsdp')), may hold values from -6 to 6
- cotangent: bfloat16 [64, 512, 512], P(('dp', 'fsdp')), may hold values from -6 to 6
- segment_ids: int32 [64, 512], P(('dp', 'fsdp')), may hold values from 0 to 5, never falling along the last dimension, each value on 1 to 200 neighbouring positions
- qkv_weight: float32 [512, 1536], P('fsdp'), may hold values from -0.25 to 0.25
- proj_weight: float32 [512, 512], P('fsdp'), may hold values from -1 to 1
- up_weight: float32 [512, 2048], P('fsdp'), may hold values from -0.25 to 0.25
- down_weight: float32 [2048, 512], P('fsdp'), may hold values from -0.125 to 0.125
- vectors: float32 [12, 512], P('fsdp'), may hold values from -1.2 to 1.6, as said below
- qkv_moment: float32 [512, 1536], P('fsdp'), as said below
- proj_moment: float32 [512, 512], P('fsdp'), as said below
- up_moment: float32 [512, 2048], P('fsdp'), as said below
- down_moment: float32 [2048, 512], P('fsdp'), as said below
- vec_first: float32 [12, 512], P('fsdp'), as said below
- vec_second: float32 [12, 512], P('fsdp'), as said below
Outputs:
- layer_out: float32 [64, 512, 512], P(('dp', 'fsdp'))
- input_grad: float32 [64, 512, 512], P(('dp', 'fsdp'))
- qkv_moment_new: float32 [512, 1536], P('fsdp')
- proj_moment_new: float32 [512, 512], P('fsdp')
- up_moment_new: float32 [512, 2048], P('fsdp')
- down_moment_new: float32 [2048, 512], P('fsdp')
- qkv_weight_new: float32 [512, 1536], P('fsdp')
- proj_weight_new: float32 [512, 512], P('fsdp')
- up_weight_new: float32 [512, 2048], P('fsdp')
- down_weight_new: float32 [2048, 512], P('fsdp')
- vec_first_new: float32 [12, 512], P('fsdp')
- vec_second_new: float32 [12, 512], P('fsdp')
- vectors_new: float32 [12, 512], P('fsdp')
The draws below stay inside these ranges and needn't reach their ends.
Inputs may be any that keep to these rules, and one draw needn't show every extreme that they name: `segment_ids`: along each sequence the document numbers never fall; every number from 0 to 5 is used; a document has 1 to 200 tokens and one has exactly 200. `vectors`: gains near 1, biases of both signs. `qkv_moment`: entries of both signs. `proj_moment`: entries of both signs. `up_moment`: entries of both signs. `down_moment`: entries of both signs. `vec_first`: entries of both signs. `vec_second`: positive entries.
All inputs are finite; a program needn't handle non-finite values.
Results may differ from the reference program's by a relative error of at most 0.014.
Values may be sent and summed in bfloat16 or wider, within the bound.
No kernel may reach another device: no remote copies, remote signals or barrier semaphores. Data moves between devices by JAX's collectives and lax.ppermute only.
A program may use at most 192 MiB of HBM per device.

```python
import math
import jax
import jax.numpy as jnp
import numpy as np
from jax import lax

D = 512
HEADS = 8
FF = 2048
HD = 64
SEQ = 512
DOCMAX = 200
DOCS = 6
NS_ITERS = 5
STEP = 10
VROWS = 12
SEQS = 64
TOKENS = 32768


def row_scales():
    kinds = jnp.arange(VROWS)
    base = jnp.where(kinds == 0, 0.1, jnp.where(kinds < 3, 0.3, jnp.where(kinds < 6, 0.5, jnp.where(kinds < 8, 1.0, 0.3))))
    return base.astype(jnp.float32)


def clipped_normal(key, shape):
    return jnp.clip(jax.random.normal(key, shape, jnp.float32), -4.0, 4.0)


def moment_draw(key, rows, cols, factor):
    return factor * jnp.sqrt(jnp.float32(TOKENS)) * clipped_normal(key, (rows, cols))


def draw_vectors(key, part):
    key = jax.random.fold_in(key, 11)
    noise = clipped_normal(key, (VROWS, D))
    kinds = jnp.arange(VROWS)
    gains = (kinds == 3) | (kinds == 6)
    return jnp.where(gains[:, None], 1.0 + 0.15 * noise, 0.3 * noise)


def draw_vec_first(key, part):
    key = jax.random.fold_in(key, 12)
    return 0.11 * jnp.sqrt(jnp.float32(TOKENS)) * row_scales()[:, None] * clipped_normal(key, (VROWS, D))


def draw_vec_second(key, part):
    key = jax.random.fold_in(key, 13)
    spread = jax.random.uniform(key, (VROWS, D), jnp.float32, 1.0, 4.0)
    scales = row_scales()
    return 0.001 * jnp.float32(TOKENS) * (scales * scales)[:, None] * spread


def draw_qkv_moment(key, part):
    key = jax.random.fold_in(key, 21)
    return moment_draw(key, D, 3 * D, 0.1)


def draw_proj_moment(key, part):
    key = jax.random.fold_in(key, 22)
    return moment_draw(key, D, D, 0.2)


def draw_up_moment(key, part):
    key = jax.random.fold_in(key, 23)
    return moment_draw(key, D, FF, 0.3)


def draw_down_moment(key, part):
    key = jax.random.fold_in(key, 24)
    return moment_draw(key, FF, D, 0.3)


def level_of(rng, extent, shards, low, largest):
    factor_of = 1.0
    for position, parts in shards:
        steps = jax.random.uniform(jax.random.fold_in(jax.random.fold_in(rng, 6), position), (parts,), jnp.float32, low / len(shards), largest / len(shards))
        factor_of = factor_of * jnp.repeat(jnp.exp(steps), extent[position] // parts).reshape((-1,) + (1,) * (len(extent) - 1 - position))
    return factor_of


def split_up(amount, total, limit, lean):
    loads = [(1 << 20) // math.isqrt(rank ** lean) + 1 for rank in range(2, amount + 1)]
    rest, holding = total - limit - (amount - 1), [1] * (amount - 1)
    while rest > 0:
        free = [i for i in range(amount - 1) if holding[i] < limit]
        pool, budget = sum([loads[i] for i in free]), rest
        for i in free:
            extra = min(limit - holding[i], max(1, budget * loads[i] // pool), rest)
            holding[i] = holding[i] + extra
            rest = rest - extra
    return np.array([limit] + holding)


def uneven(stream_key, amount, total, reach, slope):
    if amount == 2:
        one = jax.random.randint(stream_key, (), max(1, total - reach), min(reach, total - 1) + 1)
        return jnp.stack([one, total - one])
    sizes = jnp.asarray(split_up(amount, total, reach, slope), jnp.int32)
    couples = (amount - 1) // 2
    donor, taker = sizes[1:1 + 2 * couples:2], sizes[2:2 + 2 * couples:2]
    margin = jnp.minimum(donor - 1, reach - taker)
    moved = jax.random.randint(jax.random.fold_in(stream_key, 1), (couples,), 0, 1 << 20) % (margin + 1)
    sizes = sizes.at[1:1 + 2 * couples:2].set(donor - moved).at[2:2 + 2 * couples:2].set(taker + moved)
    return sizes[jax.random.permutation(jax.random.fold_in(stream_key, 2), amount)]


def bell_draw(rng, dims, scale, bound, shards=(), held_as=jnp.bfloat16):
    values = scale * jax.random.normal(rng, dims, jnp.float32)
    if shards:
        values = values * level_of(rng, dims, shards, -0.22, 0.18)
    return jnp.clip(values, -bound, bound).astype(held_as)


def setup_inputs(seed: int = 0) -> dict:
    splits = jax.random.split(jax.random.key(seed), 15)
    inputs = bell_draw(splits[0], (SEQS, SEQ, D), 1.0, 6.0, ((0, 32),))
    cotangent = bell_draw(splits[1], (SEQS, SEQ, D), 1.0, 6.0, ((0, 32),))
    segment_ids = jax.vmap(lambda own: jnp.searchsorted(jnp.cumsum(uneven(own, DOCS, SEQ, DOCMAX, 1)), jnp.arange(SEQ), side="right"))(jax.random.split(splits[2], SEQS)).reshape((SEQS, SEQ)).astype(jnp.int32)
    qkv_weight = bell_draw(splits[3], (D, 3 * D), D ** -0.5, 0.25, ((0, 2),), jnp.float32)
    proj_weight = bell_draw(splits[4], (D, D), (D // 16) ** -0.5, 1.0, ((0, 2),), jnp.float32)
    up_weight = bell_draw(splits[5], (D, FF), D ** -0.5, 0.25, ((0, 2),), jnp.float32)
    down_weight = bell_draw(splits[6], (FF, D), FF ** -0.5, 0.125, ((0, 2),), jnp.float32)
    vectors = draw_vectors(jax.random.fold_in(splits[14], 71), 0)
    qkv_moment = draw_qkv_moment(jax.random.fold_in(splits[14], 71), 0)
    proj_moment = draw_proj_moment(jax.random.fold_in(splits[14], 71), 0)
    up_moment = draw_up_moment(jax.random.fold_in(splits[14], 71), 0)
    down_moment = draw_down_moment(jax.random.fold_in(splits[14], 71), 0)
    vec_first = draw_vec_first(jax.random.fold_in(splits[14], 71), 0)
    vec_second = draw_vec_second(jax.random.fold_in(splits[14], 71), 0)
    return {"inputs": inputs, "cotangent": cotangent, "segment_ids": segment_ids, "qkv_weight": qkv_weight, "proj_weight": proj_weight, "up_weight": up_weight, "down_weight": down_weight, "vectors": vectors, "qkv_moment": qkv_moment, "proj_moment": proj_moment, "up_moment": up_moment, "down_moment": down_moment, "vec_first": vec_first, "vec_second": vec_second}


@jax.custom_vjp
def low(v):
    return lax.optimization_barrier(v.astype(jnp.bfloat16)).astype(jnp.float32)

@jax.custom_vjp
def low_back(v):
    return v

def low_keep(v):
    return (low(v), None)

def low_pass(kept, grad):
    return (grad,)

def back_keep(v):
    return (v, None)

def back_low(kept, grad):
    return (low(grad),)
low.defvjp(low_keep, low_pass)
low_back.defvjp(back_keep, back_low)
norm_epsilon = 1e-12
momentum_decay = 0.95
muon_rate = 0.6
newton_a = 3.4445
newton_b = -4.775
newton_c = 2.0315
beta_first = 0.9
beta_second = 0.999
adam_rate = 0.2
weight_decay = 0.01
adam_epsilon = 1e-08
masked_score = -1e+30

def round_both(values):
    return low(low_back(values))

def matmul_high(left, right):
    return jnp.matmul(left, right, precision=lax.Precision.HIGHEST)

def norm_rows(values, gain, shift):
    center = values - lax.optimization_barrier(jnp.mean(values, -1, keepdims=True))
    variance = lax.optimization_barrier(jnp.mean(center * center, -1, keepdims=True))
    return center * lax.rsqrt(variance + norm_epsilon) * gain + shift

def attend_one(queries, keys_block, values_block, segment):
    same = segment[:, None] == segment[None, :]
    scores = jnp.einsum('qhd,khd->hqk', queries, keys_block, precision=lax.Precision.HIGHEST) * (1.0 / math.sqrt(HD))
    scores = low_back(jnp.where(same[None], scores, masked_score))
    weights = low(jax.nn.softmax(scores, axis=-1))
    return jnp.einsum('hqk,khd->qhd', weights, values_block, precision=lax.Precision.HIGHEST)
attend_saved = jax.checkpoint(attend_one)

def layer_forward(block_in, qkv_full, proj_full, up_full, down_full, vec_full, block_seg):
    qkv_full = low(qkv_full)
    proj_full = low(proj_full)
    up_full = low(up_full)
    down_full = low(down_full)
    vec_full = low(vec_full)
    group = block_in.shape[0]
    token_rows = block_in.reshape(-1, D)
    projected = matmul_high(token_rows, qkv_full)
    queries = round_both(projected[:, :D] + vec_full[0])
    key_rows = round_both(projected[:, D:2 * D])
    value_rows = round_both(projected[:, 2 * D:] + vec_full[1])
    split = (group, SEQ, HEADS, HD)
    attended = lax.map(lambda batch_item: attend_saved(*batch_item), (queries.reshape(split), key_rows.reshape(split), value_rows.reshape(split), block_seg))
    attn_rows = round_both(attended.reshape(-1, D))
    branch_out = low_back(matmul_high(attn_rows, proj_full) + vec_full[2])
    hidden_rows = norm_rows(token_rows + branch_out, vec_full[3], vec_full[4])
    up_rows = low_back(matmul_high(low(hidden_rows), up_full) + vec_full[8:].reshape(-1))
    active = low(jax.nn.gelu(up_rows, approximate=False))
    down_rows = low_back(matmul_high(active, down_full) + vec_full[5])
    layer_rows = norm_rows(hidden_rows + down_rows, vec_full[6], vec_full[7])
    return layer_rows.reshape(block_in.shape)

def orthogonal(matrix):
    flip = matrix.shape[0] > matrix.shape[1]
    work = matrix.T if flip else matrix
    work = work / (jnp.sqrt(jnp.sum(work * work)) + 1e-07)
    for iteration in range(NS_ITERS):
        gram = matmul_high(work, work.T)
        poly = newton_b * gram + newton_c * matmul_high(gram, gram)
        work = newton_a * work + matmul_high(poly, work)
    return work.T if flip else work

def muon_update(weight, moment, grad):
    moment_new = momentum_decay * moment + grad
    direction = orthogonal(moment_new)
    rows, cols = weight.shape
    return (moment_new, weight - muon_rate * math.sqrt(max(rows, cols) / rows) * direction)

def reference(inputs, cotangent, segment_ids, qkv_weight, proj_weight, up_weight, down_weight, vectors, qkv_moment, proj_moment, up_moment, down_moment, vec_first, vec_second):
    group = math.gcd(SEQS, 8)
    blocks = SEQS // group
    xs = inputs.astype(jnp.float32).reshape(blocks, group, SEQ, D)
    cs = cotangent.astype(jnp.float32).reshape(blocks, group, SEQ, D)
    ss = segment_ids.reshape(blocks, group, SEQ)
    params = (qkv_weight, proj_weight, up_weight, down_weight, vectors)

    def one_group(running, batch_item):
        block_in, block_cot, block_seg = batch_item

        def forward(values, qkv_full, proj_full, up_full, down_full, vec_full):
            return layer_forward(values, qkv_full, proj_full, up_full, down_full, vec_full, block_seg)
        result, pull = jax.vjp(forward, block_in, qkv_weight, proj_weight, up_weight, down_weight, vectors)
        grads = pull(block_cot)
        running = tuple((total + part for total, part in zip(running, grads[1:])))
        return (running, (result, grads[0]))
    start = tuple((jnp.zeros_like(param) for param in params))
    summed, (results, input_grads) = lax.scan(one_group, start, (xs, cs, ss))
    grad_qkv, grad_proj, grad_up, grad_down, grad_vec = summed
    qkv_moment_new, qkv_weight_new = muon_update(qkv_weight, qkv_moment, grad_qkv)
    proj_moment_new, proj_weight_new = muon_update(proj_weight, proj_moment, grad_proj)
    up_moment_new, up_weight_new = muon_update(up_weight, up_moment, grad_up)
    down_moment_new, down_weight_new = muon_update(down_weight, down_moment, grad_down)
    vec_first_new = beta_first * vec_first + (1.0 - beta_first) * grad_vec
    vec_second_new = beta_second * vec_second + (1.0 - beta_second) * grad_vec * grad_vec
    fix_first = 1.0 - beta_first ** STEP
    fix_second = 1.0 - beta_second ** STEP
    vectors_new = vectors - adam_rate * (vec_first_new / fix_first / (jnp.sqrt(vec_second_new / fix_second) + adam_epsilon) + weight_decay * vectors)
    return (results.reshape(SEQS, SEQ, D), input_grads.reshape(SEQS, SEQ, D), qkv_moment_new, proj_moment_new, up_moment_new, down_moment_new, qkv_weight_new, proj_weight_new, up_weight_new, down_weight_new, vec_first_new, vec_second_new, vectors_new)
```

```python
import functools
import math

import jax
import jax.numpy as jnp
from jax import lax
from jax.experimental import pallas as pl
from jax.experimental.pallas import tpu as pltpu
from jax.sharding import PartitionSpec as P

D = 512
HEADS = 8
HD = 64
FF = 2048
NS_ITERS = 5
STEP = 10
TILE = 256

norm_epsilon = 1e-12
momentum_decay = 0.95
muon_rate = 0.6
newton_a = 3.4445
newton_b = -4.775
newton_c = 2.0315
beta_first = 0.9
beta_second = 0.999
adam_rate = 0.2
weight_decay = 0.01
adam_epsilon = 1e-08
masked_score = -1e30
softmax_scale = 1.0 / math.sqrt(HD)

BF = jnp.bfloat16
F32 = jnp.float32
MIB = 1024 * 1024


def dot(left, right):
    return jnp.dot(left, right, preferred_element_type=F32)


def against(left, right):
    return lax.dot_general(left, right, (((1,), (1,)), ((), ())), preferred_element_type=F32)


def contract_rows(left, right):
    return lax.dot_general(left, right, (((0,), (0,)), ((), ())), preferred_element_type=F32)


def fixed(shape):
    return pl.BlockSpec(shape, lambda *_: (0,) * len(shape))


def compiler_params(grid_rank=1):
    return pltpu.CompilerParams(
        dimension_semantics=("arbitrary",) * grid_rank, vmem_limit_bytes=56 * MIB
    )


def cost(flops, nbytes, trans=0):
    return pl.CostEstimate(flops=int(flops), bytes_accessed=int(nbytes), transcendentals=int(trans))


def attend_kernel(x_ref, w_ref, vec_ref, segc_ref, segr_ref, qkv_ref, o_ref, ot_ref, at_ref, qt_s, vt_s):
    projected = dot(x_ref[0], w_ref[...])
    queries = (projected[:, :D] + vec_ref[0:1, :]).astype(BF)
    keys = projected[:, D : 2 * D].astype(BF)
    values = (projected[:, 2 * D :] + vec_ref[1:2, :]).astype(BF)
    qkv_ref[0, :, :D] = queries
    qkv_ref[0, :, D : 2 * D] = keys
    qkv_ref[0, :, 2 * D :] = values
    qt_s[...] = (queries.astype(F32) * softmax_scale).T.astype(BF)
    vt_s[...] = values.astype(F32).T.astype(BF)
    same = segc_ref[0] == segr_ref[0]
    for head in range(HEADS):
        rows = slice(head * HD, (head + 1) * HD)
        scores = dot(keys[:, rows], qt_s[rows, :])
        scores = jnp.where(same, scores, masked_score)
        exponent = jnp.exp(scores - jnp.max(scores, 0, keepdims=True))
        weights = (exponent * (1.0 / jnp.sum(exponent, 0, keepdims=True))).astype(BF)
        at_ref[0, head] = weights
        ot_ref[0, rows, :] = dot(vt_s[rows, :], weights).astype(BF)
    o_ref[0] = ot_ref[0].astype(F32).T.astype(BF)


def attend(x, qkv_weight, vec, segment_ids):
    count, length = segment_ids.shape
    item = lambda *shape: pl.BlockSpec((1,) + shape, lambda i: (i,) + (0,) * len(shape))
    return pl.pallas_call(
        attend_kernel,
        grid=(count,),
        in_specs=[
            item(length, D),
            fixed((D, 3 * D)),
            fixed(vec.shape),
            item(length, 1),
            item(1, length),
        ],
        out_specs=[item(length, 3 * D), item(length, D), item(D, length), item(HEADS, length, length)],
        out_shape=[
            jax.ShapeDtypeStruct((count, length, 3 * D), BF),
            jax.ShapeDtypeStruct((count, length, D), BF),
            jax.ShapeDtypeStruct((count, D, length), BF),
            jax.ShapeDtypeStruct((count, HEADS, length, length), BF),
        ],
        scratch_shapes=[pltpu.VMEM((D, length), BF), pltpu.VMEM((D, length), BF)],
        compiler_params=compiler_params(),
        cost_estimate=cost(count * 8e9, 3e7),
        name="attend_forward",
    )(x, qkv_weight, vec, segment_ids[:, :, None], segment_ids[:, None, :])


def normed(values):
    center = values - jnp.mean(values, -1, keepdims=True)
    factor = lax.rsqrt(jnp.mean(center * center, -1, keepdims=True) + norm_epsilon)
    return center * factor, factor


def norm_pull(scaled, unit, factor):
    return factor * (
        scaled
        - jnp.mean(scaled, -1, keepdims=True)
        - unit * jnp.mean(scaled * unit, -1, keepdims=True)
    )


def gelu_and_slope(u):
    size = jnp.abs(u)
    bell = jnp.exp(-0.5 * u * u)
    t = 1.0 / (1.0 + (0.3275911 / math.sqrt(2.0)) * size)
    poly = t * (
        0.5 * 0.254829592
        + t
        * (
            0.5 * -0.284496736
            + t * (0.5 * 1.421413741 + t * (0.5 * -1.453152027 + t * (0.5 * 1.061405429)))
        )
    )
    tail = poly * bell
    cdf = jnp.where(u >= 0, 1.0 - tail, tail)
    return u * cdf, cdf + u * (bell * (1.0 / math.sqrt(2.0 * math.pi)))


def colsum(values):
    return jnp.sum(values, 0, keepdims=True)


def layer_kernel(
    x_ref, o_ref, cot_ref, vec_ref, wp_ref, wu_ref, wd_ref,
    out_ref, dy_ref, do_ref, gdown_ref, gup_ref, gproj_ref, gvec_ref,
    acc_d, acc_u, acc_p, e_s, s_s,
):
    step = pl.program_id(0)

    @pl.when(step == 0)
    def _():
        acc_d[...] = jnp.zeros_like(acc_d)
        acc_u[...] = jnp.zeros_like(acc_u)
        acc_p[...] = jnp.zeros_like(acc_p)
        gvec_ref[...] = jnp.zeros_like(gvec_ref)

    row = lambda i: vec_ref[i : i + 1, :]
    attended = o_ref[...]
    unit_one, factor_one = normed(x_ref[...].astype(F32) + (dot(attended, wp_ref[...]) + row(2)))
    hidden = unit_one * row(3) + row(4)
    hidden_low = hidden.astype(BF)
    total = jnp.zeros_like(hidden)
    for j in range(FF // D):
        cols = slice(j * D, (j + 1) * D)
        active, slope = gelu_and_slope(dot(hidden_low, wu_ref[:, cols]) + row(8 + j))
        active = active.astype(BF)
        e_s[:, cols] = active
        s_s[:, cols] = slope
        total += dot(active, wd_ref[cols, :])
    unit_two, factor_two = normed(hidden + (total + row(5)))
    out_ref[...] = unit_two * row(6) + row(7)
    cot = cot_ref[...].astype(F32)
    gvec_ref[6:7, :] += colsum(cot * unit_two)
    gvec_ref[7:8, :] += colsum(cot)
    grad_second = norm_pull(cot * row(6), unit_two, factor_two)
    grad_low = grad_second.astype(BF)
    gvec_ref[5:6, :] += colsum(grad_low.astype(F32))
    grad_hidden = grad_second
    for j in range(FF // D):
        cols = slice(j * D, (j + 1) * D)
        grad_up = (against(grad_low, wd_ref[cols, :]) * s_s[:, cols]).astype(BF)
        gvec_ref[8 + j : 9 + j, :] += colsum(grad_up.astype(F32))
        acc_d[cols, :] += contract_rows(e_s[:, cols], grad_low)
        acc_u[:, cols] += contract_rows(hidden_low, grad_up)
        grad_hidden += against(grad_up, wu_ref[:, cols])
    gvec_ref[3:4, :] += colsum(grad_hidden * unit_one)
    gvec_ref[4:5, :] += colsum(grad_hidden)
    grad_first = norm_pull(grad_hidden * row(3), unit_one, factor_one)
    dy_ref[...] = grad_first
    branch_low = grad_first.astype(BF)
    gvec_ref[2:3, :] += colsum(branch_low.astype(F32))
    acc_p[...] += contract_rows(attended, branch_low)
    do_ref[...] = against(branch_low, wp_ref[...]).astype(BF)

    @pl.when(step == pl.num_programs(0) - 1)
    def _():
        half = D // 2
        for y in range(2):
            gdown_ref[y] = acc_d[y * (FF // 2) : (y + 1) * (FF // 2), :].astype(BF)
            gproj_ref[y] = acc_p[y * half : (y + 1) * half, :].astype(BF)
            for j in range(FF // D):
                gup_ref[y, j] = acc_u[y * half : (y + 1) * half, j * D : (j + 1) * D].astype(BF)


def layer(x_rows, attended, cot_rows, vec, proj, up, down):
    tokens = x_rows.shape[0]
    tile = pl.BlockSpec((TILE, D), lambda i: (i, 0))
    shapes = [
        ((tokens, D), F32), ((tokens, D), F32), ((tokens, D), BF),
        ((2, FF // 2, D), BF), ((2, FF // D, D // 2, D), BF), ((2, D // 2, D), BF), ((16, D), F32),
    ]
    return pl.pallas_call(
        layer_kernel,
        grid=(tokens // TILE,),
        in_specs=[tile, tile, tile, fixed(vec.shape), fixed((D, D)), fixed((D, FF)), fixed((FF, D))],
        out_specs=[tile, tile, tile] + [fixed(s) for s, _ in shapes[3:]],
        out_shape=[jax.ShapeDtypeStruct(s, t) for s, t in shapes],
        scratch_shapes=[
            pltpu.VMEM((FF, D), F32),
            pltpu.VMEM((D, FF), F32),
            pltpu.VMEM((D, D), F32),
            pltpu.VMEM((TILE, FF), BF),
            pltpu.VMEM((TILE, FF), F32),
        ],
        compiler_params=compiler_params(),
        cost_estimate=cost(tokens * 3e7, 2e7),
        name="layer_both_ways",
    )(x_rows, attended, cot_rows, vec, proj, up, down)


def pull_kernel(
    x_ref, qkv_ref, at_ref, ot_ref, do_ref, dy_ref, w_ref, gproj_ref,
    gx_ref, grad_ref, gvec_ref,
    acc, dot_s, kt_s, dqt_s, dp_s,
):
    step = pl.program_id(0)

    @pl.when(step == 0)
    def _():
        acc[...] = jnp.zeros_like(acc)
        gvec_ref[...] = jnp.zeros_like(gvec_ref)

    dot_s[...] = do_ref[0].astype(F32).T.astype(BF)
    kt_s[...] = qkv_ref[0, :, D : 2 * D].astype(F32).T.astype(BF)
    for head in range(HEADS):
        rows = slice(head * HD, (head + 1) * HD)
        at = lambda third: slice(third * D + head * HD, third * D + (head + 1) * HD)
        grad_out = dot_s[rows, :]
        delta = colsum(grad_out.astype(F32) * ot_ref[0, rows, :].astype(F32))
        weights = at_ref[0, head]
        grad_probs = dot(qkv_ref[0, :, at(2)], grad_out)
        grad_scores = (weights.astype(F32) * (grad_probs - delta)).astype(BF)
        dp_s[:, at(2)] = dot(weights, do_ref[0, :, rows]).astype(BF)
        dp_s[:, at(1)] = (dot(grad_scores, qkv_ref[0, :, at(0)]) * softmax_scale).astype(BF)
        dqt_s[rows, :] = dot(kt_s[rows, :], grad_scores) * softmax_scale
    dp_s[:, :D] = dqt_s[...].T.astype(BF)
    gvec_ref[0:1, :] += colsum(dp_s[:, :D].astype(F32))
    gvec_ref[1:2, :] += colsum(dp_s[:, 2 * D :].astype(F32))
    grad_projected = dp_s[...]
    acc[...] += contract_rows(x_ref[0], grad_projected)
    gx_ref[0] = dy_ref[0] + against(grad_projected, w_ref[...])

    @pl.when(step == pl.num_programs(0) - 1)
    def _():
        half = D // 2
        for y in range(2):
            for j in range(3):
                grad_ref[y, j] = acc[y * half : (y + 1) * half, j * D : (j + 1) * D].astype(BF)
            grad_ref[y, 3] = gproj_ref[y]


def pull(x, qkv, weights, attended_t, grad_out, grad_first, qkv_weight, grad_proj):
    count, length, _ = x.shape
    item = lambda *shape: pl.BlockSpec((1,) + shape, lambda i: (i,) + (0,) * len(shape))
    return pl.pallas_call(
        pull_kernel,
        grid=(count,),
        in_specs=[
            item(length, D), item(length, 3 * D), item(HEADS, length, length), item(D, length),
            item(length, D), item(length, D), fixed((D, 3 * D)), fixed((2, D // 2, D)),
        ],
        out_specs=[item(length, D), fixed((2, 4, D // 2, D)), fixed((16, D))],
        out_shape=[
            jax.ShapeDtypeStruct((count, length, D), F32),
            jax.ShapeDtypeStruct((2, 4, D // 2, D), BF),
            jax.ShapeDtypeStruct((16, D), F32),
        ],
        scratch_shapes=[
            pltpu.VMEM((D, 3 * D), F32),
            pltpu.VMEM((D, length), BF),
            pltpu.VMEM((D, length), BF),
            pltpu.VMEM((D, length), F32),
            pltpu.VMEM((length, 3 * D), BF),
        ],
        compiler_params=compiler_params(),
        cost_estimate=cost(count * 1e10, 3e7),
        name="attend_backward",
    )(x, qkv, weights, attended_t, grad_out, grad_first, qkv_weight, grad_proj)


def newton_schulz(work, low):
    start = work[...]
    start = start * (1.0 / (jnp.sqrt(jnp.sum(start * start)) + 1e-07))
    work[...] = start
    low[...] = start.astype(BF)
    eye = lax.broadcasted_iota(jnp.int32, (D, D), 0) == lax.broadcasted_iota(jnp.int32, (D, D), 1)
    for iteration in range(NS_ITERS):
        gram = against(low[...], low[...])
        own = jnp.where(eye, gram, 0.0)
        down = jnp.sum(own, 1, keepdims=True)
        across = jnp.sum(own, 0, keepdims=True)
        rest = jnp.where(eye, 0.0, gram)
        rest_low = rest.astype(BF)
        square = dot(rest_low, rest_low)
        poly = rest * (newton_b + newton_c * (down + across)) + newton_c * square
        poly = jnp.where(eye, 0.0, poly).astype(BF)
        square_own = jnp.sum(jnp.where(eye, square, 0.0), 1, keepdims=True)
        factor = newton_a + newton_b * down + newton_c * (down * down + square_own)
        for j in range(work.shape[1] // D):
            cols = slice(j * D, (j + 1) * D)
            made = factor * work[:, cols] + dot(poly, low[:, cols])
            work[:, cols] = made
        low[...] = work[...].astype(BF)


def wide_kernel(y_ref, m_ref, out_ref, work, low, *, first):
    half = D // 2
    blocks = work.shape[1] // D
    for y in range(2):
        for j in range(blocks):
            work[y * half : (y + 1) * half, j * D : (j + 1) * D] = m_ref[y, first + j].astype(F32)
    newton_schulz(work, low)
    mine = pl.ds(pl.multiple_of(y_ref[0] * half, half), half)
    out_ref[...] = jnp.zeros_like(out_ref)
    for j in range(blocks):
        out_ref[first + j] = low[mine, j * D : (j + 1) * D]


def tall_kernel(y_ref, m_ref, out_ref, work, low):
    for j in range(FF // D):
        y, k = divmod(j, FF // D // 2)
        work[:, j * D : (j + 1) * D] = m_ref[y, k * D : (k + 1) * D, :].astype(F32).T
    newton_schulz(work, low)
    for y in range(2):

        @pl.when(y_ref[0] == y)
        def _():
            for k in range(FF // D // 2):
                j = y * (FF // D // 2) + k
                out_ref[k * D : (k + 1) * D, :] = work[:, j * D : (j + 1) * D].T.astype(BF)


def orthogonal(body, moment, out_shape, cols, y):
    flops = NS_ITERS * (4.0 * D * D * cols + 2.0 * D * D * D)
    return pl.pallas_call(
        body,
        in_specs=[
            pl.BlockSpec(memory_space=pltpu.SMEM),
            pl.BlockSpec(memory_space=pltpu.VMEM),
        ],
        out_specs=pl.BlockSpec(memory_space=pltpu.VMEM),
        out_shape=jax.ShapeDtypeStruct(out_shape, BF),
        scratch_shapes=[pltpu.VMEM((D, cols), F32), pltpu.VMEM((D, cols), BF)],
        compiler_params=pltpu.CompilerParams(vmem_limit_bytes=48 * MIB),
        cost_estimate=cost(flops, 4e6),
        name="newton_schulz",
    )(y.reshape(1), moment)


class Place:
    def __init__(self):
        self.dp = lax.axis_index("dp")
        self.y = lax.axis_index("fsdp")
        self.bits = [1 << k for k in range(lax.axis_size("dp").bit_length() - 1)]

    def high(self, bit):
        return (self.y if bit == "y" else self.dp & bit) != 0

    def swap(self, value, bit):
        if bit == "y":
            return lax.ppermute(value, "fsdp", [(0, 1), (1, 0)])
        size = lax.axis_size("dp")
        return lax.ppermute(value, "dp", [(i, i ^ bit) for i in range(size)])

    def join(self, mine, theirs, bit, axis):
        return jnp.where(
            self.high(bit),
            jnp.concatenate([theirs, mine], axis),
            jnp.concatenate([mine, theirs], axis),
        )

    def halves(self, value, bit):
        axis = 0 if bit == "y" else 1
        middle = value.shape[axis] // 2
        low = lax.slice_in_dim(value, 0, middle, axis=axis)
        high = lax.slice_in_dim(value, middle, 2 * middle, axis=axis)
        flag = self.high(bit)
        return jnp.where(flag, high, low), jnp.where(flag, low, high)

    def whole_rows(self, shard, bits):
        part = shard
        for bit in bits:
            middle = part.shape[0] // 2
            part = jnp.where(self.high(bit), part[middle:], part[:middle])
        part = self.swap(part, "y")
        for bit in reversed(bits):
            part = self.join(part, self.swap(part, bit), bit, 0)
        return self.join(shard, part, "y", 0)

    def sum_over_all(self, value):
        for bit in ["y"] + self.bits:
            value = value + self.swap(value, bit)
        return value

    def moment_sum(self, grad, moment, order):
        value = grad
        offset = jnp.int32(0)
        for bit in order:
            keep, send = self.halves(value, bit)
            got = self.swap(send, bit)
            value = (keep.astype(F32) + got.astype(F32)).astype(BF)
            if bit != "y":
                offset = offset + jnp.where(self.high(bit), value.shape[1], 0)
        own = lax.dynamic_slice_in_dim(moment, offset, value.shape[1], 0)
        value = (momentum_decay * own[None] + value.astype(F32)).astype(BF)
        for bit in reversed(order):
            value = self.join(value, self.swap(value, bit), bit, 0 if bit == "y" else 1)
        return value


def blocked(matrix):
    rows, cols = matrix.shape
    return matrix.reshape(rows, cols // D, D).transpose(1, 0, 2).reshape(-1, D)


def unblocked(stack, rows):
    return stack.reshape(-1, rows, D).transpose(1, 0, 2).reshape(rows, -1)


def step_weight(weight_shard, shape, direction):
    rows, cols = shape
    return weight_shard - muon_rate * math.sqrt(max(rows, cols) / rows) * direction.astype(F32)


def on_device(
    inputs, cotangent, segment_ids,
    qkv_weight, proj_weight, up_weight, down_weight, vectors,
    qkv_moment, proj_moment, up_moment, down_moment, vec_first, vec_second,
):
    place = Place()
    core, across, rest = place.bits[0], place.bits[1], place.bits[2:]
    half = D // 2

    vec_low = vectors.astype(BF)
    vec = place.join(vec_low, place.swap(vec_low, "y"), "y", 0).astype(F32)
    qkv_full = place.whole_rows(qkv_weight.astype(BF), [core])
    proj_full = place.whole_rows(proj_weight.astype(BF), [core])
    up_full = place.whole_rows(up_weight.astype(BF), [core, across])
    down_full = place.whole_rows(down_weight.astype(BF), [core, across])

    qkv, attended, attended_t, weights = attend(inputs, qkv_full, vec, segment_ids)
    layer_out, grad_first, grad_out, grad_down, grad_up, grad_proj, vec_one = layer(
        inputs.reshape(-1, D), attended.reshape(-1, D), cotangent.reshape(-1, D),
        vec, proj_full, up_full, down_full,
    )
    down_order = [core, "y", across] + rest
    up_order = [core, across] + rest + ["y"]
    down_whole = place.moment_sum(grad_down, down_moment, down_order)
    up_whole = place.moment_sum(grad_up.reshape(2, -1, D), blocked(up_moment), up_order)

    input_grad, grad_qkv, vec_two = pull(
        inputs, qkv, weights, attended_t, grad_out.reshape(inputs.shape),
        grad_first.reshape(inputs.shape), qkv_full, grad_proj,
    )
    grad_qkv = grad_qkv.reshape(2, -1, D)
    last_moment = jnp.concatenate([blocked(qkv_moment), proj_moment], 0)
    middle = last_moment.shape[0] // 2
    last_whole = jnp.concatenate(
        [
            place.moment_sum(grad_qkv[:, :middle], last_moment[:middle], down_order),
            place.moment_sum(grad_qkv[:, middle:], last_moment[middle:], up_order),
        ],
        1,
    )
    vec_sum = place.sum_over_all(vec_one + vec_two)
    sum_vec = jnp.where(place.y != 0, vec_sum[6:12], vec_sum[:6])

    first_core = place.dp % 2 == 0
    y = place.y
    blocks = (2, 4, half, D)
    large = lax.cond(
        first_core,
        lambda up, down: orthogonal(
            functools.partial(wide_kernel, first=0), up.reshape(blocks), blocks[1:], FF, y
        ).reshape(-1, D),
        lambda up, down: orthogonal(tall_kernel, down, (FF // 2, D), FF, y),
        up_whole,
        down_whole,
    )
    large_other = place.swap(large, core)
    up_direction = unblocked(jnp.where(first_core, large, large_other), half)
    down_direction = jnp.where(first_core, large_other, large)
    small = lax.cond(
        first_core,
        lambda both: orthogonal(functools.partial(wide_kernel, first=3), both, blocks[1:], D, y),
        lambda both: orthogonal(functools.partial(wide_kernel, first=0), both, blocks[1:], 3 * D, y),
        last_whole.reshape(blocks),
    )
    small_other = place.swap(small, core)
    qkv_direction = unblocked(jnp.where(first_core, small_other, small)[:3].reshape(-1, D), half)
    proj_direction = jnp.where(first_core, small, small_other)[3]

    mine = lambda whole: jnp.where(y != 0, whole[1], whole[0]).astype(F32)
    last_mine = mine(last_whole)
    vec_first_new = beta_first * vec_first + (1.0 - beta_first) * sum_vec
    vec_second_new = beta_second * vec_second + (1.0 - beta_second) * sum_vec * sum_vec
    fix_first = 1.0 - beta_first**STEP
    fix_second = 1.0 - beta_second**STEP
    vectors_new = vectors - adam_rate * (
        vec_first_new / fix_first / (jnp.sqrt(vec_second_new / fix_second) + adam_epsilon)
        + weight_decay * vectors
    )
    return (
        layer_out.reshape(inputs.shape),
        input_grad,
        unblocked(last_mine[: 3 * half], half),
        last_mine[3 * half :],
        unblocked(mine(up_whole), half),
        mine(down_whole),
        step_weight(qkv_weight, (D, 3 * D), qkv_direction),
        step_weight(proj_weight, (D, D), proj_direction),
        step_weight(up_weight, (D, FF), up_direction),
        step_weight(down_weight, (FF, D), down_direction),
        vec_first_new,
        vec_second_new,
        vectors_new,
    )


def solution(mesh):
    tokens = P(("dp", "fsdp"), None, None)
    rows = P("fsdp", None)
    in_specs = (tokens, tokens, P(("dp", "fsdp"), None)) + (rows,) * 11
    out_specs = (tokens, tokens) + (rows,) * 11
    return jax.shard_map(
        on_device, mesh=mesh, in_specs=in_specs, out_specs=out_specs, check_vma=False
    )
```

```python
import functools
import math

import jax
import jax.numpy as jnp
from jax import lax
from jax.experimental import pallas as pl
from jax.experimental.pallas import tpu as pltpu
from jax.sharding import PartitionSpec as P

D = 512
HEADS = 8
HD = 64
FF = 2048
NS_ITERS = 5
STEP = 10
TILE = 256

norm_epsilon = 1e-12
momentum_decay = 0.95
muon_rate = 0.6
newton_a = 3.4445
newton_b = -4.775
newton_c = 2.0315
beta_first = 0.9
beta_second = 0.999
adam_rate = 0.2
weight_decay = 0.01
adam_epsilon = 1e-08
masked_score = -1e30
softmax_scale = 1.0 / math.sqrt(HD)

BF = jnp.bfloat16
F32 = jnp.float32
MIB = 1024 * 1024


def dot(left, right):
    return jnp.dot(left, right, preferred_element_type=F32)


def against(left, right):
    return lax.dot_general(left, right, (((1,), (1,)), ((), ())), preferred_element_type=F32)


def contract_rows(left, right):
    return lax.dot_general(left, right, (((0,), (0,)), ((), ())), preferred_element_type=F32)


def fixed(shape):
    return pl.BlockSpec(shape, lambda *_: (0,) * len(shape))


SCALARS = pl.BlockSpec(memory_space=pltpu.SMEM)


def compiler_params(grid_rank=1):
    return pltpu.CompilerParams(
        dimension_semantics=("arbitrary",) * grid_rank, vmem_limit_bytes=56 * MIB
    )


def cost(flops, nbytes, trans=0):
    return pl.CostEstimate(flops=int(flops), bytes_accessed=int(nbytes), transcendentals=int(trans))


def place_rows(whole, here_ref, own, near, far):
    y, core = here_ref[0], here_ref[1]
    part = near.shape[0]
    start = lambda k: pl.ds(pl.multiple_of(k * part, part), part)
    whole[y] = own[...]
    whole[1 - y, start(core)] = near[...]
    whole[1 - y, start(1 - core)] = far[...]


def attend_kernel(
    here_ref, x_ref, own_ref, near_ref, far_ref, vec_ref, seg_ref,
    qkv_ref, o_ref, ot_ref, at_ref,
    w_s, qt_s, vt_s,
):
    @pl.when(pl.program_id(0) == 0)
    def _():
        place_rows(w_s, here_ref, own_ref, near_ref, far_ref)

    projected = dot(x_ref[0], w_s[...].reshape(D, 3 * D))
    queries = (projected[:, :D] + vec_ref[0:1, :]).astype(BF)
    keys = projected[:, D : 2 * D].astype(BF)
    values = (projected[:, 2 * D :] + vec_ref[1:2, :]).astype(BF)
    qkv_ref[0, :, :D] = queries
    qkv_ref[0, :, D : 2 * D] = keys
    qkv_ref[0, :, 2 * D :] = values
    qt_s[...] = (queries.astype(F32) * softmax_scale).T.astype(BF)
    vt_s[...] = values.astype(F32).T.astype(BF)
    document = seg_ref[0].astype(F32)
    same = jnp.broadcast_to(document, (8, document.shape[1])).T[:, :1] == document
    for head in range(HEADS):
        rows = slice(head * HD, (head + 1) * HD)
        scores = dot(keys[:, rows], qt_s[rows, :])
        scores = jnp.where(same, scores, masked_score)
        exponent = jnp.exp(scores - jnp.max(scores, 0, keepdims=True))
        weights = (exponent * (1.0 / jnp.sum(exponent, 0, keepdims=True))).astype(BF)
        at_ref[0, head] = weights
        ot_ref[0, rows, :] = dot(vt_s[rows, :], weights).astype(BF)
    o_ref[0] = ot_ref[0].astype(F32).T.astype(BF)


def attend(here, x, qkv_parts, vec, segment_ids):
    count, length = segment_ids.shape
    item = lambda *shape: pl.BlockSpec((1,) + shape, lambda i: (i,) + (0,) * len(shape))
    return pl.pallas_call(
        attend_kernel,
        grid=(count,),
        in_specs=[
            SCALARS, item(length, D), *[fixed(p.shape) for p in qkv_parts], fixed(vec.shape),
            item(1, length),
        ],
        out_specs=[item(length, 3 * D), item(length, D), item(D, length), item(HEADS, length, length)],
        out_shape=[
            jax.ShapeDtypeStruct((count, length, 3 * D), BF),
            jax.ShapeDtypeStruct((count, length, D), BF),
            jax.ShapeDtypeStruct((count, D, length), BF),
            jax.ShapeDtypeStruct((count, HEADS, length, length), BF),
        ],
        scratch_shapes=[
            pltpu.VMEM((2, D // 2, 3 * D), BF),
            pltpu.VMEM((D, length), BF),
            pltpu.VMEM((D, length), BF),
        ],
        compiler_params=compiler_params(),
        cost_estimate=cost(count * 8e9, 3e7),
        name="attend_forward",
    )(here, x, *qkv_parts, vec, segment_ids[:, None, :])


def normed(values):
    center = values - jnp.mean(values, -1, keepdims=True)
    factor = lax.rsqrt(jnp.mean(center * center, -1, keepdims=True) + norm_epsilon)
    return center * factor, factor


def norm_pull(scaled, unit, factor):
    return factor * (
        scaled
        - jnp.mean(scaled, -1, keepdims=True)
        - unit * jnp.mean(scaled * unit, -1, keepdims=True)
    )


def gelu_and_slope(u):
    size = jnp.abs(u)
    bell = jnp.exp(-0.5 * u * u)
    t = 1.0 / (1.0 + (0.3275911 / math.sqrt(2.0)) * size)
    poly = t * (
        0.5 * 0.254829592
        + t
        * (
            0.5 * -0.284496736
            + t * (0.5 * 1.421413741 + t * (0.5 * -1.453152027 + t * (0.5 * 1.061405429)))
        )
    )
    tail = poly * bell
    cdf = jnp.where(u >= 0, 1.0 - tail, tail)
    return u * cdf, cdf + u * (bell * (1.0 / math.sqrt(2.0 * math.pi)))


def colsum(values):
    return jnp.sum(values, 0, keepdims=True)


def layer_kernel(
    here_ref, x_ref, o_ref, cot_ref, vec_ref, own_ref, near_ref, far_ref,
    out_ref, dy_ref, do_ref, keep_ref, send_ref, gproj_ref, gvec_ref,
    w_s, acc_d, acc_u, acc_p, e_s, s_s,
):
    step = pl.program_id(0)
    half = D // 2

    @pl.when(step == 0)
    def _():
        place_rows(w_s, here_ref, own_ref, near_ref, far_ref)
        acc_d[...] = jnp.zeros_like(acc_d)
        acc_u[...] = jnp.zeros_like(acc_u)
        acc_p[...] = jnp.zeros_like(acc_p)
        gvec_ref[...] = jnp.zeros_like(gvec_ref)

    def rows_of(start):
        return jnp.concatenate([w_s[0, start : start + half], w_s[1, start : start + half]], 0)

    down_block = lambda j: w_s[j // 2, (j % 2) * D : (j % 2 + 1) * D, :]
    up_block = lambda j: rows_of(FF // 2 + j * half)
    row = lambda i: vec_ref[i : i + 1, :]
    attended = o_ref[...]
    proj = rows_of(FF)
    unit_one, factor_one = normed(x_ref[...].astype(F32) + (dot(attended, proj) + row(2)))
    hidden = unit_one * row(3) + row(4)
    hidden_low = hidden.astype(BF)
    total = jnp.zeros_like(hidden)
    for j in range(FF // D):
        cols = slice(j * D, (j + 1) * D)
        active, slope = gelu_and_slope(dot(hidden_low, up_block(j)) + row(8 + j))
        active = active.astype(BF)
        e_s[:, cols] = active
        s_s[:, cols] = slope
        total += dot(active, down_block(j))
    unit_two, factor_two = normed(hidden + (total + row(5)))
    out_ref[...] = unit_two * row(6) + row(7)
    cot = cot_ref[...].astype(F32)
    gvec_ref[6:7, :] += colsum(cot * unit_two)
    gvec_ref[7:8, :] += colsum(cot)
    grad_second = norm_pull(cot * row(6), unit_two, factor_two)
    grad_low = grad_second.astype(BF)
    gvec_ref[5:6, :] += colsum(grad_low.astype(F32))
    grad_hidden = grad_second
    for j in range(FF // D):
        cols = slice(j * D, (j + 1) * D)
        grad_up = (against(grad_low, down_block(j)) * s_s[:, cols]).astype(BF)
        gvec_ref[8 + j : 9 + j, :] += colsum(grad_up.astype(F32))
        acc_d[cols, :] += contract_rows(e_s[:, cols], grad_low)
        acc_u[:, cols] += contract_rows(hidden_low, grad_up)
        grad_hidden += against(grad_up, up_block(j))
    gvec_ref[3:4, :] += colsum(grad_hidden * unit_one)
    gvec_ref[4:5, :] += colsum(grad_hidden)
    grad_first = norm_pull(grad_hidden * row(3), unit_one, factor_one)
    dy_ref[...] = grad_first
    branch_low = grad_first.astype(BF)
    gvec_ref[2:3, :] += colsum(branch_low.astype(F32))
    acc_p[...] += contract_rows(attended, branch_low)
    do_ref[...] = against(branch_low, proj).astype(BF)

    @pl.when(step == pl.num_programs(0) - 1)
    def _():
        def put(up_ref, down_ref):
            for y in range(2):
                rows = slice(y * half, (y + 1) * half)
                down_ref[y] = acc_d[y * (FF // 2) : (y + 1) * (FF // 2), :].astype(BF)
                for j in range(FF // D):
                    cols = slice(j * D, (j + 1) * D)
                    up_ref[y, j * half : (j + 1) * half, :] = acc_u[rows, cols].astype(BF)

        for y in range(2):
            gproj_ref[y] = acc_p[y * half : (y + 1) * half, :].astype(BF)

        @pl.when(here_ref[1] == 0)
        def _():
            put(keep_ref, send_ref)

        @pl.when(here_ref[1] != 0)
        def _():
            put(send_ref, keep_ref)


def layer(here, x_rows, attended, cot_rows, vec, parts):
    tokens = x_rows.shape[0]
    tile = pl.BlockSpec((TILE, D), lambda i: (i, 0))
    shapes = [
        ((tokens, D), F32), ((tokens, D), F32), ((tokens, D), BF),
        ((2, FF // 2, D), BF), ((2, FF // 2, D), BF), ((2, D // 2, D), BF), ((16, D), F32),
    ]
    return pl.pallas_call(
        layer_kernel,
        grid=(tokens // TILE,),
        in_specs=[SCALARS, tile, tile, tile, fixed(vec.shape)] + [fixed(p.shape) for p in parts],
        out_specs=[tile, tile, tile] + [fixed(s) for s, _ in shapes[3:]],
        out_shape=[jax.ShapeDtypeStruct(s, t) for s, t in shapes],
        scratch_shapes=[
            pltpu.VMEM((2,) + parts[0].shape, BF),
            pltpu.VMEM((FF, D), F32),
            pltpu.VMEM((D, FF), F32),
            pltpu.VMEM((D, D), F32),
            pltpu.VMEM((TILE, FF), BF),
            pltpu.VMEM((TILE, FF), F32),
        ],
        compiler_params=compiler_params(),
        cost_estimate=cost(tokens * 3e7, 2e7),
        name="layer_both_ways",
    )(here, x_rows, attended, cot_rows, vec, *parts)


def pull_kernel(
    here_ref, x_ref, qkv_ref, at_ref, ot_ref, do_ref, dy_ref, own_ref, near_ref, far_ref, gproj_ref, vec_one_ref,
    gx_ref, grad_ref, vec_out_ref,
    w_s, gvec_ref, acc, dot_s, kt_s, dqt_s, dp_s,
):
    step = pl.program_id(0)

    @pl.when(step == 0)
    def _():
        place_rows(w_s, here_ref, own_ref, near_ref, far_ref)
        acc[...] = jnp.zeros_like(acc)
        gvec_ref[...] = vec_one_ref[...]

    dot_s[...] = do_ref[0].astype(F32).T.astype(BF)
    kt_s[...] = qkv_ref[0, :, D : 2 * D].astype(F32).T.astype(BF)
    for head in range(HEADS):
        rows = slice(head * HD, (head + 1) * HD)
        at = lambda third: slice(third * D + head * HD, third * D + (head + 1) * HD)
        grad_out = dot_s[rows, :]
        delta = colsum(grad_out.astype(F32) * ot_ref[0, rows, :].astype(F32))
        weights = at_ref[0, head]
        grad_probs = dot(qkv_ref[0, :, at(2)], grad_out)
        grad_scores = (weights.astype(F32) * (grad_probs - delta)).astype(BF)
        dp_s[:, at(2)] = dot(weights, do_ref[0, :, rows]).astype(BF)
        dp_s[:, at(1)] = (dot(grad_scores, qkv_ref[0, :, at(0)]) * softmax_scale).astype(BF)
        dqt_s[rows, :] = dot(kt_s[rows, :], grad_scores) * softmax_scale
    dp_s[:, :D] = dqt_s[...].T.astype(BF)
    gvec_ref[0:1, :] += colsum(dp_s[:, :D].astype(F32))
    gvec_ref[1:2, :] += colsum(dp_s[:, 2 * D :].astype(F32))
    grad_projected = dp_s[...]
    acc[...] += contract_rows(x_ref[0], grad_projected)
    gx_ref[0] = dy_ref[0] + against(grad_projected, w_s[...].reshape(D, 3 * D))

    @pl.when(step == pl.num_programs(0) - 1)
    def _():
        half = D // 2
        for y in range(2):
            for j in range(3):
                grad_ref[y, j] = acc[y * half : (y + 1) * half, j * D : (j + 1) * D].astype(BF)
            grad_ref[y, 3] = gproj_ref[y]
        vec_out_ref[...] = gvec_ref[...].astype(BF)


def pull(here, x, qkv, weights, attended_t, grad_out, grad_first, qkv_parts, grad_proj, vec_one):
    count, length, _ = x.shape
    item = lambda *shape: pl.BlockSpec((1,) + shape, lambda i: (i,) + (0,) * len(shape))
    return pl.pallas_call(
        pull_kernel,
        grid=(count,),
        in_specs=[
            SCALARS, item(length, D), item(length, 3 * D), item(HEADS, length, length),
            item(D, length), item(length, D), item(length, D),
            *[fixed(p.shape) for p in qkv_parts], fixed((2, D // 2, D)), fixed((16, D)),
        ],
        out_specs=[item(length, D), fixed((2, 4, D // 2, D)), fixed((16, D))],
        out_shape=[
            jax.ShapeDtypeStruct((count, length, D), F32),
            jax.ShapeDtypeStruct((2, 4, D // 2, D), BF),
            jax.ShapeDtypeStruct((16, D), BF),
        ],
        scratch_shapes=[
            pltpu.VMEM((2, D // 2, 3 * D), BF),
            pltpu.VMEM((16, D), F32),
            pltpu.VMEM((D, 3 * D), F32),
            pltpu.VMEM((D, length), BF),
            pltpu.VMEM((D, length), BF),
            pltpu.VMEM((D, length), F32),
            pltpu.VMEM((length, 3 * D), BF),
        ],
        compiler_params=compiler_params(),
        cost_estimate=cost(count * 1e10, 3e7),
        name="attend_backward",
    )(here, x, qkv, weights, attended_t, grad_out, grad_first, *qkv_parts, grad_proj, vec_one)


def newton_schulz(cols, work, low):
    blocks = [slice(start, start + D) for start in range(0, cols, D)]
    squares = sum(colsum(work[:, block] * work[:, block]) for block in blocks)
    scale = 1.0 / (jnp.sqrt(jnp.sum(squares)) + 1e-07)
    for block in blocks:
        made = work[:, block] * scale
        work[:, block] = made
        low[:, block] = made.astype(BF)
    eye = lax.broadcasted_iota(jnp.int32, (D, D), 0) == lax.broadcasted_iota(jnp.int32, (D, D), 1)

    def iterate(_, carry):
        gram = against(low[:, :cols], low[:, :cols])
        own = jnp.where(eye, gram, 0.0)
        down = jnp.sum(own, 1, keepdims=True)
        across = jnp.sum(own, 0, keepdims=True)
        rest = jnp.where(eye, 0.0, gram)
        rest_low = rest.astype(BF)
        square = dot(rest_low, rest_low)
        poly = rest * (newton_b + newton_c * (down + across)) + newton_c * square
        poly = jnp.where(eye, 0.0, poly).astype(BF)
        square_own = jnp.sum(jnp.where(eye, square, 0.0), 1, keepdims=True)
        factor = newton_a + newton_b * down + newton_c * (down * down + square_own)
        for block in blocks:
            made = factor * work[:, block] + dot(poly, low[:, block])
            work[:, block] = made
            low[:, block] = made.astype(BF)
        return carry

    lax.fori_loop(0, NS_ITERS, iterate, 0)


def load_blocks(m_ref, work, blocks):
    half = D // 2
    for k, j in enumerate(blocks):
        for y in range(2):
            rows = slice(y * half, (y + 1) * half)
            work[rows, k * D : (k + 1) * D] = m_ref[y, j * half : (j + 1) * half, :].astype(F32)


def store_blocks(y, out_ref, low, count):
    half = D // 2
    rows = pl.ds(pl.multiple_of(y * half, half), half)
    for k in range(count):
        out_ref[k * half : (k + 1) * half, :] = low[rows, k * D : (k + 1) * D]


def large_kernel(here_ref, m_ref, out_ref, work, low):
    y, core = here_ref[0], here_ref[1]
    blocks = FF // D

    @pl.when(core == 0)
    def _():
        load_blocks(m_ref, work, range(blocks))

    @pl.when(core != 0)
    def _():
        for j in range(blocks):
            rows = slice((j % 2) * D, (j % 2 + 1) * D)
            work[:, j * D : (j + 1) * D] = m_ref[j // 2, rows, :].astype(F32).T

    newton_schulz(FF, work, low)

    @pl.when(core == 0)
    def _():
        store_blocks(y, out_ref, low, blocks)

    for k in range(2):

        @pl.when((core != 0) & (y == k))
        def _():
            for j in range(blocks // 2):
                cols = slice((k * blocks // 2 + j) * D, (k * blocks // 2 + j + 1) * D)
                out_ref[j * D : (j + 1) * D, :] = work[:, cols].T.astype(BF)


def small_kernel(here_ref, m_ref, out_ref, work, low):
    y, core = here_ref[0], here_ref[1]

    @pl.when(core == 0)
    def _():
        load_blocks(m_ref, work, [3])
        newton_schulz(D, work, low)
        out_ref[...] = jnp.zeros_like(out_ref)
        store_blocks(y, out_ref, low, 1)

    @pl.when(core != 0)
    def _():
        load_blocks(m_ref, work, range(3))
        newton_schulz(3 * D, work, low)
        store_blocks(y, out_ref, low, 3)


def orthogonal(body, here, moment, rows, blocks):
    flops = NS_ITERS * (4.0 * blocks + 2.0) * D * D * D
    return pl.pallas_call(
        body,
        in_specs=[SCALARS, pl.BlockSpec(memory_space=pltpu.VMEM)],
        out_specs=pl.BlockSpec(memory_space=pltpu.VMEM),
        out_shape=jax.ShapeDtypeStruct((rows, D), BF),
        scratch_shapes=[pltpu.VMEM((D, blocks * D), F32), pltpu.VMEM((D, blocks * D), BF)],
        compiler_params=pltpu.CompilerParams(vmem_limit_bytes=48 * MIB),
        cost_estimate=cost(flops, 4e6),
        name="newton_schulz",
    )(here, moment)


def rate(rows, cols):
    return muon_rate * math.sqrt(max(rows, cols) / rows)


def sort_large_kernel(here_ref, mine_ref, other_ref, up_ref, down_ref):
    first = here_ref[1] == 0
    mine, other = mine_ref[0].astype(F32), other_ref[...].astype(F32)
    up_ref[...] = jnp.where(first, mine, other)
    down_ref[...] = jnp.where(first, other, mine)


def step_large_kernel(here_ref, x_ref, x_other_ref, up_ref, down_ref, up_out, down_out):
    first = here_ref[1] == 0
    x, x_other = x_ref[...].astype(F32), x_other_ref[...].astype(F32)
    up_out[...] = up_ref[...] - rate(D, FF) * jnp.where(first, x, x_other)
    down_out[...] = down_ref[...] - rate(FF, D) * jnp.where(first, x_other, x)


def finish(body, here, operands, in_specs, out_specs, shapes, grid, nbytes):
    return pl.pallas_call(
        body,
        grid_spec=pltpu.PrefetchScalarGridSpec(
            num_scalar_prefetch=1, grid=grid, in_specs=in_specs, out_specs=out_specs
        ),
        out_shape=[jax.ShapeDtypeStruct(s, F32) for s in shapes],
        compiler_params=pltpu.CompilerParams(
            dimension_semantics=("arbitrary",), vmem_limit_bytes=20 * MIB
        ),
        cost_estimate=cost(nbytes, nbytes),
        name="finish",
    )(here, *operands)


HALF = D // 2
ACROSS = pl.BlockSpec((HALF, D), lambda j, here: (0, j))
ALONG = pl.BlockSpec((HALF, D), lambda j, here: (j, 0))
MINE = pl.BlockSpec((1, HALF, D), lambda j, here: (here[0], j, 0))


def sort_large(here, whole, other, up, down):
    return finish(
        sort_large_kernel, here, (whole, other), [MINE, ALONG], [ACROSS, ALONG],
        (up.shape, down.shape), (FF // D,), 1.2e7,
    )


def step_large(here, x, x_other, up, down):
    return finish(
        step_large_kernel, here, (x, x_other, up, down), [ALONG, ALONG, ACROSS, ALONG],
        [ACROSS, ALONG], (up.shape, down.shape), (FF // D,), 1e7,
    )


def step_small_kernel(
    here_ref, m_ref, x_ref, x_other_ref, qkv_ref, proj_ref, sum_ref, vec_ref, one_ref, two_ref,
    qkv_m_ref, proj_m_ref, qkv_w_ref, proj_w_ref, vec_out, one_out, two_out,
):
    first = here_ref[1] == 0
    j = pl.program_id(0)
    m = m_ref[0].astype(F32)
    x, x_other = x_ref[...].astype(F32), x_other_ref[...].astype(F32)

    @pl.when(j == 0)
    def _():
        whole = sum_ref[...].astype(F32)
        own = jnp.where(here_ref[0] == 0, whole[:6], whole[6:12])
        one = beta_first * one_ref[...] + (1.0 - beta_first) * own
        two = beta_second * two_ref[...] + (1.0 - beta_second) * own * own
        one_out[...] = one
        two_out[...] = two
        fix_first = 1.0 - beta_first**STEP
        fix_second = 1.0 - beta_second**STEP
        vec_out[...] = vec_ref[...] - adam_rate * (
            one / fix_first / (jnp.sqrt(two / fix_second) + adam_epsilon)
            + weight_decay * vec_ref[...]
        )

    @pl.when(j < 3)
    def _():
        qkv_m_ref[...] = m
        qkv_w_ref[...] = qkv_ref[...] - rate(D, 3 * D) * jnp.where(first, x_other, x)

    @pl.when(j == 3)
    def _():
        proj_m_ref[...] = m
        proj_w_ref[...] = proj_ref[...] - rate(D, D) * jnp.where(first, x, x_other)


def step_small(here, whole, x, x_other, qkv, proj, vec_sum, vectors, vec_first, vec_second):
    across = pl.BlockSpec((HALF, D), lambda j, here: (0, jnp.minimum(j, 2)))
    along = pl.BlockSpec((HALF, D), lambda j, here: (lax.rem(j, 3), 0))
    alone = pl.BlockSpec((HALF, D), lambda j, here: (0, 0))
    rows = fixed(vectors.shape)
    return finish(
        step_small_kernel, here,
        (whole, x, x_other, qkv, proj, vec_sum, vectors, vec_first, vec_second),
        [MINE, along, along, across, alone, fixed(vec_sum.shape), rows, rows, rows],
        [across, alone, across, alone, rows, rows, rows],
        (qkv.shape, proj.shape) * 2 + (vectors.shape,) * 3, (4,), 8e6,
    )


def after(value, *others):
    for other in others:
        row = other.reshape(-1, other.shape[-1])[:1, :D].astype(F32) * 0.0
        value = (value.astype(F32) + row).astype(value.dtype)
    return value


class Place:
    def __init__(self):
        self.dp = lax.axis_index("dp")
        self.y = lax.axis_index("fsdp")
        self.bits = [1 << k for k in range(lax.axis_size("dp").bit_length() - 1)]

    def high(self, bit):
        return (self.y if bit == "y" else self.dp & bit) != 0

    def swap(self, value, bit):
        if bit == "y":
            return lax.ppermute(value, "fsdp", [(0, 1), (1, 0)])
        size = lax.axis_size("dp")
        return lax.ppermute(value, "dp", [(i, i ^ bit) for i in range(size)])

    def join(self, mine, theirs, bit, axis):
        return jnp.where(
            self.high(bit),
            jnp.concatenate([theirs, mine], axis),
            jnp.concatenate([mine, theirs], axis),
        )

    def halves(self, value, bit):
        axis = 0 if bit == "y" else 1
        middle = value.shape[axis] // 2
        low = lax.slice_in_dim(value, 0, middle, axis=axis)
        high = lax.slice_in_dim(value, middle, 2 * middle, axis=axis)
        flag = self.high(bit)
        return jnp.where(flag, high, low), jnp.where(flag, low, high)


class Chain:
    def __init__(self, place, grad, order, rider=None):
        self.place, self.value, self.order, self.rider = place, grad, list(order), rider
        self.offset = jnp.int32(0)

    def send(self, k):
        self.keep, out = self.place.halves(self.value, self.order[k])
        if self.rider is None:
            return out
        return jnp.concatenate([out.reshape(-1, D), self.rider], 0)

    def add(self, got, k):
        self.last = got
        if self.rider is not None:
            self.rider = (self.rider.astype(F32) + got[-16:].astype(F32)).astype(BF)
            got = got[:-16].reshape(self.keep.shape)
        self.value = (self.keep.astype(F32) + got.astype(F32)).astype(BF)
        if self.order[k] != "y":
            self.offset = self.offset + jnp.where(
                self.place.high(self.order[k]), self.value.shape[1], 0
            )

    def scatter(self, steps, *waits):
        for k in steps:
            self.add(after(self.place.swap(self.send(k), self.order[k]), *waits), k)

    def decay(self, rows_at):
        own = rows_at(self.offset, self.value.shape[1])
        self.value = (momentum_decay * own[None] + self.value.astype(F32)).astype(BF)

    def gather(self, steps=None, *waits):
        for k in reversed(range(len(self.order))) if steps is None else steps:
            bit = self.order[k]
            self.last = self.place.swap(self.value, bit)
            theirs = after(self.last, *waits)
            self.value = self.place.join(self.value, theirs, bit, 0 if bit == "y" else 1)
        return self.value


def blocked(matrix):
    rows, cols = matrix.shape
    return matrix.reshape(rows, cols // D, D).transpose(1, 0, 2).reshape(-1, D)


def block_rows(matrix, offset, count):
    rows, cols = matrix.shape
    block = jnp.minimum(offset // rows, cols // D - 1)
    return lax.dynamic_slice(matrix, (offset % rows, block * D), (count, D))


def on_device(
    inputs, cotangent, segment_ids,
    qkv_weight, proj_weight, up_weight, down_weight, vectors,
    qkv_moment, proj_moment, up_moment, down_moment, vec_first, vec_second,
):
    place = Place()
    core, across, rest = place.bits[0], place.bits[1], place.bits[2:]
    half = D // 2
    here = jnp.stack([place.y, place.dp % 2]).astype(jnp.int32)
    first_core = place.dp % 2 == 0

    def core_part(value):
        middle = value.shape[0] // 2
        return jnp.where(first_core, value[:middle], value[middle:])

    vec_low = vectors.astype(BF)
    vec_other = place.swap(vec_low, "y")
    vec = place.join(vec_low, vec_other, "y", 0).astype(F32)
    qkv_own = qkv_weight.astype(BF)
    qkv_near = place.swap(core_part(qkv_own), "y")
    rest_own = jnp.concatenate([down_weight, blocked(up_weight), proj_weight], 0).astype(BF)
    qkv_far = place.swap(qkv_near, core)
    rest_part = after(core_part(rest_own), qkv_far, vec_other)
    qkv_parts = (qkv_own, qkv_near, qkv_far)
    rest_near = place.swap(rest_part, "y")
    qkv, attended, attended_t, weights = attend(here, inputs, qkv_parts, vec, segment_ids)
    rest_near = after(rest_near, attended)
    rest_parts = (rest_own, rest_near, place.swap(rest_near, core))

    layer_out, grad_first, grad_out, keep, send, grad_proj, vec_one = layer(
        here, inputs.reshape(-1, D), attended.reshape(-1, D), cotangent.reshape(-1, D), vec, rest_parts
    )
    got = place.swap(send, core)
    large = (keep.astype(F32) + got.astype(F32)).astype(BF)
    middle = large.shape[1] // 2
    chain_one = Chain(place, large[:, :middle], ["y", across])
    chain_two = Chain(place, large[:, middle:], [across, "y"])
    send_one, send_two = chain_one.send(0), chain_two.send(0)
    grad_out, send_one, send_two = lax.optimization_barrier((grad_out, send_one, send_two))
    chain_one.add(place.swap(send_one, "y"), 0)
    chain_two.add(place.swap(send_two, across), 0)

    input_grad, grad_qkv, vec_sum = pull(
        here, inputs, qkv, weights, attended_t, grad_out.reshape(inputs.shape),
        grad_first.reshape(inputs.shape), qkv_parts, grad_proj, vec_one,
    )
    chain_small = Chain(place, grad_qkv.reshape(2, -1, D), [core, "y", across] + rest, vec_sum)

    chain_one.scatter([1])
    chain_two.scatter([1])
    apart = chain_one.value.shape[1]
    chain_both = Chain(place, jnp.concatenate([chain_one.value, chain_two.value], 1), rest)
    chain_both.scatter(range(len(rest)))

    def large_rows(offset, count):
        offset = jnp.where(offset >= apart, middle - apart, 0) + chain_one.offset + offset
        return jnp.where(
            first_core, block_rows(up_moment, offset, count), block_rows(down_moment, offset, count)
        )

    chain_both.decay(large_rows)
    count = len(rest)
    chain_small.scatter([0], chain_one.last, chain_two.last)
    chain_small.scatter([1], chain_both.last)
    both = chain_both.gather([count - 1])
    chain_small.scatter([2], chain_both.last)
    both = chain_both.gather(reversed(range(count - 1)))
    chain_small.scatter(range(3, 2 + count), chain_both.last)
    chain_one.value, chain_two.value = both[:, :apart], both[:, apart:]
    chain_one.gather([1])
    chain_two.gather([1])
    chain_small.scatter([2 + count], chain_one.last, chain_two.last)
    chain_small.decay(
        lambda offset, count: jnp.where(
            offset >= 3 * half,
            block_rows(proj_moment, offset % half, count),
            block_rows(qkv_moment, offset, count),
        )
    )
    chain_small.gather(reversed(range(2, 3 + count)))
    large_whole = jnp.concatenate(
        [chain_one.gather([0]), chain_two.gather([0], chain_small.last)], 1
    )
    large_x = orthogonal(large_kernel, here, large_whole, FF // 2, FF // D)
    large_other = place.swap(jnp.where(place.y != 0, large_whole[1], large_whole[0]), core)
    up_moment_new, down_moment_new = sort_large(here, large_whole, large_other, up_weight, down_weight)
    chain_small.gather([1], large_x)
    small_whole = chain_small.gather([0], up_moment_new)
    up_weight_new, down_weight_new = step_large(
        here, large_x, place.swap(large_x, core), up_weight, down_weight
    )
    small_x = orthogonal(small_kernel, here, small_whole, 3 * half, 3)
    (
        qkv_moment_new, proj_moment_new, qkv_weight_new, proj_weight_new,
        vectors_new, vec_first_new, vec_second_new,
    ) = step_small(
        here, small_whole, small_x, place.swap(small_x, core), qkv_weight, proj_weight,
        chain_small.rider, vectors, vec_first, vec_second,
    )
    return (
        layer_out.reshape(inputs.shape),
        input_grad,
        qkv_moment_new,
        proj_moment_new,
        up_moment_new,
        down_moment_new,
        qkv_weight_new,
        proj_weight_new,
        up_weight_new,
        down_weight_new,
        vec_first_new,
        vec_second_new,
        vectors_new,
    )


def solution(mesh):
    tokens = P(("dp", "fsdp"), None, None)
    rows = P("fsdp", None)
    in_specs = (tokens, tokens, P(("dp", "fsdp"), None)) + (rows,) * 11
    out_specs = (tokens, tokens) + (rows,) * 11
    return jax.shard_map(
        on_device, mesh=mesh, in_specs=in_specs, out_specs=out_specs, check_vma=False
    )
```

```python
import functools
import math

import jax
import jax.numpy as jnp
from jax import lax
from jax.experimental import pallas as pl
from jax.experimental.pallas import tpu as pltpu
from jax.sharding import PartitionSpec as P

D = 512
HEADS = 8
HD = 64
FF = 2048
NS_ITERS = 5
STEP = 10
TILE = 512

norm_epsilon = 1e-12
momentum_decay = 0.95
muon_rate = 0.6
newton_a = 3.4445
newton_b = -4.775
newton_c = 2.0315
beta_first = 0.9
beta_second = 0.999
adam_rate = 0.2
weight_decay = 0.01
adam_epsilon = 1e-08
masked_score = -1e30
softmax_scale = 1.0 / math.sqrt(HD)

BF = jnp.bfloat16
F32 = jnp.float32
MIB = 1024 * 1024


def dot(left, right):
    return jnp.dot(left, right, preferred_element_type=F32)


def against(left, right):
    return lax.dot_general(left, right, (((1,), (1,)), ((), ())), preferred_element_type=F32)


def contract_rows(left, right):
    return lax.dot_general(left, right, (((0,), (0,)), ((), ())), preferred_element_type=F32)


def fixed(shape):
    return pl.BlockSpec(shape, lambda *_: (0,) * len(shape))


SCALARS = pl.BlockSpec(memory_space=pltpu.SMEM)


def compiler_params(grid_rank=1):
    return pltpu.CompilerParams(
        dimension_semantics=("arbitrary",) * grid_rank, vmem_limit_bytes=56 * MIB
    )


def cost(flops, nbytes, trans=0):
    return pl.CostEstimate(flops=int(flops), bytes_accessed=int(nbytes), transcendentals=int(trans))


def place_rows(whole, here_ref, own, near, far):
    y, core = here_ref[0], here_ref[1]
    part = near.shape[0]
    start = lambda k: pl.ds(pl.multiple_of(k * part, part), part)
    whole[y] = own[...]
    whole[1 - y, start(core)] = near[...]
    whole[1 - y, start(1 - core)] = far[...]


def attend_kernel(
    here_ref, x_ref, own_ref, near_ref, far_ref, vec_ref, seg_ref,
    qkv_ref, o_ref, ot_ref, at_ref,
    w_s, qt_s, vt_s,
):
    @pl.when(pl.program_id(0) == 0)
    def _():
        place_rows(w_s, here_ref, own_ref, near_ref, far_ref)

    projected = dot(x_ref[0], w_s[...].reshape(D, 3 * D))
    queries = (projected[:, :D] + vec_ref[0:1, :]).astype(BF)
    keys = projected[:, D : 2 * D].astype(BF)
    values = (projected[:, 2 * D :] + vec_ref[1:2, :]).astype(BF)
    qkv_ref[0, :, :D] = queries
    qkv_ref[0, :, D : 2 * D] = keys
    qkv_ref[0, :, 2 * D :] = values
    qt_s[...] = (queries.astype(F32) * softmax_scale).T.astype(BF)
    vt_s[...] = values.astype(F32).T.astype(BF)
    document = seg_ref[0].astype(F32)
    same = jnp.broadcast_to(document, (8, document.shape[1])).T[:, :1] == document
    for head in range(HEADS):
        rows = slice(head * HD, (head + 1) * HD)
        scores = dot(keys[:, rows], qt_s[rows, :])
        scores = jnp.where(same, scores, masked_score)
        exponent = jnp.exp(scores - jnp.max(scores, 0, keepdims=True))
        weights = (exponent * (1.0 / jnp.sum(exponent, 0, keepdims=True))).astype(BF)
        at_ref[0, head] = weights
        ot_ref[0, rows, :] = dot(vt_s[rows, :], weights).astype(BF)
    o_ref[0] = ot_ref[0].astype(F32).T.astype(BF)


def attend(here, x, qkv_parts, vec, segment_ids):
    count, length = segment_ids.shape
    item = lambda *shape: pl.BlockSpec((1,) + shape, lambda i: (i,) + (0,) * len(shape))
    return pl.pallas_call(
        attend_kernel,
        grid=(count,),
        in_specs=[
            SCALARS, item(length, D), *[fixed(p.shape) for p in qkv_parts], fixed(vec.shape),
            item(1, length),
        ],
        out_specs=[item(length, 3 * D), item(length, D), item(D, length), item(HEADS, length, length)],
        out_shape=[
            jax.ShapeDtypeStruct((count, length, 3 * D), BF),
            jax.ShapeDtypeStruct((count, length, D), BF),
            jax.ShapeDtypeStruct((count, D, length), BF),
            jax.ShapeDtypeStruct((count, HEADS, length, length), BF),
        ],
        scratch_shapes=[
            pltpu.VMEM((2, D // 2, 3 * D), BF),
            pltpu.VMEM((D, length), BF),
            pltpu.VMEM((D, length), BF),
        ],
        compiler_params=compiler_params(),
        cost_estimate=cost(count * 8e9, 3e7),
        name="attend_forward",
    )(here, x, *qkv_parts, vec, segment_ids[:, None, :])


def normed(values):
    center = values - jnp.mean(values, -1, keepdims=True)
    factor = lax.rsqrt(jnp.mean(center * center, -1, keepdims=True) + norm_epsilon)
    return center * factor, factor


def norm_pull(scaled, unit, factor):
    return factor * (
        scaled
        - jnp.mean(scaled, -1, keepdims=True)
        - unit * jnp.mean(scaled * unit, -1, keepdims=True)
    )


def gelu_and_slope(u):
    cdf = 0.5 + 0.5 * lax.erf(u * math.sqrt(0.5))
    return u * cdf, cdf + u * (jnp.exp(-0.5 * u * u) * (1.0 / math.sqrt(2.0 * math.pi)))


def colsum(values):
    return jnp.sum(values, 0, keepdims=True)


def layer_kernel(
    here_ref, x_ref, o_ref, cot_ref, vec_ref, own_ref, near_ref, far_ref,
    out_ref, dy_ref, do_ref, keep_ref, send_ref, gproj_ref, gvec_ref,
    w_s, acc_d, acc_u, acc_p, e_s, s_s,
):
    step = pl.program_id(0)
    half = D // 2

    @pl.when(step == 0)
    def _():
        place_rows(w_s, here_ref, own_ref, near_ref, far_ref)
        acc_d[...] = jnp.zeros_like(acc_d)
        acc_u[...] = jnp.zeros_like(acc_u)
        acc_p[...] = jnp.zeros_like(acc_p)
        gvec_ref[...] = jnp.zeros_like(gvec_ref)

    def rows_of(start):
        return jnp.concatenate([w_s[0, start : start + half], w_s[1, start : start + half]], 0)

    down_block = lambda j: w_s[j // 2, (j % 2) * D : (j % 2 + 1) * D, :]
    up_block = lambda j: rows_of(FF // 2 + j * half)
    row = lambda i: vec_ref[i : i + 1, :]
    attended = o_ref[...]
    proj = rows_of(FF)
    unit_one, factor_one = normed(x_ref[...].astype(F32) + (dot(attended, proj) + row(2)))
    hidden = unit_one * row(3) + row(4)
    hidden_low = hidden.astype(BF)
    total = jnp.zeros_like(hidden)
    for j in range(FF // D):
        cols = slice(j * D, (j + 1) * D)
        active, slope = gelu_and_slope(dot(hidden_low, up_block(j)) + row(8 + j))
        active = active.astype(BF)
        e_s[:, cols] = active
        s_s[:, cols] = slope
        total += dot(active, down_block(j))
    unit_two, factor_two = normed(hidden + (total + row(5)))
    out_ref[...] = unit_two * row(6) + row(7)
    cot = cot_ref[...].astype(F32)
    gvec_ref[6:7, :] += colsum(cot * unit_two)
    gvec_ref[7:8, :] += colsum(cot)
    grad_second = norm_pull(cot * row(6), unit_two, factor_two)
    grad_low = grad_second.astype(BF)
    gvec_ref[5:6, :] += colsum(grad_low.astype(F32))
    grad_hidden = grad_second
    for j in range(FF // D):
        cols = slice(j * D, (j + 1) * D)
        grad_up = (against(grad_low, down_block(j)) * s_s[:, cols]).astype(BF)
        gvec_ref[8 + j : 9 + j, :] += colsum(grad_up.astype(F32))
        acc_d[cols, :] += contract_rows(e_s[:, cols], grad_low)
        acc_u[:, cols] += contract_rows(hidden_low, grad_up)
        grad_hidden += against(grad_up, up_block(j))
    gvec_ref[3:4, :] += colsum(grad_hidden * unit_one)
    gvec_ref[4:5, :] += colsum(grad_hidden)
    grad_first = norm_pull(grad_hidden * row(3), unit_one, factor_one)
    dy_ref[...] = grad_first
    branch_low = grad_first.astype(BF)
    gvec_ref[2:3, :] += colsum(branch_low.astype(F32))
    acc_p[...] += contract_rows(attended, branch_low)
    do_ref[...] = against(branch_low, proj).astype(BF)

    @pl.when(step == pl.num_programs(0) - 1)
    def _():
        def put(up_ref, down_ref):
            for y in range(2):
                rows = slice(y * half, (y + 1) * half)
                down_ref[y] = acc_d[y * (FF // 2) : (y + 1) * (FF // 2), :].astype(BF)
                for j in range(FF // D):
                    cols = slice(j * D, (j + 1) * D)
                    up_ref[y, j * half : (j + 1) * half, :] = acc_u[rows, cols].astype(BF)

        for y in range(2):
            gproj_ref[y] = acc_p[y * half : (y + 1) * half, :].astype(BF)

        @pl.when(here_ref[1] == 0)
        def _():
            put(keep_ref, send_ref)

        @pl.when(here_ref[1] != 0)
        def _():
            put(send_ref, keep_ref)


def layer(here, x_rows, attended, cot_rows, vec, parts):
    tokens = x_rows.shape[0]
    tile = pl.BlockSpec((TILE, D), lambda i: (i, 0))
    shapes = [
        ((tokens, D), F32), ((tokens, D), F32), ((tokens, D), BF),
        ((2, FF // 2, D), BF), ((2, FF // 2, D), BF), ((2, D // 2, D), BF), ((16, D), F32),
    ]
    return pl.pallas_call(
        layer_kernel,
        grid=(tokens // TILE,),
        in_specs=[SCALARS, tile, tile, tile, fixed(vec.shape)] + [fixed(p.shape) for p in parts],
        out_specs=[tile, tile, tile] + [fixed(s) for s, _ in shapes[3:]],
        out_shape=[jax.ShapeDtypeStruct(s, t) for s, t in shapes],
        scratch_shapes=[
            pltpu.VMEM((2,) + parts[0].shape, BF),
            pltpu.VMEM((FF, D), F32),
            pltpu.VMEM((D, FF), F32),
            pltpu.VMEM((D, D), F32),
            pltpu.VMEM((TILE, FF), BF),
            pltpu.VMEM((TILE, FF), F32),
        ],
        compiler_params=compiler_params(),
        cost_estimate=cost(tokens * 3e7, 2e7),
        name="layer_both_ways",
    )(here, x_rows, attended, cot_rows, vec, *parts)


def attend_pull_kernel(q_ref, k_ref, v_ref, at_ref, ot_ref, do_ref, dq_ref, dk_ref, dv_ref, dqt_s):
    grad_out_t = do_ref[0].astype(F32).T.astype(BF)
    keys_t = k_ref[0].astype(F32).T.astype(BF)
    for head in range(2):
        rows = slice(head * HD, (head + 1) * HD)
        grad_out = grad_out_t[rows, :]
        delta = colsum(grad_out.astype(F32) * ot_ref[0, rows, :].astype(F32))
        weights = at_ref[0, head]
        grad_probs = dot(v_ref[0, :, rows], grad_out)
        grad_scores = (weights.astype(F32) * (grad_probs - delta)).astype(BF)
        dv_ref[0, :, rows] = dot(weights, do_ref[0, :, rows]).astype(BF)
        dk_ref[0, :, rows] = (dot(grad_scores, q_ref[0, :, rows]) * softmax_scale).astype(BF)
        dqt_s[rows, :] = dot(keys_t[rows, :], grad_scores) * softmax_scale
    dq_ref[0] = dqt_s[...].T.astype(BF)


def attend_pull(qkv, weights, attended_t, grad_out):
    count, length, _ = qkv.shape
    pairs, wide = HEADS // 2, 2 * HD
    third = lambda k: pl.BlockSpec((1, length, wide), lambda i, p: (i, 0, k * pairs + p))
    return pl.pallas_call(
        attend_pull_kernel,
        grid=(count, pairs),
        in_specs=[
            third(0), third(1), third(2),
            pl.BlockSpec((1, 2, length, length), lambda i, p: (i, p, 0, 0)),
            pl.BlockSpec((1, wide, length), lambda i, p: (i, p, 0)),
            third(0),
        ],
        out_specs=[third(0)] * 3,
        out_shape=[jax.ShapeDtypeStruct((count, length, D), BF)] * 3,
        scratch_shapes=[pltpu.VMEM((wide, length), F32)],
        compiler_params=compiler_params(2),
        cost_estimate=cost(count * 6e9, 2e7),
        name="attend_backward",
    )(qkv, qkv, qkv, weights, attended_t, grad_out)


def project_pull_kernel(
    here_ref, x_ref, dq_ref, dk_ref, dv_ref, dy_ref, own_ref, near_ref, far_ref, gproj_ref, vec_one_ref,
    gx_ref, keep_ref, send_ref, vec_out_ref,
    w_s, gvec_ref, acc,
):
    step = pl.program_id(0)

    @pl.when(step == 0)
    def _():
        place_rows(w_s, here_ref, own_ref, near_ref, far_ref)
        acc[...] = jnp.zeros_like(acc)
        gvec_ref[...] = vec_one_ref[...]

    gvec_ref[0:1, :] += colsum(dq_ref[0].astype(F32))
    gvec_ref[1:2, :] += colsum(dv_ref[0].astype(F32))
    total = dy_ref[0]
    for k, grad_ref_k in enumerate((dq_ref, dk_ref, dv_ref)):
        cols = slice(k * D, (k + 1) * D)
        grad = grad_ref_k[0]
        acc[:, cols] += contract_rows(x_ref[0], grad)
        total += against(grad, w_s[:, :, cols].reshape(D, D))
    gx_ref[0] = total

    @pl.when(step == pl.num_programs(0) - 1)
    def _():
        half = D // 2
        vec_low = gvec_ref[...].astype(BF)
        vec_out_ref[...] = vec_low
        send_ref[4 * half :, :] = vec_low

        def block(y, j):
            if j == 3:
                return gproj_ref[y]
            return acc[y * half : (y + 1) * half, j * D : (j + 1) * D].astype(BF)

        for core in range(2):

            @pl.when(here_ref[1] == core)
            def _():
                for y in range(2):
                    for j in range(2):
                        rows = slice((2 * y + j) * half, (2 * y + j + 1) * half)
                        keep_ref[y, j * half : (j + 1) * half, :] = block(y, 2 * core + j)
                        send_ref[rows, :] = block(y, 2 - 2 * core + j)


def project_pull(here, x, grads, grad_first, qkv_parts, grad_proj, vec_one):
    count, length, _ = x.shape
    item = pl.BlockSpec((1, length, D), lambda i: (i, 0, 0))
    return pl.pallas_call(
        project_pull_kernel,
        grid=(count,),
        in_specs=[SCALARS, item, item, item, item, item]
        + [fixed(p.shape) for p in qkv_parts]
        + [fixed((2, D // 2, D)), fixed((16, D))],
        out_specs=[item, fixed((2, D, D)), fixed((2 * D + 16, D)), fixed((16, D))],
        out_shape=[
            jax.ShapeDtypeStruct((count, length, D), F32),
            jax.ShapeDtypeStruct((2, D, D), BF),
            jax.ShapeDtypeStruct((2 * D + 16, D), BF),
            jax.ShapeDtypeStruct((16, D), BF),
        ],
        scratch_shapes=[
            pltpu.VMEM((2, D // 2, 3 * D), BF),
            pltpu.VMEM((16, D), F32),
            pltpu.VMEM((D, 3 * D), F32),
        ],
        compiler_params=compiler_params(),
        cost_estimate=cost(count * 4e9, 1.5e7),
        name="project_backward",
    )(here, x, *grads, grad_first, *qkv_parts, grad_proj, vec_one)


def column_blocks(cols):
    return [slice(start, start + D) for start in range(0, cols, D)]


def normalize(cols, work, low):
    squares = sum(colsum(work[:, block] * work[:, block]) for block in column_blocks(cols))
    scale = 1.0 / (jnp.sqrt(jnp.sum(squares)) + 1e-07)
    for block in column_blocks(cols):
        made = work[:, block] * scale
        work[:, block] = made
        low[:, block] = made.astype(BF)


def iterate(cols, work, low):
    eye = lax.broadcasted_iota(jnp.int32, (D, D), 0) == lax.broadcasted_iota(jnp.int32, (D, D), 1)
    gram = against(low[:, :cols], low[:, :cols])
    own = jnp.where(eye, gram, 0.0)
    down = jnp.sum(own, 1, keepdims=True)
    across = jnp.sum(own, 0, keepdims=True)
    rest = jnp.where(eye, 0.0, gram)
    rest_low = rest.astype(BF)
    square = dot(rest_low, rest_low)
    poly = rest * (newton_b + newton_c * (down + across)) + newton_c * square
    poly = jnp.where(eye, 0.0, poly).astype(BF)
    square_own = jnp.sum(jnp.where(eye, square, 0.0), 1, keepdims=True)
    factor = newton_a + newton_b * down + newton_c * (down * down + square_own)
    for block in column_blocks(cols):
        made = factor * work[:, block] + dot(poly, low[:, block])
        work[:, block] = made
        low[:, block] = made.astype(BF)


def load_blocks(m_ref, work, blocks):
    half = D // 2
    for k, j in enumerate(blocks):
        for y in range(2):
            rows = slice(y * half, (y + 1) * half)
            work[rows, k * D : (k + 1) * D] = m_ref[y, j * half : (j + 1) * half, :].astype(F32)


def store_blocks(y, out_ref, low, count):
    half = D // 2
    rows = pl.ds(pl.multiple_of(y * half, half), half)
    for k in range(count):
        out_ref[k * half : (k + 1) * half, :] = low[rows, k * D : (k + 1) * D]


def large_kernel(here_ref, m_ref, out_ref, work, low):
    y, core = here_ref[0], here_ref[1]
    blocks = FF // D

    @pl.when(core == 0)
    def _():
        load_blocks(m_ref, work, range(blocks))

    @pl.when(core != 0)
    def _():
        for j in range(blocks):
            rows = slice((j % 2) * D, (j % 2 + 1) * D)
            work[:, j * D : (j + 1) * D] = m_ref[j // 2, rows, :].astype(F32).T

    normalize(FF, work, low)

    @pl.loop(0, NS_ITERS)
    def _(_):
        iterate(FF, work, low)

    @pl.when(core == 0)
    def _():
        store_blocks(y, out_ref, low, blocks)

    for k in range(2):

        @pl.when((core != 0) & (y == k))
        def _():
            for j in range(blocks // 2):
                cols = slice((k * blocks // 2 + j) * D, (k * blocks // 2 + j + 1) * D)
                out_ref[j * D : (j + 1) * D, :] = work[:, cols].T.astype(BF)


def orthogonal_large(here, moment):
    blocks = FF // D
    return pl.pallas_call(
        large_kernel,
        in_specs=[SCALARS, pl.BlockSpec(memory_space=pltpu.VMEM)],
        out_specs=pl.BlockSpec(memory_space=pltpu.VMEM),
        out_shape=jax.ShapeDtypeStruct((FF // 2, D), BF),
        scratch_shapes=[pltpu.VMEM((D, FF), F32), pltpu.VMEM((D, FF), BF)],
        compiler_params=pltpu.CompilerParams(vmem_limit_bytes=48 * MIB),
        cost_estimate=cost(NS_ITERS * (4.0 * blocks + 2.0) * D * D * D, 4e6),
        name="newton_schulz_large",
    )(here, moment)


def rate(rows, cols):
    return muon_rate * math.sqrt(max(rows, cols) / rows)


def small_kernel(
    here_ref, m_ref, large_m, large_m_other, large_x, large_x_other, up_w, down_w,
    out_ref, up_m_new, down_m_new, up_w_new, down_w_new, qkv_m_new, proj_m_new,
    work, low, m_s, m_other_s, x_s, x_other_s, up_w_s, down_w_s,
    up_m_s, down_m_s, qkv_m_s, proj_m_s, in_sems, out_sems,
):
    half = D // 2
    y, core = here_ref[0], here_ref[1]
    first = core == 0
    arrivals = [
        pltpu.make_async_copy(source, target, in_sems.at[k])
        for k, (source, target) in enumerate(
            [
                (large_m.at[y], m_s), (large_m_other, m_other_s), (large_x, x_s),
                (large_x_other, x_other_s), (up_w, up_w_s), (down_w, down_w_s),
            ]
        )
    ]
    results = [
        pltpu.make_async_copy(source, target, out_sems.at[k])
        for k, (source, target) in enumerate(
            [
                (up_m_s, up_m_new), (down_m_s, down_m_new), (up_w_s, up_w_new),
                (down_w_s, down_w_new), (qkv_m_s, qkv_m_new), (proj_m_s, proj_m_new),
            ]
        )
    ]
    for copy in arrivals:
        copy.start()

    @pl.when(first)
    def _():
        load_blocks(m_ref, work, [3])
        normalize(D, work, low)

    @pl.when(core != 0)
    def _():
        load_blocks(m_ref, work, range(3))
        normalize(3 * D, work, low)

    @pl.loop(0, NS_ITERS)
    def _(step):
        @pl.when(first)
        def _():
            iterate(D, work, low)

        @pl.when(core != 0)
        def _():
            iterate(3 * D, work, low)

        @pl.when(step == 1)
        def _():
            for copy in arrivals:
                copy.wait()
            for j in range(FF // D):
                rows, cols = slice(j * half, (j + 1) * half), slice(j * D, (j + 1) * D)
                m, m_other = m_s[rows, :].astype(F32), m_other_s[rows, :].astype(F32)
                x, x_other = x_s[rows, :].astype(F32), x_other_s[rows, :].astype(F32)
                up_m_s[:, cols] = jnp.where(first, m, m_other)
                down_m_s[rows, :] = jnp.where(first, m_other, m)
                up_w_s[:, cols] -= rate(D, FF) * jnp.where(first, x, x_other)
                down_w_s[rows, :] -= rate(FF, D) * jnp.where(first, x_other, x)
                own = m_ref[y, rows, :].astype(F32)
                if j < 3:
                    qkv_m_s[:, cols] = own
                else:
                    proj_m_s[...] = own
            for copy in results:
                copy.start()

    @pl.when(first)
    def _():
        out_ref[...] = jnp.zeros_like(out_ref)
        store_blocks(y, out_ref, low, 1)

    @pl.when(core != 0)
    def _():
        store_blocks(y, out_ref, low, 3)

    for copy in results:
        copy.wait()


def orthogonal_small(here, moment, large_whole, m_other, x, x_other, up, down):
    half = D // 2
    spaces = lambda kind, count: [pl.BlockSpec(memory_space=kind)] * count
    large = pltpu.VMEM((FF // 2, D), BF)
    shapes = [up.shape, down.shape, up.shape, down.shape, (half, 3 * D), (half, D)]
    return pl.pallas_call(
        small_kernel,
        in_specs=[SCALARS] + spaces(pltpu.VMEM, 1) + spaces(pl.ANY, 6),
        out_specs=spaces(pltpu.VMEM, 1) + spaces(pl.ANY, 6),
        out_shape=[jax.ShapeDtypeStruct((3 * half, D), BF)]
        + [jax.ShapeDtypeStruct(shape, F32) for shape in shapes],
        scratch_shapes=[
            pltpu.VMEM((D, 3 * D), F32), pltpu.VMEM((D, 3 * D), BF),
            large, large, large, large, pltpu.VMEM(up.shape, F32), pltpu.VMEM(down.shape, F32),
            pltpu.VMEM(up.shape, F32), pltpu.VMEM(down.shape, F32),
            pltpu.VMEM((half, 3 * D), F32), pltpu.VMEM((half, D), F32),
            pltpu.SemaphoreType.DMA((6,)), pltpu.SemaphoreType.DMA((6,)),
        ],
        compiler_params=pltpu.CompilerParams(vmem_limit_bytes=44 * MIB),
        cost_estimate=cost(NS_ITERS * 14.0 * D * D * D, 4e6),
        name="newton_schulz_small",
    )(here, moment, large_whole, m_other, x, x_other, up, down)


def step_small_kernel(
    here_ref, x_ref, x_other_ref, qkv_ref, proj_ref, sum_ref, vec_ref, one_ref, two_ref,
    qkv_w_ref, proj_w_ref, vec_out, one_out, two_out,
):
    first = here_ref[1] == 0
    j = pl.program_id(0)
    x, x_other = x_ref[...].astype(F32), x_other_ref[...].astype(F32)
    qkv_w_ref[...] = qkv_ref[...] - rate(D, 3 * D) * jnp.where(first, x_other, x)

    @pl.when(j == 0)
    def _():
        proj_w_ref[...] = proj_ref[...] - rate(D, D) * jnp.where(first, x, x_other)
        whole = sum_ref[...].astype(F32)
        own = jnp.where(here_ref[0] == 0, whole[:6], whole[6:12])
        one = beta_first * one_ref[...] + (1.0 - beta_first) * own
        two = beta_second * two_ref[...] + (1.0 - beta_second) * own * own
        one_out[...] = one
        two_out[...] = two
        fix_first = 1.0 - beta_first**STEP
        fix_second = 1.0 - beta_second**STEP
        vec_out[...] = vec_ref[...] - adam_rate * (
            one / fix_first / (jnp.sqrt(two / fix_second) + adam_epsilon)
            + weight_decay * vec_ref[...]
        )


def step_small(here, x, x_other, qkv, proj, vec_sum, vectors, vec_first, vec_second):
    half = D // 2
    across = pl.BlockSpec((half, D), lambda j, here: (0, j))
    along = pl.BlockSpec((half, D), lambda j, here: (j, 0))
    alone = fixed((half, D))
    rows = fixed(vectors.shape)
    shapes = (qkv.shape, proj.shape) + (vectors.shape,) * 3
    return pl.pallas_call(
        step_small_kernel,
        grid_spec=pltpu.PrefetchScalarGridSpec(
            num_scalar_prefetch=1,
            grid=(3,),
            in_specs=[along, along, across, alone, fixed(vec_sum.shape), rows, rows, rows],
            out_specs=[across, alone, rows, rows, rows],
        ),
        out_shape=[jax.ShapeDtypeStruct(s, F32) for s in shapes],
        compiler_params=pltpu.CompilerParams(
            dimension_semantics=("arbitrary",), vmem_limit_bytes=20 * MIB
        ),
        cost_estimate=cost(4e6, 6e6),
        name="step_small",
    )(here, x, x_other, qkv, proj, vec_sum, vectors, vec_first, vec_second)


def after(value, *others):
    for other in others:
        row = other.reshape(-1, other.shape[-1])[:1, :D].astype(F32) * 0.0
        value = (value.astype(F32) + row).astype(value.dtype)
    return value


class Place:
    def __init__(self):
        self.dp = lax.axis_index("dp")
        self.y = lax.axis_index("fsdp")
        self.bits = [1 << k for k in range(lax.axis_size("dp").bit_length() - 1)]

    def high(self, bit):
        return (self.y if bit == "y" else self.dp & bit) != 0

    def swap(self, value, bit):
        if bit == "y":
            return lax.ppermute(value, "fsdp", [(0, 1), (1, 0)])
        size = lax.axis_size("dp")
        return lax.ppermute(value, "dp", [(i, i ^ bit) for i in range(size)])

    def join(self, mine, theirs, bit, axis):
        return jnp.where(
            self.high(bit),
            jnp.concatenate([theirs, mine], axis),
            jnp.concatenate([mine, theirs], axis),
        )

    def halves(self, value, bit):
        axis = 0 if bit == "y" else 1
        middle = value.shape[axis] // 2
        low = lax.slice_in_dim(value, 0, middle, axis=axis)
        high = lax.slice_in_dim(value, middle, 2 * middle, axis=axis)
        flag = self.high(bit)
        return jnp.where(flag, high, low), jnp.where(flag, low, high)


class Chain:
    def __init__(self, place, grad, order, rider=None):
        self.place, self.value, self.order, self.rider = place, grad, list(order), rider
        self.offset = jnp.int32(0)

    def send(self, k):
        self.keep, out = self.place.halves(self.value, self.order[k])
        if self.rider is None:
            return out
        return jnp.concatenate([out.reshape(-1, D), self.rider], 0)

    def add(self, got, k):
        self.last = got
        if self.rider is not None:
            self.rider = (self.rider.astype(F32) + got[-16:].astype(F32)).astype(BF)
            got = got[:-16].reshape(self.keep.shape)
        self.value = (self.keep.astype(F32) + got.astype(F32)).astype(BF)
        if self.order[k] != "y":
            self.offset = self.offset + jnp.where(
                self.place.high(self.order[k]), self.value.shape[1], 0
            )

    def scatter(self, steps, *waits):
        for k in steps:
            self.add(after(self.place.swap(self.send(k), self.order[k]), *waits), k)

    def decay(self, rows_at):
        own = rows_at(self.offset, self.value.shape[1])
        self.value = (momentum_decay * own[None] + self.value.astype(F32)).astype(BF)

    def gather(self, steps=None, *waits):
        for k in reversed(range(len(self.order))) if steps is None else steps:
            bit = self.order[k]
            self.last = self.place.swap(self.value, bit)
            theirs = after(self.last, *waits)
            self.value = self.place.join(self.value, theirs, bit, 0 if bit == "y" else 1)
        return self.value


def blocked(matrix):
    rows, cols = matrix.shape
    return matrix.reshape(rows, cols // D, D).transpose(1, 0, 2).reshape(-1, D)


def block_rows(matrix, offset, count):
    rows, cols = matrix.shape
    block = jnp.minimum(offset // rows, cols // D - 1)
    return lax.dynamic_slice(matrix, (offset % rows, block * D), (count, D))


def on_device(
    inputs, cotangent, segment_ids,
    qkv_weight, proj_weight, up_weight, down_weight, vectors,
    qkv_moment, proj_moment, up_moment, down_moment, vec_first, vec_second,
):
    place = Place()
    core, across, rest = place.bits[0], place.bits[1], place.bits[2:]
    half = D // 2
    here = jnp.stack([place.y, place.dp % 2]).astype(jnp.int32)
    first_core = place.dp % 2 == 0

    def core_part(value):
        middle = value.shape[0] // 2
        return jnp.where(first_core, value[:middle], value[middle:])

    vec_low = vectors.astype(BF)
    vec_other = place.swap(vec_low, "y")
    vec = place.join(vec_low, vec_other, "y", 0).astype(F32)
    qkv_own = qkv_weight.astype(BF)
    qkv_near = place.swap(core_part(qkv_own), "y")
    rest_own = jnp.concatenate([down_weight, blocked(up_weight), proj_weight], 0).astype(BF)
    qkv_far = place.swap(qkv_near, core)
    rest_part = after(core_part(rest_own), qkv_near, vec_other)
    qkv_parts = (qkv_own, qkv_near, qkv_far)
    rest_near = place.swap(rest_part, "y")
    qkv, attended, attended_t, weights = attend(here, inputs, qkv_parts, vec, segment_ids)
    rest_near = after(rest_near, attended)
    rest_parts = (rest_own, rest_near, place.swap(rest_near, core))

    layer_out, grad_first, grad_out, keep, send, grad_proj, vec_one = layer(
        here, inputs.reshape(-1, D), attended.reshape(-1, D), cotangent.reshape(-1, D), vec, rest_parts
    )
    got = place.swap(send, core)
    large = (keep.astype(F32) + got.astype(F32)).astype(BF)
    middle = large.shape[1] // 2
    chain_one = Chain(place, large[:, :middle], ["y", across])
    chain_two = Chain(place, large[:, middle:], [across, "y"])
    send_one, send_two = chain_one.send(0), chain_two.send(0)
    grad_out, send_one, send_two = lax.optimization_barrier((grad_out, send_one, send_two))
    chain_one.add(place.swap(send_one, "y"), 0)
    chain_two.add(place.swap(send_two, across), 0)

    grads = attend_pull(qkv, weights, attended_t, grad_out.reshape(inputs.shape))
    input_grad, keep, send, vec_sum = project_pull(
        here, inputs, grads, grad_first.reshape(inputs.shape), qkv_parts, grad_proj,
        after(vec_one, chain_one.last, chain_two.last),
    )
    chain_small = Chain(place, keep, [core, "y", across] + rest, vec_sum)
    chain_small.keep = keep

    chain_one.scatter([1])
    chain_two.scatter([1])
    apart = chain_one.value.shape[1]
    chain_both = Chain(place, jnp.concatenate([chain_one.value, chain_two.value], 1), rest)
    chain_both.value = after(chain_both.value, keep)
    chain_both.scatter(range(len(rest)))

    def large_rows(offset, count):
        offset = jnp.where(offset >= apart, middle - apart, 0) + chain_one.offset + offset
        return jnp.where(
            first_core, block_rows(up_moment, offset, count), block_rows(down_moment, offset, count)
        )

    chain_both.decay(large_rows)
    count = len(rest)
    chain_small.add(after(place.swap(send, core), chain_one.last, chain_two.last), 0)
    chain_small.scatter([1], chain_both.last)
    both = chain_both.gather([count - 1])
    chain_both.value = after(chain_both.value, chain_small.last)
    chain_small.scatter([2], chain_both.last)
    both = chain_both.gather(reversed(range(count - 1)))
    chain_small.scatter(range(3, 2 + count), chain_both.last)
    chain_one.value, chain_two.value = both[:, :apart], both[:, apart:]
    chain_one.gather([1])
    chain_two.gather([1])
    chain_small.scatter([2 + count], chain_one.last, chain_two.last)
    chain_small.decay(
        lambda offset, count: jnp.where(
            offset >= 3 * half,
            block_rows(proj_moment, offset % half, count),
            block_rows(qkv_moment, offset, count),
        )
    )
    chain_small.gather(reversed(range(3, 3 + count)))
    large_whole = jnp.concatenate([chain_one.gather([0]), chain_two.gather([0])], 1)
    chain_small.value = after(chain_small.value, chain_one.last, chain_two.last)
    chain_small.gather([2])
    large_whole = after(large_whole, chain_small.last)
    large_x = orthogonal_large(here, large_whole)
    large_other = place.swap(jnp.where(place.y != 0, large_whole[1], large_whole[0]), core)
    chain_small.gather([1], large_x)
    small_whole = chain_small.gather([0])
    (
        small_x, up_moment_new, down_moment_new, up_weight_new, down_weight_new,
        qkv_moment_new, proj_moment_new,
    ) = orthogonal_small(
        here, small_whole, large_whole, large_other, large_x,
        place.swap(after(large_x, large_other), core),
        up_weight, down_weight,
    )
    qkv_weight_new, proj_weight_new, vectors_new, vec_first_new, vec_second_new = step_small(
        here, small_x, place.swap(small_x, core), qkv_weight, proj_weight,
        chain_small.rider, vectors, vec_first, vec_second,
    )
    return (
        layer_out.reshape(inputs.shape),
        input_grad,
        qkv_moment_new,
        proj_moment_new,
        up_moment_new,
        down_moment_new,
        qkv_weight_new,
        proj_weight_new,
        up_weight_new,
        down_weight_new,
        vec_first_new,
        vec_second_new,
        vectors_new,
    )


def solution(mesh):
    tokens = P(("dp", "fsdp"), None, None)
    rows = P("fsdp", None)
    in_specs = (tokens, tokens, P(("dp", "fsdp"), None)) + (rows,) * 11
    out_specs = (tokens, tokens) + (rows,) * 11
    return jax.shard_map(
        on_device, mesh=mesh, in_specs=in_specs, out_specs=out_specs, check_vma=False
    )
```

```python
import functools
import math

import jax
import jax.numpy as jnp
from jax import lax
from jax.experimental import pallas as pl
from jax.experimental.pallas import tpu as pltpu
from jax.sharding import PartitionSpec as P

D = 512
HEADS = 8
HD = 64
FF = 2048
NS_ITERS = 5
STEP = 10
TILE = 512

norm_epsilon = 1e-12
momentum_decay = 0.95
muon_rate = 0.6
newton_a = 3.4445
newton_b = -4.775
newton_c = 2.0315
beta_first = 0.9
beta_second = 0.999
adam_rate = 0.2
weight_decay = 0.01
adam_epsilon = 1e-08
masked_score = -1e30
softmax_scale = 1.0 / math.sqrt(HD)

BF = jnp.bfloat16
F32 = jnp.float32
MIB = 1024 * 1024


def dot(left, right):
    return jnp.dot(left, right, preferred_element_type=F32)


def against(left, right):
    return lax.dot_general(left, right, (((1,), (1,)), ((), ())), preferred_element_type=F32)


def contract_rows(left, right):
    return lax.dot_general(left, right, (((0,), (0,)), ((), ())), preferred_element_type=F32)


def fixed(shape):
    return pl.BlockSpec(shape, lambda *_: (0,) * len(shape))


SCALARS = pl.BlockSpec(memory_space=pltpu.SMEM)


def compiler_params(mib, grid_rank=1):
    return pltpu.CompilerParams(
        dimension_semantics=("arbitrary",) * grid_rank, vmem_limit_bytes=mib * MIB
    )


def cost(flops, nbytes, trans=0):
    return pl.CostEstimate(flops=int(flops), bytes_accessed=int(nbytes), transcendentals=int(trans))


def place_rows(whole, here_ref, own, near, far):
    y, core = here_ref[0], here_ref[1]
    part = near.shape[0]
    start = lambda k: pl.ds(pl.multiple_of(k * part, part), part)
    whole[y] = own[...]
    whole[1 - y, start(core)] = near[...]
    whole[1 - y, start(1 - core)] = far[...]


def attend_kernel(
    here_ref, x_ref, own_ref, near_ref, far_ref, vec_ref, seg_ref,
    qkv_ref, o_ref, ot_ref, at_ref,
    w_s, qt_s, vt_s,
):
    @pl.when(pl.program_id(0) == 0)
    def _():
        place_rows(w_s, here_ref, own_ref, near_ref, far_ref)

    projected = dot(x_ref[0], w_s[...].reshape(D, 3 * D))
    queries = (projected[:, :D] + vec_ref[0:1, :]).astype(BF)
    keys = projected[:, D : 2 * D].astype(BF)
    values = (projected[:, 2 * D :] + vec_ref[1:2, :]).astype(BF)
    qkv_ref[0, :, :D] = queries
    qkv_ref[0, :, D : 2 * D] = keys
    qkv_ref[0, :, 2 * D :] = values
    qt_s[...] = (queries.astype(F32) * softmax_scale).T.astype(BF)
    vt_s[...] = values.astype(F32).T.astype(BF)
    document = seg_ref[0].astype(F32)
    same = jnp.broadcast_to(document, (8, document.shape[1])).T[:, :1] == document
    for head in range(HEADS):
        rows = slice(head * HD, (head + 1) * HD)
        scores = dot(keys[:, rows], qt_s[rows, :])
        scores = jnp.where(same, scores, masked_score)
        exponent = jnp.exp(scores - jnp.max(scores, 0, keepdims=True))
        weights = (exponent * (1.0 / jnp.sum(exponent, 0, keepdims=True))).astype(BF)
        at_ref[0, head] = weights
        ot_ref[0, rows, :] = dot(vt_s[rows, :], weights).astype(BF)
    o_ref[0] = ot_ref[0].astype(F32).T.astype(BF)


def attend(here, x, qkv_parts, vec, segment_ids):
    count, length = segment_ids.shape
    item = lambda *shape: pl.BlockSpec((1,) + shape, lambda i: (i,) + (0,) * len(shape))
    return pl.pallas_call(
        attend_kernel,
        grid=(count,),
        in_specs=[
            SCALARS, item(length, D), *[fixed(p.shape) for p in qkv_parts], fixed(vec.shape),
            item(1, length),
        ],
        out_specs=[item(length, 3 * D), item(length, D), item(D, length), item(HEADS, length, length)],
        out_shape=[
            jax.ShapeDtypeStruct((count, length, 3 * D), BF),
            jax.ShapeDtypeStruct((count, length, D), BF),
            jax.ShapeDtypeStruct((count, D, length), BF),
            jax.ShapeDtypeStruct((count, HEADS, length, length), BF),
        ],
        scratch_shapes=[
            pltpu.VMEM((2, D // 2, 3 * D), BF),
            pltpu.VMEM((D, length), BF),
            pltpu.VMEM((D, length), BF),
        ],
        compiler_params=compiler_params(36),
        cost_estimate=cost(count * 8e9, 3e7),
        name="attend_forward",
    )(here, x, *qkv_parts, vec, segment_ids[:, None, :])


def normed(values):
    center = values - jnp.mean(values, -1, keepdims=True)
    factor = lax.rsqrt(jnp.mean(center * center, -1, keepdims=True) + norm_epsilon)
    return center * factor, factor


def norm_pull(scaled, unit, factor):
    return factor * (
        scaled
        - jnp.mean(scaled, -1, keepdims=True)
        - unit * jnp.mean(scaled * unit, -1, keepdims=True)
    )


def gelu_and_slope(u):
    cdf = 0.5 + 0.5 * lax.erf(u * math.sqrt(0.5))
    return u * cdf, cdf + u * (jnp.exp(-0.5 * u * u) * (1.0 / math.sqrt(2.0 * math.pi)))


def colsum(values):
    return jnp.sum(values, 0, keepdims=True)


def layer_kernel(
    here_ref, x_ref, o_ref, cot_ref, vec_ref, own_ref, near_ref, far_ref,
    out_ref, dy_ref, do_ref, keep_ref, send_ref, gproj_ref, gvec_ref,
    w_s, acc_d, acc_u, acc_p, e_s, s_s,
):
    step = pl.program_id(0)
    half = D // 2

    @pl.when(step == 0)
    def _():
        place_rows(w_s, here_ref, own_ref, near_ref, far_ref)
        acc_d[...] = jnp.zeros_like(acc_d)
        acc_u[...] = jnp.zeros_like(acc_u)
        acc_p[...] = jnp.zeros_like(acc_p)
        gvec_ref[...] = jnp.zeros_like(gvec_ref)

    def rows_of(start):
        return jnp.concatenate([w_s[0, start : start + half], w_s[1, start : start + half]], 0)

    down_block = lambda j: w_s[j // 2, (j % 2) * D : (j % 2 + 1) * D, :]
    up_block = lambda j: rows_of(FF // 2 + j * half)
    row = lambda i: vec_ref[i : i + 1, :]
    attended = o_ref[...]
    proj = rows_of(FF)
    unit_one, factor_one = normed(x_ref[...].astype(F32) + (dot(attended, proj) + row(2)))
    hidden = unit_one * row(3) + row(4)
    hidden_low = hidden.astype(BF)
    total = jnp.zeros_like(hidden)
    for j in range(FF // D):
        cols = slice(j * D, (j + 1) * D)
        active, slope = gelu_and_slope(dot(hidden_low, up_block(j)) + row(8 + j))
        active = active.astype(BF)
        e_s[:, cols] = active
        s_s[:, cols] = slope
        total += dot(active, down_block(j))
    unit_two, factor_two = normed(hidden + (total + row(5)))
    out_ref[...] = unit_two * row(6) + row(7)
    cot = cot_ref[...].astype(F32)
    gvec_ref[6:7, :] += colsum(cot * unit_two)
    gvec_ref[7:8, :] += colsum(cot)
    grad_second = norm_pull(cot * row(6), unit_two, factor_two)
    grad_low = grad_second.astype(BF)
    gvec_ref[5:6, :] += colsum(grad_low.astype(F32))
    grad_hidden = grad_second
    for j in range(FF // D):
        cols = slice(j * D, (j + 1) * D)
        grad_up = (against(grad_low, down_block(j)) * s_s[:, cols]).astype(BF)
        gvec_ref[8 + j : 9 + j, :] += colsum(grad_up.astype(F32))
        acc_d[cols, :] += contract_rows(e_s[:, cols], grad_low)
        acc_u[:, cols] += contract_rows(hidden_low, grad_up)
        grad_hidden += against(grad_up, up_block(j))
    gvec_ref[3:4, :] += colsum(grad_hidden * unit_one)
    gvec_ref[4:5, :] += colsum(grad_hidden)
    grad_first = norm_pull(grad_hidden * row(3), unit_one, factor_one)
    dy_ref[...] = grad_first
    branch_low = grad_first.astype(BF)
    gvec_ref[2:3, :] += colsum(branch_low.astype(F32))
    acc_p[...] += contract_rows(attended, branch_low)
    do_ref[...] = against(branch_low, proj).astype(BF)

    @pl.when(step == pl.num_programs(0) - 1)
    def _():
        def put(up_ref, down_ref):
            for y in range(2):
                rows = slice(y * half, (y + 1) * half)
                down_ref[y] = acc_d[y * (FF // 2) : (y + 1) * (FF // 2), :].astype(BF)
                for j in range(FF // D):
                    cols = slice(j * D, (j + 1) * D)
                    up_ref[y, j * half : (j + 1) * half, :] = acc_u[rows, cols].astype(BF)

        for y in range(2):
            gproj_ref[y] = acc_p[y * half : (y + 1) * half, :].astype(BF)

        @pl.when(here_ref[1] == 0)
        def _():
            put(keep_ref, send_ref)

        @pl.when(here_ref[1] != 0)
        def _():
            put(send_ref, keep_ref)


def layer(here, x_rows, attended, cot_rows, vec, parts):
    tokens = x_rows.shape[0]
    tile = pl.BlockSpec((TILE, D), lambda i: (i, 0))
    shapes = [
        ((tokens, D), F32), ((tokens, D), F32), ((tokens, D), BF),
        ((2, FF // 2, D), BF), ((2, FF // 2, D), BF), ((2, D // 2, D), BF), ((16, D), F32),
    ]
    return pl.pallas_call(
        layer_kernel,
        grid=(tokens // TILE,),
        in_specs=[SCALARS, tile, tile, tile, fixed(vec.shape)] + [fixed(p.shape) for p in parts],
        out_specs=[tile, tile, tile] + [fixed(s) for s, _ in shapes[3:]],
        out_shape=[jax.ShapeDtypeStruct(s, t) for s, t in shapes],
        scratch_shapes=[
            pltpu.VMEM((2,) + parts[0].shape, BF),
            pltpu.VMEM((FF, D), F32),
            pltpu.VMEM((D, FF), F32),
            pltpu.VMEM((D, D), F32),
            pltpu.VMEM((TILE, FF), BF),
            pltpu.VMEM((TILE, FF), F32),
        ],
        compiler_params=compiler_params(46),
        cost_estimate=cost(tokens * 3e7, 2e7),
        name="layer_both_ways",
    )(here, x_rows, attended, cot_rows, vec, *parts)


def attend_pull_kernel(q_ref, k_ref, v_ref, at_ref, ot_ref, do_ref, dq_ref, dk_ref, dv_ref, dqt_s):
    grad_out_t = do_ref[0].astype(F32).T.astype(BF)
    keys_t = k_ref[0].astype(F32).T.astype(BF)
    for head in range(2):
        rows = slice(head * HD, (head + 1) * HD)
        grad_out = grad_out_t[rows, :]
        delta = colsum(grad_out.astype(F32) * ot_ref[0, rows, :].astype(F32))
        weights = at_ref[0, head]
        grad_probs = dot(v_ref[0, :, rows], grad_out)
        grad_scores = (weights.astype(F32) * (grad_probs - delta)).astype(BF)
        dv_ref[0, :, rows] = dot(weights, do_ref[0, :, rows]).astype(BF)
        dk_ref[0, :, rows] = (dot(grad_scores, q_ref[0, :, rows]) * softmax_scale).astype(BF)
        dqt_s[rows, :] = dot(keys_t[rows, :], grad_scores) * softmax_scale
    dq_ref[0] = dqt_s[...].T.astype(BF)


def attend_pull(qkv, weights, attended_t, grad_out):
    count, length, _ = qkv.shape
    pairs, wide = HEADS // 2, 2 * HD
    third = lambda k: pl.BlockSpec((1, length, wide), lambda i, p: (i, 0, k * pairs + p))
    return pl.pallas_call(
        attend_pull_kernel,
        grid=(count, pairs),
        in_specs=[
            third(0), third(1), third(2),
            pl.BlockSpec((1, 2, length, length), lambda i, p: (i, p, 0, 0)),
            pl.BlockSpec((1, wide, length), lambda i, p: (i, p, 0)),
            third(0),
        ],
        out_specs=[third(0)] * 3,
        out_shape=[jax.ShapeDtypeStruct((count, length, D), BF)] * 3,
        scratch_shapes=[pltpu.VMEM((wide, length), F32)],
        compiler_params=compiler_params(56, 2),
        cost_estimate=cost(count * 6e9, 2e7),
        name="attend_backward",
    )(qkv, qkv, qkv, weights, attended_t, grad_out)


def project_pull_kernel(
    here_ref, x_ref, dq_ref, dk_ref, dv_ref, dy_ref, own_ref, near_ref, far_ref, gproj_ref, vec_one_ref,
    gx_ref, keep_ref, send_ref, vec_out_ref,
    w_s, gvec_ref, acc,
):
    step = pl.program_id(0)

    @pl.when(step == 0)
    def _():
        place_rows(w_s, here_ref, own_ref, near_ref, far_ref)
        acc[...] = jnp.zeros_like(acc)
        gvec_ref[...] = vec_one_ref[...]

    gvec_ref[0:1, :] += colsum(dq_ref[0].astype(F32))
    gvec_ref[1:2, :] += colsum(dv_ref[0].astype(F32))
    total = dy_ref[0]
    for k, grad_ref_k in enumerate((dq_ref, dk_ref, dv_ref)):
        cols = slice(k * D, (k + 1) * D)
        grad = grad_ref_k[0]
        acc[:, cols] += contract_rows(x_ref[0], grad)
        total += against(grad, w_s[:, :, cols].reshape(D, D))
    gx_ref[0] = total

    @pl.when(step == pl.num_programs(0) - 1)
    def _():
        half = D // 2
        vec_low = gvec_ref[...].astype(BF)
        vec_out_ref[...] = vec_low
        send_ref[4 * half :, :] = vec_low

        def block(y, j):
            if j == 3:
                return gproj_ref[y]
            return acc[y * half : (y + 1) * half, j * D : (j + 1) * D].astype(BF)

        for core in range(2):

            @pl.when(here_ref[1] == core)
            def _():
                for y in range(2):
                    for j in range(2):
                        rows = slice((2 * y + j) * half, (2 * y + j + 1) * half)
                        keep_ref[y, j * half : (j + 1) * half, :] = block(y, 2 * core + j)
                        send_ref[rows, :] = block(y, 2 - 2 * core + j)


def project_pull(here, x, grads, grad_first, qkv_parts, grad_proj, vec_one):
    count, length, _ = x.shape
    item = pl.BlockSpec((1, length, D), lambda i: (i, 0, 0))
    return pl.pallas_call(
        project_pull_kernel,
        grid=(count,),
        in_specs=[SCALARS, item, item, item, item, item]
        + [fixed(p.shape) for p in qkv_parts]
        + [fixed((2, D // 2, D)), fixed((16, D))],
        out_specs=[item, fixed((2, D, D)), fixed((2 * D + 16, D)), fixed((16, D))],
        out_shape=[
            jax.ShapeDtypeStruct((count, length, D), F32),
            jax.ShapeDtypeStruct((2, D, D), BF),
            jax.ShapeDtypeStruct((2 * D + 16, D), BF),
            jax.ShapeDtypeStruct((16, D), BF),
        ],
        scratch_shapes=[
            pltpu.VMEM((2, D // 2, 3 * D), BF),
            pltpu.VMEM((16, D), F32),
            pltpu.VMEM((D, 3 * D), F32),
        ],
        compiler_params=compiler_params(36),
        cost_estimate=cost(count * 4e9, 1.5e7),
        name="project_backward",
    )(here, x, *grads, grad_first, *qkv_parts, grad_proj, vec_one)


def column_blocks(cols):
    return [slice(start, start + D) for start in range(0, cols, D)]


def normalize(cols, work, low):
    squares = sum(colsum(work[:, block] * work[:, block]) for block in column_blocks(cols))
    scale = 1.0 / (jnp.sqrt(jnp.sum(squares)) + 1e-07)
    for block in column_blocks(cols):
        made = work[:, block] * scale
        work[:, block] = made
        low[:, block] = made.astype(BF)


def iterate(cols, work, low):
    eye = lax.broadcasted_iota(jnp.int32, (D, D), 0) == lax.broadcasted_iota(jnp.int32, (D, D), 1)
    gram = against(low[:, :cols], low[:, :cols])
    own = jnp.where(eye, gram, 0.0)
    down = jnp.sum(own, 1, keepdims=True)
    across = jnp.sum(own, 0, keepdims=True)
    rest = jnp.where(eye, 0.0, gram)
    rest_low = rest.astype(BF)
    square = dot(rest_low, rest_low)
    poly = rest * (newton_b + newton_c * (down + across)) + newton_c * square
    poly = jnp.where(eye, 0.0, poly).astype(BF)
    square_own = jnp.sum(jnp.where(eye, square, 0.0), 1, keepdims=True)
    factor = newton_a + newton_b * down + newton_c * (down * down + square_own)
    for block in column_blocks(cols):
        made = factor * work[:, block] + dot(poly, low[:, block])
        work[:, block] = made
        low[:, block] = made.astype(BF)


def load_blocks(m_ref, work, blocks):
    half = D // 2
    for k, j in enumerate(blocks):
        for y in range(2):
            rows = slice(y * half, (y + 1) * half)
            work[rows, k * D : (k + 1) * D] = m_ref[y, j * half : (j + 1) * half, :].astype(F32)


def store_blocks(y, out_ref, low, count):
    half = D // 2
    rows = pl.ds(pl.multiple_of(y * half, half), half)
    for k in range(count):
        out_ref[k * half : (k + 1) * half, :] = low[rows, k * D : (k + 1) * D]


def large_kernel(here_ref, m_ref, out_ref, work, low):
    y, core = here_ref[0], here_ref[1]
    blocks = FF // D

    @pl.when(core == 0)
    def _():
        load_blocks(m_ref, work, range(blocks))

    @pl.when(core != 0)
    def _():
        for j in range(blocks):
            rows = slice((j % 2) * D, (j % 2 + 1) * D)
            work[:, j * D : (j + 1) * D] = m_ref[j // 2, rows, :].astype(F32).T

    normalize(FF, work, low)

    @pl.loop(0, NS_ITERS)
    def _(_):
        iterate(FF, work, low)

    @pl.when(core == 0)
    def _():
        store_blocks(y, out_ref, low, blocks)

    for k in range(2):

        @pl.when((core != 0) & (y == k))
        def _():
            for j in range(blocks // 2):
                cols = slice((k * blocks // 2 + j) * D, (k * blocks // 2 + j + 1) * D)
                out_ref[j * D : (j + 1) * D, :] = work[:, cols].T.astype(BF)


def orthogonal_large(here, moment):
    blocks = FF // D
    return pl.pallas_call(
        large_kernel,
        in_specs=[SCALARS, pl.BlockSpec(memory_space=pltpu.VMEM)],
        out_specs=pl.BlockSpec(memory_space=pltpu.VMEM),
        out_shape=jax.ShapeDtypeStruct((FF // 2, D), BF),
        scratch_shapes=[pltpu.VMEM((D, FF), F32), pltpu.VMEM((D, FF), BF)],
        compiler_params=pltpu.CompilerParams(vmem_limit_bytes=48 * MIB),
        cost_estimate=cost(NS_ITERS * (4.0 * blocks + 2.0) * D * D * D, 4e6),
        name="newton_schulz_large",
    )(here, moment)


def rate(rows, cols):
    return muon_rate * math.sqrt(max(rows, cols) / rows)


def small_kernel(
    here_ref, m_ref, large_m, large_m_other, large_x, large_x_other, up_w, down_w,
    out_ref, up_m_new, down_m_new, up_w_new, down_w_new, qkv_m_new, proj_m_new,
    work, low, m_s, m_other_s, x_s, x_other_s, up_w_s, down_w_s,
    up_m_s, down_m_s, qkv_m_s, proj_m_s, in_sems, out_sems,
):
    half = D // 2
    y, core = here_ref[0], here_ref[1]
    first = core == 0
    arrivals = [
        pltpu.make_async_copy(source, target, in_sems.at[k])
        for k, (source, target) in enumerate(
            [
                (large_m.at[y], m_s), (large_m_other, m_other_s), (large_x, x_s),
                (large_x_other, x_other_s), (up_w, up_w_s), (down_w, down_w_s),
            ]
        )
    ]
    results = [
        pltpu.make_async_copy(source, target, out_sems.at[k])
        for k, (source, target) in enumerate(
            [
                (up_m_s, up_m_new), (down_m_s, down_m_new), (up_w_s, up_w_new),
                (down_w_s, down_w_new), (qkv_m_s, qkv_m_new), (proj_m_s, proj_m_new),
            ]
        )
    ]
    for copy in arrivals:
        copy.start()

    @pl.when(first)
    def _():
        load_blocks(m_ref, work, [3])
        normalize(D, work, low)

    @pl.when(core != 0)
    def _():
        load_blocks(m_ref, work, range(3))
        normalize(3 * D, work, low)

    @pl.loop(0, NS_ITERS)
    def _(step):
        @pl.when(first)
        def _():
            iterate(D, work, low)

        @pl.when(core != 0)
        def _():
            iterate(3 * D, work, low)

        @pl.when(step == 1)
        def _():
            for copy in arrivals:
                copy.wait()
            for j in range(FF // D):
                rows, cols = slice(j * half, (j + 1) * half), slice(j * D, (j + 1) * D)
                m, m_other = m_s[rows, :].astype(F32), m_other_s[rows, :].astype(F32)
                x, x_other = x_s[rows, :].astype(F32), x_other_s[rows, :].astype(F32)
                up_m_s[:, cols] = jnp.where(first, m, m_other)
                down_m_s[rows, :] = jnp.where(first, m_other, m)
                up_w_s[:, cols] -= rate(D, FF) * jnp.where(first, x, x_other)
                down_w_s[rows, :] -= rate(FF, D) * jnp.where(first, x_other, x)
                own = m_ref[y, rows, :].astype(F32)
                if j < 3:
                    qkv_m_s[:, cols] = own
                else:
                    proj_m_s[...] = own
            for copy in results:
                copy.start()

    @pl.when(first)
    def _():
        out_ref[...] = jnp.zeros_like(out_ref)
        store_blocks(y, out_ref, low, 1)

    @pl.when(core != 0)
    def _():
        store_blocks(y, out_ref, low, 3)

    for copy in results:
        copy.wait()


def orthogonal_small(here, moment, large_whole, m_other, x, x_other, up, down):
    half = D // 2
    spaces = lambda kind, count: [pl.BlockSpec(memory_space=kind)] * count
    large = pltpu.VMEM((FF // 2, D), BF)
    shapes = [up.shape, down.shape, up.shape, down.shape, (half, 3 * D), (half, D)]
    return pl.pallas_call(
        small_kernel,
        in_specs=[SCALARS] + spaces(pltpu.VMEM, 1) + spaces(pl.ANY, 6),
        out_specs=spaces(pltpu.VMEM, 1) + spaces(pl.ANY, 6),
        out_shape=[jax.ShapeDtypeStruct((3 * half, D), BF)]
        + [jax.ShapeDtypeStruct(shape, F32) for shape in shapes],
        scratch_shapes=[
            pltpu.VMEM((D, 3 * D), F32), pltpu.VMEM((D, 3 * D), BF),
            large, large, large, large, pltpu.VMEM(up.shape, F32), pltpu.VMEM(down.shape, F32),
            pltpu.VMEM(up.shape, F32), pltpu.VMEM(down.shape, F32),
            pltpu.VMEM((half, 3 * D), F32), pltpu.VMEM((half, D), F32),
            pltpu.SemaphoreType.DMA((6,)), pltpu.SemaphoreType.DMA((6,)),
        ],
        compiler_params=pltpu.CompilerParams(vmem_limit_bytes=44 * MIB),
        cost_estimate=cost(NS_ITERS * 14.0 * D * D * D, 4e6),
        name="newton_schulz_small",
    )(here, moment, large_whole, m_other, x, x_other, up, down)


def step_small_kernel(
    here_ref, x_ref, x_other_ref, qkv_ref, proj_ref, sum_ref, vec_ref, one_ref, two_ref,
    qkv_w_ref, proj_w_ref, vec_out, one_out, two_out,
):
    first = here_ref[1] == 0
    j = pl.program_id(0)
    x, x_other = x_ref[...].astype(F32), x_other_ref[...].astype(F32)
    qkv_w_ref[...] = qkv_ref[...] - rate(D, 3 * D) * jnp.where(first, x_other, x)

    @pl.when(j == 0)
    def _():
        proj_w_ref[...] = proj_ref[...] - rate(D, D) * jnp.where(first, x, x_other)
        whole = sum_ref[...].astype(F32)
        own = jnp.where(here_ref[0] == 0, whole[:6], whole[6:12])
        one = beta_first * one_ref[...] + (1.0 - beta_first) * own
        two = beta_second * two_ref[...] + (1.0 - beta_second) * own * own
        one_out[...] = one
        two_out[...] = two
        fix_first = 1.0 - beta_first**STEP
        fix_second = 1.0 - beta_second**STEP
        vec_out[...] = vec_ref[...] - adam_rate * (
            one / fix_first / (jnp.sqrt(two / fix_second) + adam_epsilon)
            + weight_decay * vec_ref[...]
        )


def step_small(here, x, x_other, qkv, proj, vec_sum, vectors, vec_first, vec_second):
    half = D // 2
    across = pl.BlockSpec((half, D), lambda j, here: (0, j))
    along = pl.BlockSpec((half, D), lambda j, here: (j, 0))
    alone = fixed((half, D))
    rows = fixed(vectors.shape)
    shapes = (qkv.shape, proj.shape) + (vectors.shape,) * 3
    return pl.pallas_call(
        step_small_kernel,
        grid_spec=pltpu.PrefetchScalarGridSpec(
            num_scalar_prefetch=1,
            grid=(3,),
            in_specs=[along, along, across, alone, fixed(vec_sum.shape), rows, rows, rows],
            out_specs=[across, alone, rows, rows, rows],
        ),
        out_shape=[jax.ShapeDtypeStruct(s, F32) for s in shapes],
        compiler_params=pltpu.CompilerParams(
            dimension_semantics=("arbitrary",), vmem_limit_bytes=20 * MIB
        ),
        cost_estimate=cost(4e6, 6e6),
        name="step_small",
    )(here, x, x_other, qkv, proj, vec_sum, vectors, vec_first, vec_second)


def after(value, *others):
    for other in others:
        row = other.reshape(-1, other.shape[-1])[:1, :D].astype(F32) * 0.0
        value = (value.astype(F32) + row).astype(value.dtype)
    return value


class Place:
    def __init__(self):
        self.dp = lax.axis_index("dp")
        self.y = lax.axis_index("fsdp")
        self.bits = [1 << k for k in range(lax.axis_size("dp").bit_length() - 1)]

    def high(self, bit):
        return (self.y if bit == "y" else self.dp & bit) != 0

    def swap(self, value, bit):
        if bit == "y":
            return lax.ppermute(value, "fsdp", [(0, 1), (1, 0)])
        size = lax.axis_size("dp")
        return lax.ppermute(value, "dp", [(i, i ^ bit) for i in range(size)])

    def join(self, mine, theirs, bit, axis):
        return jnp.where(
            self.high(bit),
            jnp.concatenate([theirs, mine], axis),
            jnp.concatenate([mine, theirs], axis),
        )

    def halves(self, value, bit):
        axis = 0 if bit == "y" else 1
        middle = value.shape[axis] // 2
        low = lax.slice_in_dim(value, 0, middle, axis=axis)
        high = lax.slice_in_dim(value, middle, 2 * middle, axis=axis)
        flag = self.high(bit)
        return jnp.where(flag, high, low), jnp.where(flag, low, high)


class Chain:
    def __init__(self, place, grad, order, rider=None):
        self.place, self.value, self.order, self.rider = place, grad, list(order), rider
        self.offset = jnp.int32(0)

    def send(self, k):
        self.keep, out = self.place.halves(self.value, self.order[k])
        if self.rider is None:
            return out
        return jnp.concatenate([out.reshape(-1, D), self.rider], 0)

    def add(self, got, k):
        self.last = got
        if self.rider is not None:
            self.rider = (self.rider.astype(F32) + got[-16:].astype(F32)).astype(BF)
            got = got[:-16].reshape(self.keep.shape)
        self.value = (self.keep.astype(F32) + got.astype(F32)).astype(BF)
        if self.order[k] != "y":
            self.offset = self.offset + jnp.where(
                self.place.high(self.order[k]), self.value.shape[1], 0
            )

    def scatter(self, steps, *waits):
        for k in steps:
            self.add(after(self.place.swap(self.send(k), self.order[k]), *waits), k)

    def decay(self, rows_at):
        own = rows_at(self.offset, self.value.shape[1])
        self.value = (momentum_decay * own[None] + self.value.astype(F32)).astype(BF)

    def gather(self, steps=None, *waits):
        for k in reversed(range(len(self.order))) if steps is None else steps:
            bit = self.order[k]
            self.last = self.place.swap(self.value, bit)
            theirs = after(self.last, *waits)
            self.value = self.place.join(self.value, theirs, bit, 0 if bit == "y" else 1)
        return self.value


def blocked(matrix):
    rows, cols = matrix.shape
    return matrix.reshape(rows, cols // D, D).transpose(1, 0, 2).reshape(-1, D)


def block_rows(matrix, offset, count):
    rows, cols = matrix.shape
    block = jnp.minimum(offset // rows, cols // D - 1)
    return lax.dynamic_slice(matrix, (offset % rows, block * D), (count, D))


def on_device(
    inputs, cotangent, segment_ids,
    qkv_weight, proj_weight, up_weight, down_weight, vectors,
    qkv_moment, proj_moment, up_moment, down_moment, vec_first, vec_second,
):
    place = Place()
    core, across, rest = place.bits[0], place.bits[1], place.bits[2:]
    half = D // 2
    here = jnp.stack([place.y, place.dp % 2]).astype(jnp.int32)
    first_core = place.dp % 2 == 0

    def core_part(value):
        middle = value.shape[0] // 2
        return jnp.where(first_core, value[:middle], value[middle:])

    vec_low = vectors.astype(BF)
    vec_other = place.swap(vec_low, "y")
    vec = place.join(vec_low, vec_other, "y", 0).astype(F32)
    qkv_own = qkv_weight.astype(BF)
    qkv_near = place.swap(core_part(qkv_weight).astype(BF), "y")
    rest_own = jnp.concatenate([down_weight, blocked(up_weight), proj_weight], 0).astype(BF)
    qkv_far = place.swap(qkv_near, core)
    rest_part = after(core_part(rest_own), qkv_near, vec_other)
    qkv_parts = (qkv_own, qkv_near, qkv_far)
    rest_near = place.swap(rest_part, "y")
    qkv, attended, attended_t, weights = attend(here, inputs, qkv_parts, vec, segment_ids)
    rest_near = after(rest_near, attended)
    rest_parts = (rest_own, rest_near, place.swap(rest_near, core))

    layer_out, grad_first, grad_out, keep, send, grad_proj, vec_one = layer(
        here, inputs.reshape(-1, D), attended.reshape(-1, D), cotangent.reshape(-1, D), vec, rest_parts
    )
    got = place.swap(send, core)
    large = (keep.astype(F32) + got.astype(F32)).astype(BF)
    middle = large.shape[1] // 2
    chain_one = Chain(place, large[:, :middle], ["y", across])
    chain_two = Chain(place, large[:, middle:], [across, "y"])
    send_one, send_two = chain_one.send(0), chain_two.send(0)
    grad_out, send_one, send_two = lax.optimization_barrier((grad_out, send_one, send_two))
    chain_one.add(place.swap(send_one, "y"), 0)
    chain_two.add(place.swap(send_two, across), 0)

    grads = attend_pull(qkv, weights, attended_t, grad_out.reshape(inputs.shape))
    input_grad, keep, send, vec_sum = project_pull(
        here, inputs, grads, grad_first.reshape(inputs.shape), qkv_parts, grad_proj,
        after(vec_one, chain_one.last, chain_two.last),
    )
    chain_small = Chain(place, keep, [core, "y", across] + rest, vec_sum)
    chain_small.keep = keep

    chain_one.scatter([1])
    chain_two.scatter([1])
    apart = chain_one.value.shape[1]
    chain_both = Chain(place, jnp.concatenate([chain_one.value, chain_two.value], 1), rest)
    chain_both.value = after(chain_both.value, keep)
    chain_both.scatter(range(len(rest)))

    def large_rows(offset, count):
        offset = jnp.where(offset >= apart, middle - apart, 0) + chain_one.offset + offset
        return jnp.where(
            first_core, block_rows(up_moment, offset, count), block_rows(down_moment, offset, count)
        )

    chain_both.decay(large_rows)
    count = len(rest)
    chain_small.add(after(place.swap(send, core), chain_one.last, chain_two.last), 0)
    chain_small.scatter([1], chain_both.last)
    both = chain_both.gather([count - 1])
    chain_both.value = after(chain_both.value, chain_small.last)
    chain_small.scatter([2], chain_both.last)
    both = chain_both.gather(reversed(range(count - 1)))
    chain_small.scatter(range(3, 2 + count), chain_both.last)
    chain_one.value, chain_two.value = both[:, :apart], both[:, apart:]
    chain_one.gather([1])
    chain_two.gather([1])
    chain_small.scatter([2 + count], chain_one.last, chain_two.last)
    chain_small.decay(
        lambda offset, count: jnp.where(
            offset >= 3 * half,
            block_rows(proj_moment, offset % half, count),
            block_rows(qkv_moment, offset, count),
        )
    )
    chain_small.gather(reversed(range(3, 3 + count)))
    large_whole = jnp.concatenate([chain_one.gather([0]), chain_two.gather([0])], 1)
    chain_small.value = after(chain_small.value, chain_one.last, chain_two.last)
    chain_small.gather([2])
    large_whole = after(large_whole, chain_small.last)
    large_x = orthogonal_large(here, large_whole)
    large_other = place.swap(jnp.where(place.y != 0, large_whole[1], large_whole[0]), core)
    chain_small.gather([1], large_x)
    small_whole = chain_small.gather([0])
    (
        small_x, up_moment_new, down_moment_new, up_weight_new, down_weight_new,
        qkv_moment_new, proj_moment_new,
    ) = orthogonal_small(
        here, small_whole, large_whole, large_other, large_x,
        place.swap(after(large_x, large_other), core),
        up_weight, down_weight,
    )
    qkv_weight_new, proj_weight_new, vectors_new, vec_first_new, vec_second_new = step_small(
        here, small_x, place.swap(small_x, core), qkv_weight, proj_weight,
        chain_small.rider, vectors, vec_first, vec_second,
    )
    return (
        layer_out.reshape(inputs.shape),
        input_grad,
        qkv_moment_new,
        proj_moment_new,
        up_moment_new,
        down_moment_new,
        qkv_weight_new,
        proj_weight_new,
        up_weight_new,
        down_weight_new,
        vec_first_new,
        vec_second_new,
        vectors_new,
    )


def solution(mesh):
    tokens = P(("dp", "fsdp"), None, None)
    rows = P("fsdp", None)
    in_specs = (tokens, tokens, P(("dp", "fsdp"), None)) + (rows,) * 11
    out_specs = (tokens, tokens) + (rows,) * 11
    return jax.shard_map(
        on_device, mesh=mesh, in_specs=in_specs, out_specs=out_specs, check_vma=False
    )
```

```python
import functools
import math

import jax
import jax.numpy as jnp
from jax import lax
from jax.experimental import pallas as pl
from jax.experimental.pallas import tpu as pltpu
from jax.sharding import PartitionSpec as P

D = 512
HEADS = 8
HD = 64
FF = 2048
NS_ITERS = 5
STEP = 10
TILE = 512

norm_epsilon = 1e-12
momentum_decay = 0.95
muon_rate = 0.6
newton_a = 3.4445
newton_b = -4.775
newton_c = 2.0315
beta_first = 0.9
beta_second = 0.999
adam_rate = 0.2
weight_decay = 0.01
adam_epsilon = 1e-08
masked_score = -1e30
softmax_scale = 1.0 / math.sqrt(HD)

BF = jnp.bfloat16
F32 = jnp.float32
MIB = 1024 * 1024


def dot(left, right):
    return jnp.dot(left, right, preferred_element_type=F32)


def against(left, right):
    return lax.dot_general(left, right, (((1,), (1,)), ((), ())), preferred_element_type=F32)


def contract_rows(left, right):
    return lax.dot_general(left, right, (((0,), (0,)), ((), ())), preferred_element_type=F32)


def fixed(shape):
    return pl.BlockSpec(shape, lambda *_: (0,) * len(shape))


SCALARS = pl.BlockSpec(memory_space=pltpu.SMEM)


def compiler_params(mib, grid_rank=1):
    return pltpu.CompilerParams(
        dimension_semantics=("arbitrary",) * grid_rank, vmem_limit_bytes=mib * MIB
    )


def cost(flops, nbytes, trans=0):
    return pl.CostEstimate(flops=int(flops), bytes_accessed=int(nbytes), transcendentals=int(trans))


def place_rows(whole, here_ref, own, near, far):
    y, core = here_ref[0], here_ref[1]
    part = near.shape[0]
    start = lambda k: pl.ds(pl.multiple_of(k * part, part), part)
    whole[y] = own[...]
    whole[1 - y, start(core)] = near[...]
    whole[1 - y, start(1 - core)] = far[...]


def attend_kernel(
    here_ref, x_ref, own_ref, near_ref, far_ref, vec_ref, seg_ref,
    qkv_ref, o_ref, ot_ref, at_ref,
    w_s, qt_s, vt_s,
):
    @pl.when(pl.program_id(0) == 0)
    def _():
        place_rows(w_s, here_ref, own_ref, near_ref, far_ref)

    projected = dot(x_ref[0], w_s[...].reshape(D, 3 * D))
    queries = (projected[:, :D] + vec_ref[0:1, :]).astype(BF)
    keys = projected[:, D : 2 * D].astype(BF)
    values = (projected[:, 2 * D :] + vec_ref[1:2, :]).astype(BF)
    qkv_ref[0, :, :D] = queries
    qkv_ref[0, :, D : 2 * D] = keys
    qkv_ref[0, :, 2 * D :] = values
    qt_s[...] = (queries.astype(F32) * softmax_scale).T.astype(BF)
    vt_s[...] = values.astype(F32).T.astype(BF)
    document = seg_ref[0].astype(F32)
    same = jnp.broadcast_to(document, (8, document.shape[1])).T[:, :1] == document
    for head in range(HEADS):
        rows = slice(head * HD, (head + 1) * HD)
        scores = dot(keys[:, rows], qt_s[rows, :])
        scores = jnp.where(same, scores, masked_score)
        exponent = jnp.exp(scores - jnp.max(scores, 0, keepdims=True))
        weights = (exponent * (1.0 / jnp.sum(exponent, 0, keepdims=True))).astype(BF)
        at_ref[0, head] = weights
        ot_ref[0, rows, :] = dot(vt_s[rows, :], weights).astype(BF)
    o_ref[0] = ot_ref[0].astype(F32).T.astype(BF)


def attend(here, x, qkv_parts, vec, segment_ids):
    count, length = segment_ids.shape
    item = lambda *shape: pl.BlockSpec((1,) + shape, lambda i: (i,) + (0,) * len(shape))
    return pl.pallas_call(
        attend_kernel,
        grid=(count,),
        in_specs=[
            SCALARS, item(length, D), *[fixed(p.shape) for p in qkv_parts], fixed(vec.shape),
            item(1, length),
        ],
        out_specs=[item(length, 3 * D), item(length, D), item(D, length), item(HEADS, length, length)],
        out_shape=[
            jax.ShapeDtypeStruct((count, length, 3 * D), BF),
            jax.ShapeDtypeStruct((count, length, D), BF),
            jax.ShapeDtypeStruct((count, D, length), BF),
            jax.ShapeDtypeStruct((count, HEADS, length, length), BF),
        ],
        scratch_shapes=[
            pltpu.VMEM((2, D // 2, 3 * D), BF),
            pltpu.VMEM((D, length), BF),
            pltpu.VMEM((D, length), BF),
        ],
        compiler_params=compiler_params(36),
        cost_estimate=cost(count * 8e9, 3e7),
        name="attend_forward",
    )(here, x, *qkv_parts, vec, segment_ids[:, None, :])


def normed(values):
    center = values - jnp.mean(values, -1, keepdims=True)
    factor = lax.rsqrt(jnp.mean(center * center, -1, keepdims=True) + norm_epsilon)
    return center * factor, factor


def norm_pull(scaled, unit, factor):
    return factor * (
        scaled
        - jnp.mean(scaled, -1, keepdims=True)
        - unit * jnp.mean(scaled * unit, -1, keepdims=True)
    )


def gelu_and_slope(u):
    cdf = 0.5 + 0.5 * lax.erf(u * math.sqrt(0.5))
    return u * cdf, cdf + u * (jnp.exp(-0.5 * u * u) * (1.0 / math.sqrt(2.0 * math.pi)))


def colsum(values):
    return jnp.sum(values, 0, keepdims=True)


def layer_kernel(
    here_ref, x_ref, o_ref, cot_ref, vec_ref, own_ref, near_ref, far_ref,
    out_ref, dy_ref, do_ref, keep_ref, send_ref, gproj_ref, gvec_ref,
    w_s, acc_d, acc_u, acc_p, e_s, s_s,
):
    step = pl.program_id(0)
    half = D // 2

    @pl.when(step == 0)
    def _():
        place_rows(w_s, here_ref, own_ref, near_ref, far_ref)
        acc_d[...] = jnp.zeros_like(acc_d)
        acc_u[...] = jnp.zeros_like(acc_u)
        acc_p[...] = jnp.zeros_like(acc_p)
        gvec_ref[...] = jnp.zeros_like(gvec_ref)

    def rows_of(start):
        return jnp.concatenate([w_s[0, start : start + half], w_s[1, start : start + half]], 0)

    down_block = lambda j: w_s[j // 2, (j % 2) * D : (j % 2 + 1) * D, :]
    up_block = lambda j: rows_of(FF // 2 + j * half)
    row = lambda i: vec_ref[i : i + 1, :]
    attended = o_ref[...]
    proj = rows_of(FF)
    unit_one, factor_one = normed(x_ref[...].astype(F32) + (dot(attended, proj) + row(2)))
    hidden = unit_one * row(3) + row(4)
    hidden_low = hidden.astype(BF)
    total = jnp.zeros_like(hidden)
    for j in range(FF // D):
        cols = slice(j * D, (j + 1) * D)
        active, slope = gelu_and_slope(dot(hidden_low, up_block(j)) + row(8 + j))
        active = active.astype(BF)
        e_s[:, cols] = active
        s_s[:, cols] = slope
        total += dot(active, down_block(j))
    unit_two, factor_two = normed(hidden + (total + row(5)))
    out_ref[...] = unit_two * row(6) + row(7)
    cot = cot_ref[...].astype(F32)
    gvec_ref[6:7, :] += colsum(cot * unit_two)
    gvec_ref[7:8, :] += colsum(cot)
    grad_second = norm_pull(cot * row(6), unit_two, factor_two)
    grad_low = grad_second.astype(BF)
    gvec_ref[5:6, :] += colsum(grad_low.astype(F32))
    grad_hidden = grad_second
    for j in range(FF // D):
        cols = slice(j * D, (j + 1) * D)
        grad_up = (against(grad_low, down_block(j)) * s_s[:, cols]).astype(BF)
        gvec_ref[8 + j : 9 + j, :] += colsum(grad_up.astype(F32))
        acc_d[cols, :] += contract_rows(e_s[:, cols], grad_low)
        acc_u[:, cols] += contract_rows(hidden_low, grad_up)
        grad_hidden += against(grad_up, up_block(j))
    gvec_ref[3:4, :] += colsum(grad_hidden * unit_one)
    gvec_ref[4:5, :] += colsum(grad_hidden)
    grad_first = norm_pull(grad_hidden * row(3), unit_one, factor_one)
    dy_ref[...] = grad_first
    branch_low = grad_first.astype(BF)
    gvec_ref[2:3, :] += colsum(branch_low.astype(F32))
    acc_p[...] += contract_rows(attended, branch_low)
    do_ref[...] = against(branch_low, proj).astype(BF)

    @pl.when(step == pl.num_programs(0) - 1)
    def _():
        def put(up_ref, down_ref):
            for y in range(2):
                rows = slice(y * half, (y + 1) * half)
                down_ref[y] = acc_d[y * (FF // 2) : (y + 1) * (FF // 2), :].astype(BF)
                for j in range(FF // D):
                    cols = slice(j * D, (j + 1) * D)
                    up_ref[y, j * half : (j + 1) * half, :] = acc_u[rows, cols].astype(BF)

        for y in range(2):
            gproj_ref[y] = acc_p[y * half : (y + 1) * half, :].astype(BF)

        @pl.when(here_ref[1] == 0)
        def _():
            put(keep_ref, send_ref)

        @pl.when(here_ref[1] != 0)
        def _():
            put(send_ref, keep_ref)


def layer(here, x_rows, attended, cot_rows, vec, parts):
    tokens = x_rows.shape[0]
    tile = pl.BlockSpec((TILE, D), lambda i: (i, 0))
    shapes = [
        ((tokens, D), F32), ((tokens, D), F32), ((tokens, D), BF),
        ((2, FF // 2, D), BF), ((2, FF // 2, D), BF), ((2, D // 2, D), BF), ((16, D), F32),
    ]
    return pl.pallas_call(
        layer_kernel,
        grid=(tokens // TILE,),
        in_specs=[SCALARS, tile, tile, tile, fixed(vec.shape)] + [fixed(p.shape) for p in parts],
        out_specs=[tile, tile, tile] + [fixed(s) for s, _ in shapes[3:]],
        out_shape=[jax.ShapeDtypeStruct(s, t) for s, t in shapes],
        scratch_shapes=[
            pltpu.VMEM((2,) + parts[0].shape, BF),
            pltpu.VMEM((FF, D), F32),
            pltpu.VMEM((D, FF), F32),
            pltpu.VMEM((D, D), F32),
            pltpu.VMEM((TILE, FF), BF),
            pltpu.VMEM((TILE, FF), F32),
        ],
        compiler_params=compiler_params(41),
        cost_estimate=cost(tokens * 3e7, 2e7),
        name="layer_both_ways",
    )(here, x_rows, attended, cot_rows, vec, *parts)


def attend_pull_kernel(q_ref, k_ref, v_ref, at_ref, ot_ref, do_ref, dq_ref, dk_ref, dv_ref, dqt_s):
    grad_out_t = do_ref[0].astype(F32).T.astype(BF)
    keys_t = k_ref[0].astype(F32).T.astype(BF)
    for head in range(2):
        rows = slice(head * HD, (head + 1) * HD)
        grad_out = grad_out_t[rows, :]
        delta = colsum(grad_out.astype(F32) * ot_ref[0, rows, :].astype(F32))
        weights = at_ref[0, head]
        grad_probs = dot(v_ref[0, :, rows], grad_out)
        grad_scores = (weights.astype(F32) * (grad_probs - delta)).astype(BF)
        dv_ref[0, :, rows] = dot(weights, do_ref[0, :, rows]).astype(BF)
        dk_ref[0, :, rows] = (dot(grad_scores, q_ref[0, :, rows]) * softmax_scale).astype(BF)
        dqt_s[rows, :] = dot(keys_t[rows, :], grad_scores) * softmax_scale
    dq_ref[0] = dqt_s[...].T.astype(BF)


def attend_pull(qkv, weights, attended_t, grad_out):
    count, length, _ = qkv.shape
    pairs, wide = HEADS // 2, 2 * HD
    third = lambda k: pl.BlockSpec((1, length, wide), lambda i, p: (i, 0, k * pairs + p))
    return pl.pallas_call(
        attend_pull_kernel,
        grid=(count, pairs),
        in_specs=[
            third(0), third(1), third(2),
            pl.BlockSpec((1, 2, length, length), lambda i, p: (i, p, 0, 0)),
            pl.BlockSpec((1, wide, length), lambda i, p: (i, p, 0)),
            third(0),
        ],
        out_specs=[third(0)] * 3,
        out_shape=[jax.ShapeDtypeStruct((count, length, D), BF)] * 3,
        scratch_shapes=[pltpu.VMEM((wide, length), F32)],
        compiler_params=compiler_params(56, 2),
        cost_estimate=cost(count * 6e9, 2e7),
        name="attend_backward",
    )(qkv, qkv, qkv, weights, attended_t, grad_out)


def project_pull_kernel(
    here_ref, x_ref, dq_ref, dk_ref, dv_ref, dy_ref, own_ref, near_ref, far_ref, gproj_ref, vec_one_ref,
    gx_ref, keep_ref, send_ref, vec_out_ref,
    w_s, gvec_ref, acc,
):
    step = pl.program_id(0)

    @pl.when(step == 0)
    def _():
        place_rows(w_s, here_ref, own_ref, near_ref, far_ref)
        acc[...] = jnp.zeros_like(acc)
        gvec_ref[...] = vec_one_ref[...]

    gvec_ref[0:1, :] += colsum(dq_ref[0].astype(F32))
    gvec_ref[1:2, :] += colsum(dv_ref[0].astype(F32))
    total = dy_ref[0]
    for k, grad_ref_k in enumerate((dq_ref, dk_ref, dv_ref)):
        cols = slice(k * D, (k + 1) * D)
        grad = grad_ref_k[0]
        acc[:, cols] += contract_rows(x_ref[0], grad)
        total += against(grad, w_s[:, :, cols].reshape(D, D))
    gx_ref[0] = total

    @pl.when(step == pl.num_programs(0) - 1)
    def _():
        half = D // 2
        vec_low = gvec_ref[...].astype(BF)
        vec_out_ref[...] = vec_low
        send_ref[4 * half :, :] = vec_low

        def block(y, j):
            if j == 3:
                return gproj_ref[y]
            return acc[y * half : (y + 1) * half, j * D : (j + 1) * D].astype(BF)

        for core in range(2):

            @pl.when(here_ref[1] == core)
            def _():
                for y in range(2):
                    for j in range(2):
                        rows = slice((2 * y + j) * half, (2 * y + j + 1) * half)
                        keep_ref[y, j * half : (j + 1) * half, :] = block(y, 2 * core + j)
                        send_ref[rows, :] = block(y, 2 - 2 * core + j)


def project_pull(here, x, grads, grad_first, qkv_parts, grad_proj, vec_one):
    count, length, _ = x.shape
    item = pl.BlockSpec((1, length, D), lambda i: (i, 0, 0))
    return pl.pallas_call(
        project_pull_kernel,
        grid=(count,),
        in_specs=[SCALARS, item, item, item, item, item]
        + [fixed(p.shape) for p in qkv_parts]
        + [fixed((2, D // 2, D)), fixed((16, D))],
        out_specs=[item, fixed((2, D, D)), fixed((2 * D + 16, D)), fixed((16, D))],
        out_shape=[
            jax.ShapeDtypeStruct((count, length, D), F32),
            jax.ShapeDtypeStruct((2, D, D), BF),
            jax.ShapeDtypeStruct((2 * D + 16, D), BF),
            jax.ShapeDtypeStruct((16, D), BF),
        ],
        scratch_shapes=[
            pltpu.VMEM((2, D // 2, 3 * D), BF),
            pltpu.VMEM((16, D), F32),
            pltpu.VMEM((D, 3 * D), F32),
        ],
        compiler_params=compiler_params(36),
        cost_estimate=cost(count * 4e9, 1.5e7),
        name="project_backward",
    )(here, x, *grads, grad_first, *qkv_parts, grad_proj, vec_one)


def column_blocks(cols):
    return [slice(start, start + D) for start in range(0, cols, D)]


def normalize(cols, work, low):
    squares = sum(colsum(work[:, block] * work[:, block]) for block in column_blocks(cols))
    scale = 1.0 / (jnp.sqrt(jnp.sum(squares)) + 1e-07)
    for block in column_blocks(cols):
        made = work[:, block] * scale
        work[:, block] = made
        low[:, block] = made.astype(BF)


def iterate(cols, work, low):
    eye = lax.broadcasted_iota(jnp.int32, (D, D), 0) == lax.broadcasted_iota(jnp.int32, (D, D), 1)
    gram = against(low[:, :cols], low[:, :cols])
    own = jnp.where(eye, gram, 0.0)
    down = jnp.sum(own, 1, keepdims=True)
    across = jnp.sum(own, 0, keepdims=True)
    rest = jnp.where(eye, 0.0, gram)
    rest_low = rest.astype(BF)
    square = dot(rest_low, rest_low)
    poly = rest * (newton_b + newton_c * (down + across)) + newton_c * square
    poly = jnp.where(eye, 0.0, poly).astype(BF)
    square_own = jnp.sum(jnp.where(eye, square, 0.0), 1, keepdims=True)
    factor = newton_a + newton_b * down + newton_c * (down * down + square_own)
    for block in column_blocks(cols):
        made = factor * work[:, block] + dot(poly, low[:, block])
        work[:, block] = made
        low[:, block] = made.astype(BF)


def load_blocks(work, blocks):
    half = D // 2
    for k, (ref, j) in enumerate(blocks):
        for y in range(2):
            rows = slice(y * half, (y + 1) * half)
            work[rows, k * D : (k + 1) * D] = ref[y, j * half : (j + 1) * half, :].astype(F32)


def store_blocks(y, out_ref, low, count):
    half = D // 2
    rows = pl.ds(pl.multiple_of(y * half, half), half)
    for k in range(count):
        out_ref[k * half : (k + 1) * half, :] = low[rows, k * D : (k + 1) * D]


def large_kernel(here_ref, m_ref, out_ref, work, low):
    y, core = here_ref[0], here_ref[1]
    blocks = FF // D

    @pl.when(core == 0)
    def _():
        load_blocks(work, [(m_ref, j) for j in range(blocks)])

    @pl.when(core != 0)
    def _():
        for j in range(blocks):
            rows = slice((j % 2) * D, (j % 2 + 1) * D)
            work[:, j * D : (j + 1) * D] = m_ref[j // 2, rows, :].astype(F32).T

    normalize(FF, work, low)

    @pl.loop(0, NS_ITERS)
    def _(_):
        iterate(FF, work, low)

    @pl.when(core == 0)
    def _():
        store_blocks(y, out_ref, low, blocks)

    for k in range(2):

        @pl.when((core != 0) & (y == k))
        def _():
            for j in range(blocks // 2):
                cols = slice((k * blocks // 2 + j) * D, (k * blocks // 2 + j + 1) * D)
                out_ref[j * D : (j + 1) * D, :] = work[:, cols].T.astype(BF)


def orthogonal_large(here, moment):
    blocks = FF // D
    return pl.pallas_call(
        large_kernel,
        in_specs=[SCALARS, pl.BlockSpec(memory_space=pltpu.VMEM)],
        out_specs=pl.BlockSpec(memory_space=pltpu.VMEM),
        out_shape=jax.ShapeDtypeStruct((FF // 2, D), BF),
        scratch_shapes=[pltpu.VMEM((D, FF), F32), pltpu.VMEM((D, FF), BF)],
        compiler_params=pltpu.CompilerParams(vmem_limit_bytes=32 * MIB),
        cost_estimate=cost(NS_ITERS * (4.0 * blocks + 2.0) * D * D * D, 4e6),
        name="newton_schulz_large",
    )(here, moment)


def rate(rows, cols):
    return muon_rate * math.sqrt(max(rows, cols) / rows)


def small_kernel(
    here_ref, mine_ref, other_ref, large_m, large_m_other, large_x, large_x_other, up_w, down_w,
    out_ref, up_m_new, down_m_new, up_w_new, down_w_new, qkv_m_new, proj_m_new,
    work, low, m_s, m_other_s, x_s, x_other_s, up_w_s, down_w_s,
    up_m_s, down_m_s, qkv_m_s, proj_m_s, in_sems, out_sems,
):
    half = D // 2
    y, core = here_ref[0], here_ref[1]
    first = core == 0
    arrivals = [
        pltpu.make_async_copy(source, target, in_sems.at[k])
        for k, (source, target) in enumerate(
            [
                (large_m.at[y], m_s), (large_m_other, m_other_s), (large_x, x_s),
                (large_x_other, x_other_s), (up_w, up_w_s), (down_w, down_w_s),
            ]
        )
    ]
    results = [
        pltpu.make_async_copy(source, target, out_sems.at[k])
        for k, (source, target) in enumerate(
            [
                (up_m_s, up_m_new), (down_m_s, down_m_new), (up_w_s, up_w_new),
                (down_w_s, down_w_new), (qkv_m_s, qkv_m_new), (proj_m_s, proj_m_new),
            ]
        )
    ]
    for copy in arrivals:
        copy.start()

    @pl.when(first)
    def _():
        load_blocks(work, [(other_ref, 1)])
        normalize(D, work, low)

    @pl.when(core != 0)
    def _():
        load_blocks(work, [(other_ref, 0), (other_ref, 1), (mine_ref, 0)])
        normalize(3 * D, work, low)

    @pl.loop(0, NS_ITERS)
    def _(step):
        @pl.when(first)
        def _():
            iterate(D, work, low)

        @pl.when(core != 0)
        def _():
            iterate(3 * D, work, low)

        @pl.when(step == 1)
        def _():
            for copy in arrivals:
                copy.wait()
            for j in range(FF // D):
                rows, cols = slice(j * half, (j + 1) * half), slice(j * D, (j + 1) * D)
                m, m_other = m_s[rows, :].astype(F32), m_other_s[rows, :].astype(F32)
                x, x_other = x_s[rows, :].astype(F32), x_other_s[rows, :].astype(F32)
                up_m_s[:, cols] = jnp.where(first, m, m_other)
                down_m_s[rows, :] = jnp.where(first, m_other, m)
                up_w_s[:, cols] -= rate(D, FF) * jnp.where(first, x, x_other)
                down_w_s[rows, :] -= rate(FF, D) * jnp.where(first, x_other, x)
                part = slice(j % 2 * half, (j % 2 + 1) * half)
                mine, other = mine_ref[y, part, :].astype(F32), other_ref[y, part, :].astype(F32)
                own = jnp.where(first == (j < 2), mine, other)
                if j < 3:
                    qkv_m_s[:, cols] = own
                else:
                    proj_m_s[...] = own
            for copy in results:
                copy.start()

    @pl.when(first)
    def _():
        out_ref[...] = jnp.zeros_like(out_ref)
        store_blocks(y, out_ref, low, 1)

    @pl.when(core != 0)
    def _():
        store_blocks(y, out_ref, low, 3)

    for copy in results:
        copy.wait()


def orthogonal_small(here, mine, other, large_whole, m_other, x, x_other, up, down):
    half = D // 2
    spaces = lambda kind, count: [pl.BlockSpec(memory_space=kind)] * count
    large = pltpu.VMEM((FF // 2, D), BF)
    shapes = [up.shape, down.shape, up.shape, down.shape, (half, 3 * D), (half, D)]
    return pl.pallas_call(
        small_kernel,
        in_specs=[SCALARS] + spaces(pltpu.VMEM, 2) + spaces(pl.ANY, 6),
        out_specs=spaces(pltpu.VMEM, 1) + spaces(pl.ANY, 6),
        out_shape=[jax.ShapeDtypeStruct((3 * half, D), BF)]
        + [jax.ShapeDtypeStruct(shape, F32) for shape in shapes],
        scratch_shapes=[
            pltpu.VMEM((D, 3 * D), F32), pltpu.VMEM((D, 3 * D), BF),
            large, large, large, large, pltpu.VMEM(up.shape, F32), pltpu.VMEM(down.shape, F32),
            pltpu.VMEM(up.shape, F32), pltpu.VMEM(down.shape, F32),
            pltpu.VMEM((half, 3 * D), F32), pltpu.VMEM((half, D), F32),
            pltpu.SemaphoreType.DMA((6,)), pltpu.SemaphoreType.DMA((6,)),
        ],
        compiler_params=pltpu.CompilerParams(vmem_limit_bytes=44 * MIB),
        cost_estimate=cost(NS_ITERS * 14.0 * D * D * D, 4e6),
        name="newton_schulz_small",
    )(here, mine, other, large_whole, m_other, x, x_other, up, down)


def step_small_kernel(
    here_ref, x_ref, x_other_ref, qkv_ref, proj_ref, sum_ref, vec_ref, one_ref, two_ref,
    qkv_w_ref, proj_w_ref, vec_out, one_out, two_out,
):
    first = here_ref[1] == 0
    half = D // 2
    for j in range(3):
        rows, cols = slice(j * half, (j + 1) * half), slice(j * D, (j + 1) * D)
        x, x_other = x_ref[rows, :].astype(F32), x_other_ref[rows, :].astype(F32)
        qkv_w_ref[:, cols] = qkv_ref[:, cols] - rate(D, 3 * D) * jnp.where(first, x_other, x)
        if j == 0:
            proj_w_ref[...] = proj_ref[...] - rate(D, D) * jnp.where(first, x, x_other)
    whole = sum_ref[...].astype(F32)
    own = jnp.where(here_ref[0] == 0, whole[:6], whole[6:12])
    one = beta_first * one_ref[...] + (1.0 - beta_first) * own
    two = beta_second * two_ref[...] + (1.0 - beta_second) * own * own
    one_out[...] = one
    two_out[...] = two
    fix_first = 1.0 - beta_first**STEP
    fix_second = 1.0 - beta_second**STEP
    vec_out[...] = vec_ref[...] - adam_rate * (
        one / fix_first / (jnp.sqrt(two / fix_second) + adam_epsilon) + weight_decay * vec_ref[...]
    )


def step_small(here, x, x_other, qkv, proj, vec_sum, vectors, vec_first, vec_second):
    whole = pl.BlockSpec(memory_space=pltpu.VMEM)
    shapes = (qkv.shape, proj.shape) + (vectors.shape,) * 3
    return pl.pallas_call(
        step_small_kernel,
        in_specs=[SCALARS] + [whole] * 8,
        out_specs=[whole] * 5,
        out_shape=[jax.ShapeDtypeStruct(s, F32) for s in shapes],
        compiler_params=pltpu.CompilerParams(vmem_limit_bytes=20 * MIB),
        cost_estimate=cost(4e6, 6e6),
        name="step_small",
    )(here, x, x_other, qkv, proj, vec_sum, vectors, vec_first, vec_second)


def after(value, *others):
    for other in others:
        row = other.reshape(-1, other.shape[-1])[:1, :D].astype(F32) * 0.0
        value = (value.astype(F32) + row).astype(value.dtype)
    return value


class Place:
    def __init__(self):
        self.dp = lax.axis_index("dp")
        self.y = lax.axis_index("fsdp")
        self.bits = [1 << k for k in range(lax.axis_size("dp").bit_length() - 1)]

    def high(self, bit):
        return (self.y if bit == "y" else self.dp & bit) != 0

    def swap(self, value, bit):
        if bit == "y":
            return lax.ppermute(value, "fsdp", [(0, 1), (1, 0)])
        size = lax.axis_size("dp")
        return lax.ppermute(value, "dp", [(i, i ^ bit) for i in range(size)])

    def join(self, mine, theirs, bit, axis):
        return jnp.where(
            self.high(bit),
            jnp.concatenate([theirs, mine], axis),
            jnp.concatenate([mine, theirs], axis),
        )

    def halves(self, value, bit):
        axis = 0 if bit == "y" else 1
        middle = value.shape[axis] // 2
        low = lax.slice_in_dim(value, 0, middle, axis=axis)
        high = lax.slice_in_dim(value, middle, 2 * middle, axis=axis)
        flag = self.high(bit)
        return jnp.where(flag, high, low), jnp.where(flag, low, high)


class Chain:
    def __init__(self, place, grad, order, rider=None):
        self.place, self.value, self.order, self.rider = place, grad, list(order), rider
        self.offset = jnp.int32(0)

    def send(self, k):
        self.keep, out = self.place.halves(self.value, self.order[k])
        if self.rider is None:
            return out
        return jnp.concatenate([out.reshape(-1, D), self.rider], 0)

    def add(self, got, k):
        self.last = got
        if self.rider is not None:
            self.rider = (self.rider.astype(F32) + got[-16:].astype(F32)).astype(BF)
            got = got[:-16].reshape(self.keep.shape)
        self.value = (self.keep.astype(F32) + got.astype(F32)).astype(BF)
        if self.order[k] != "y":
            self.offset = self.offset + jnp.where(
                self.place.high(self.order[k]), self.value.shape[1], 0
            )

    def scatter(self, steps, *waits):
        for k in steps:
            self.add(after(self.place.swap(self.send(k), self.order[k]), *waits), k)

    def decay(self, rows_at):
        own = rows_at(self.offset, self.value.shape[1])
        self.value = (momentum_decay * own[None] + self.value.astype(F32)).astype(BF)

    def gather(self, steps=None, *waits):
        for k in reversed(range(len(self.order))) if steps is None else steps:
            bit = self.order[k]
            self.last = self.place.swap(self.value, bit)
            theirs = after(self.last, *waits)
            self.value = self.place.join(self.value, theirs, bit, 0 if bit == "y" else 1)
        return self.value


def blocked(matrix):
    rows, cols = matrix.shape
    return matrix.reshape(rows, cols // D, D).transpose(1, 0, 2).reshape(-1, D)


def block_rows(matrix, offset, count):
    rows, cols = matrix.shape
    block = jnp.minimum(offset // rows, cols // D - 1)
    return lax.dynamic_slice(matrix, (offset % rows, block * D), (count, D))


def on_device(
    inputs, cotangent, segment_ids,
    qkv_weight, proj_weight, up_weight, down_weight, vectors,
    qkv_moment, proj_moment, up_moment, down_moment, vec_first, vec_second,
):
    place = Place()
    core, across, rest = place.bits[0], place.bits[1], place.bits[2:]
    half = D // 2
    here = jnp.stack([place.y, place.dp % 2]).astype(jnp.int32)
    first_core = place.dp % 2 == 0

    def core_part(value):
        middle = value.shape[0] // 2
        return jnp.where(first_core, value[:middle], value[middle:])

    vec_low = vectors.astype(BF)
    vec_other = place.swap(vec_low, "y")
    vec = place.join(vec_low, vec_other, "y", 0).astype(F32)
    qkv_own = qkv_weight.astype(BF)
    qkv_near = place.swap(core_part(qkv_weight).astype(BF), "y")
    rest_own = jnp.concatenate([down_weight, blocked(up_weight), proj_weight], 0).astype(BF)
    qkv_far = place.swap(qkv_near, core)
    rest_part = after(core_part(rest_own), qkv_near, vec_other)
    qkv_parts = (qkv_own, qkv_near, qkv_far)
    rest_near = place.swap(rest_part, "y")
    qkv, attended, attended_t, weights = attend(here, inputs, qkv_parts, vec, segment_ids)
    rest_near = after(rest_near, attended)
    rest_parts = (rest_own, rest_near, place.swap(rest_near, core))

    layer_out, grad_first, grad_out, keep, send, grad_proj, vec_one = layer(
        here, inputs.reshape(-1, D), attended.reshape(-1, D), cotangent.reshape(-1, D), vec, rest_parts
    )
    got = place.swap(send, core)
    large = (keep.astype(F32) + got.astype(F32)).astype(BF)
    middle = large.shape[1] // 2
    chain_one = Chain(place, large[:, :middle], ["y", across])
    chain_two = Chain(place, large[:, middle:], [across, "y"])
    send_one, send_two = chain_one.send(0), chain_two.send(0)
    grad_out, send_one, send_two = lax.optimization_barrier((grad_out, send_one, send_two))
    chain_one.add(place.swap(send_one, "y"), 0)
    chain_two.add(place.swap(send_two, across), 0)

    grads = attend_pull(qkv, weights, attended_t, grad_out.reshape(inputs.shape))
    input_grad, keep, send, vec_sum = project_pull(
        here, inputs, grads, grad_first.reshape(inputs.shape), qkv_parts, grad_proj,
        after(vec_one, chain_one.last, chain_two.last),
    )
    chain_small = Chain(place, keep, [core, "y", across] + rest, vec_sum)
    chain_small.keep = keep

    chain_one.scatter([1])
    chain_two.scatter([1])
    apart = chain_one.value.shape[1]
    chain_both = Chain(place, jnp.concatenate([chain_one.value, chain_two.value], 1), rest)
    chain_both.value = after(chain_both.value, keep)
    chain_both.scatter(range(len(rest)))

    def large_rows(offset, count):
        offset = jnp.where(offset >= apart, middle - apart, 0) + chain_one.offset + offset
        return jnp.where(
            first_core, block_rows(up_moment, offset, count), block_rows(down_moment, offset, count)
        )

    chain_both.decay(large_rows)
    count = len(rest)
    chain_small.add(after(place.swap(send, core), chain_one.last, chain_two.last), 0)
    chain_small.scatter([1], chain_both.last)
    both = chain_both.gather([count - 1])
    chain_both.value = after(chain_both.value, chain_small.last)
    chain_small.scatter([2], chain_both.last)
    both = chain_both.gather(reversed(range(count - 1)))
    chain_small.scatter(range(3, 2 + count), chain_both.last)
    chain_one.value, chain_two.value = both[:, :apart], both[:, apart:]
    chain_one.gather([1])
    chain_two.gather([1])
    chain_small.scatter([2 + count], chain_one.last, chain_two.last)
    chain_small.decay(
        lambda offset, count: jnp.where(
            offset >= 3 * half,
            block_rows(proj_moment, offset % half, count),
            block_rows(qkv_moment, offset, count),
        )
    )
    chain_small.gather(reversed(range(3, 3 + count)))
    large_whole = jnp.concatenate([chain_one.gather([0]), chain_two.gather([0])], 1)
    chain_small.value = after(chain_small.value, chain_one.last, chain_two.last)
    chain_small.gather([2])
    large_whole = after(large_whole, chain_small.last)
    large_x = orthogonal_large(here, large_whole)
    large_other = place.swap(jnp.where(place.y != 0, large_whole[1], large_whole[0]), core)
    chain_small.gather([1], large_x)
    small_mine = chain_small.value
    small_other = place.swap(small_mine, core)
    (
        small_x, up_moment_new, down_moment_new, up_weight_new, down_weight_new,
        qkv_moment_new, proj_moment_new,
    ) = orthogonal_small(
        here, small_mine, small_other, large_whole, large_other, large_x,
        place.swap(after(large_x, large_other), core),
        up_weight, down_weight,
    )
    qkv_weight_new, proj_weight_new, vectors_new, vec_first_new, vec_second_new = step_small(
        here, small_x, place.swap(small_x, core), qkv_weight, proj_weight,
        chain_small.rider, vectors, vec_first, vec_second,
    )
    return (
        layer_out.reshape(inputs.shape),
        input_grad,
        qkv_moment_new,
        proj_moment_new,
        up_moment_new,
        down_moment_new,
        qkv_weight_new,
        proj_weight_new,
        up_weight_new,
        down_weight_new,
        vec_first_new,
        vec_second_new,
        vectors_new,
    )


def solution(mesh):
    tokens = P(("dp", "fsdp"), None, None)
    rows = P("fsdp", None)
    in_specs = (tokens, tokens, P(("dp", "fsdp"), None)) + (rows,) * 11
    out_specs = (tokens, tokens) + (rows,) * 11
    return jax.shard_map(
        on_device, mesh=mesh, in_specs=in_specs, out_specs=out_specs, check_vma=False
    )
```

```python
import functools
import math

import jax
import jax.numpy as jnp
from jax import lax
from jax.experimental import pallas as pl
from jax.experimental.pallas import tpu as pltpu
from jax.sharding import PartitionSpec as P

D = 512
HEADS = 8
HD = 64
FF = 2048
NS_ITERS = 5
STEP = 10
TILE = 512

norm_epsilon = 1e-12
momentum_decay = 0.95
muon_rate = 0.6
newton_a = 3.4445
newton_b = -4.775
newton_c = 2.0315
beta_first = 0.9
beta_second = 0.999
adam_rate = 0.2
weight_decay = 0.01
adam_epsilon = 1e-08
masked_score = -1e30
softmax_scale = 1.0 / math.sqrt(HD)

BF = jnp.bfloat16
F32 = jnp.float32
MIB = 1024 * 1024


def dot(left, right):
    return jnp.dot(left, right, preferred_element_type=F32)


def against(left, right):
    return lax.dot_general(left, right, (((1,), (1,)), ((), ())), preferred_element_type=F32)


def contract_rows(left, right):
    return lax.dot_general(left, right, (((0,), (0,)), ((), ())), preferred_element_type=F32)


def fixed(shape):
    return pl.BlockSpec(shape, lambda *_: (0,) * len(shape))


SCALARS = pl.BlockSpec(memory_space=pltpu.SMEM)


def compiler_params(mib, grid_rank=1):
    return pltpu.CompilerParams(
        dimension_semantics=("arbitrary",) * grid_rank, vmem_limit_bytes=mib * MIB
    )


def cost(flops, nbytes, trans=0):
    return pl.CostEstimate(flops=int(flops), bytes_accessed=int(nbytes), transcendentals=int(trans))


def place_rows(whole, here_ref, own, near, far):
    y, core = here_ref[0], here_ref[1]
    part = near.shape[0]
    start = lambda k: pl.ds(pl.multiple_of(k * part, part), part)
    whole[y] = own[...]
    whole[1 - y, start(core)] = near[...]
    whole[1 - y, start(1 - core)] = far[...]


def attend_kernel(
    here_ref, x_ref, own_ref, near_ref, far_ref, vec_ref, seg_ref,
    qkv_ref, o_ref, ot_ref, at_ref,
    w_s, qt_s, vt_s,
):
    @pl.when(pl.program_id(0) == 0)
    def _():
        place_rows(w_s, here_ref, own_ref, near_ref, far_ref)

    projected = dot(x_ref[0], w_s[...].reshape(D, 3 * D))
    queries = (projected[:, :D] + vec_ref[0:1, :]).astype(BF)
    keys = projected[:, D : 2 * D].astype(BF)
    values = (projected[:, 2 * D :] + vec_ref[1:2, :]).astype(BF)
    qkv_ref[0, :, :D] = queries
    qkv_ref[0, :, D : 2 * D] = keys
    qkv_ref[0, :, 2 * D :] = values
    qt_s[...] = (queries.astype(F32) * softmax_scale).T.astype(BF)
    vt_s[...] = values.astype(F32).T.astype(BF)
    document = seg_ref[0].astype(F32)
    same = jnp.broadcast_to(document, (8, document.shape[1])).T[:, :1] == document
    for head in range(HEADS):
        rows = slice(head * HD, (head + 1) * HD)
        scores = dot(keys[:, rows], qt_s[rows, :])
        scores = jnp.where(same, scores, masked_score)
        exponent = jnp.exp(scores - jnp.max(scores, 0, keepdims=True))
        weights = (exponent * (1.0 / jnp.sum(exponent, 0, keepdims=True))).astype(BF)
        at_ref[0, head] = weights
        ot_ref[0, rows, :] = dot(vt_s[rows, :], weights).astype(BF)
    o_ref[0] = ot_ref[0].astype(F32).T.astype(BF)


def attend(here, x, qkv_parts, vec, segment_ids):
    count, length = segment_ids.shape
    item = lambda *shape: pl.BlockSpec((1,) + shape, lambda i: (i,) + (0,) * len(shape))
    return pl.pallas_call(
        attend_kernel,
        grid=(count,),
        in_specs=[
            SCALARS, item(length, D), *[fixed(p.shape) for p in qkv_parts], fixed(vec.shape),
            item(1, length),
        ],
        out_specs=[item(length, 3 * D), item(length, D), item(D, length), item(HEADS, length, length)],
        out_shape=[
            jax.ShapeDtypeStruct((count, length, 3 * D), BF),
            jax.ShapeDtypeStruct((count, length, D), BF),
            jax.ShapeDtypeStruct((count, D, length), BF),
            jax.ShapeDtypeStruct((count, HEADS, length, length), BF),
        ],
        scratch_shapes=[
            pltpu.VMEM((2, D // 2, 3 * D), BF),
            pltpu.VMEM((D, length), BF),
            pltpu.VMEM((D, length), BF),
        ],
        compiler_params=compiler_params(36),
        cost_estimate=cost(count * 8e9, 3e7),
        name="attend_forward",
    )(here, x, *qkv_parts, vec, segment_ids[:, None, :])


def normed(values):
    center = values - jnp.mean(values, -1, keepdims=True)
    factor = lax.rsqrt(jnp.mean(center * center, -1, keepdims=True) + norm_epsilon)
    return center * factor, factor


def norm_pull(scaled, unit, factor):
    return factor * (
        scaled
        - jnp.mean(scaled, -1, keepdims=True)
        - unit * jnp.mean(scaled * unit, -1, keepdims=True)
    )


def gelu_and_slope(u):
    cdf = 0.5 + 0.5 * lax.erf(u * math.sqrt(0.5))
    return u * cdf, cdf + u * (jnp.exp(-0.5 * u * u) * (1.0 / math.sqrt(2.0 * math.pi)))


def colsum(values):
    return jnp.sum(values, 0, keepdims=True)


def layer_kernel(
    here_ref, x_ref, o_ref, cot_ref, vec_ref, own_ref, near_ref, far_ref,
    out_ref, dy_ref, do_ref, keep_ref, send_ref, gproj_ref, gvec_ref,
    w_s, acc_d, acc_u, acc_p, e_s, s_s,
):
    step = pl.program_id(0)
    half = D // 2

    @pl.when(step == 0)
    def _():
        place_rows(w_s, here_ref, own_ref, near_ref, far_ref)
        acc_d[...] = jnp.zeros_like(acc_d)
        acc_u[...] = jnp.zeros_like(acc_u)
        acc_p[...] = jnp.zeros_like(acc_p)
        gvec_ref[...] = jnp.zeros_like(gvec_ref)

    def rows_of(start):
        return jnp.concatenate([w_s[0, start : start + half], w_s[1, start : start + half]], 0)

    down_block = lambda j: w_s[j // 2, (j % 2) * D : (j % 2 + 1) * D, :]
    up_block = lambda j: rows_of(FF // 2 + j * half)
    row = lambda i: vec_ref[i : i + 1, :]
    attended = o_ref[...]
    proj = rows_of(FF)
    unit_one, factor_one = normed(x_ref[...].astype(F32) + (dot(attended, proj) + row(2)))
    hidden = unit_one * row(3) + row(4)
    hidden_low = hidden.astype(BF)
    total = jnp.zeros_like(hidden)
    for j in range(FF // D):
        cols = slice(j * D, (j + 1) * D)
        active, slope = gelu_and_slope(dot(hidden_low, up_block(j)) + row(8 + j))
        active = active.astype(BF)
        e_s[:, cols] = active
        s_s[:, cols] = slope
        total += dot(active, down_block(j))
    unit_two, factor_two = normed(hidden + (total + row(5)))
    out_ref[...] = unit_two * row(6) + row(7)
    cot = cot_ref[...].astype(F32)
    gvec_ref[6:7, :] += colsum(cot * unit_two)
    gvec_ref[7:8, :] += colsum(cot)
    grad_second = norm_pull(cot * row(6), unit_two, factor_two)
    grad_low = grad_second.astype(BF)
    gvec_ref[5:6, :] += colsum(grad_low.astype(F32))
    grad_hidden = grad_second
    for j in range(FF // D):
        cols = slice(j * D, (j + 1) * D)
        grad_up = (against(grad_low, down_block(j)) * s_s[:, cols]).astype(BF)
        gvec_ref[8 + j : 9 + j, :] += colsum(grad_up.astype(F32))
        acc_d[cols, :] += contract_rows(e_s[:, cols], grad_low)
        acc_u[:, cols] += contract_rows(hidden_low, grad_up)
        grad_hidden += against(grad_up, up_block(j))
    gvec_ref[3:4, :] += colsum(grad_hidden * unit_one)
    gvec_ref[4:5, :] += colsum(grad_hidden)
    grad_first = norm_pull(grad_hidden * row(3), unit_one, factor_one)
    dy_ref[...] = grad_first
    branch_low = grad_first.astype(BF)
    gvec_ref[2:3, :] += colsum(branch_low.astype(F32))
    acc_p[...] += contract_rows(attended, branch_low)
    do_ref[...] = against(branch_low, proj).astype(BF)

    @pl.when(step == pl.num_programs(0) - 1)
    def _():
        def put(up_ref, down_ref):
            for y in range(2):
                rows = slice(y * half, (y + 1) * half)
                down_ref[y] = acc_d[y * (FF // 2) : (y + 1) * (FF // 2), :].astype(BF)
                for j in range(FF // D):
                    cols = slice(j * D, (j + 1) * D)
                    up_ref[y, j * half : (j + 1) * half, :] = acc_u[rows, cols].astype(BF)

        for y in range(2):
            gproj_ref[y] = acc_p[y * half : (y + 1) * half, :].astype(BF)

        @pl.when(here_ref[1] == 0)
        def _():
            put(keep_ref, send_ref)

        @pl.when(here_ref[1] != 0)
        def _():
            put(send_ref, keep_ref)


def layer(here, x_rows, attended, cot_rows, vec, parts):
    tokens = x_rows.shape[0]
    tile = pl.BlockSpec((TILE, D), lambda i: (i, 0))
    shapes = [
        ((tokens, D), F32), ((tokens, D), F32), ((tokens, D), BF),
        ((2, FF // 2, D), BF), ((2, FF // 2, D), BF), ((2, D // 2, D), BF), ((16, D), F32),
    ]
    return pl.pallas_call(
        layer_kernel,
        grid=(tokens // TILE,),
        in_specs=[SCALARS, tile, tile, tile, fixed(vec.shape)] + [fixed(p.shape) for p in parts],
        out_specs=[tile, tile, tile] + [fixed(s) for s, _ in shapes[3:]],
        out_shape=[jax.ShapeDtypeStruct(s, t) for s, t in shapes],
        scratch_shapes=[
            pltpu.VMEM((2,) + parts[0].shape, BF),
            pltpu.VMEM((FF, D), F32),
            pltpu.VMEM((D, FF), F32),
            pltpu.VMEM((D, D), F32),
            pltpu.VMEM((TILE, FF), BF),
            pltpu.VMEM((TILE, FF), F32),
        ],
        compiler_params=compiler_params(41),
        cost_estimate=cost(tokens * 3e7, 2e7),
        name="layer_both_ways",
    )(here, x_rows, attended, cot_rows, vec, *parts)


def attend_pull_kernel(q_ref, k_ref, v_ref, at_ref, ot_ref, do_ref, dq_ref, dk_ref, dv_ref, dqt_s):
    grad_out_t = do_ref[0].astype(F32).T.astype(BF)
    keys_t = k_ref[0].astype(F32).T.astype(BF)
    for head in range(2):
        rows = slice(head * HD, (head + 1) * HD)
        grad_out = grad_out_t[rows, :]
        delta = colsum(grad_out.astype(F32) * ot_ref[0, rows, :].astype(F32))
        weights = at_ref[0, head]
        grad_probs = dot(v_ref[0, :, rows], grad_out)
        grad_scores = (weights.astype(F32) * (grad_probs - delta)).astype(BF)
        dv_ref[0, :, rows] = dot(weights, do_ref[0, :, rows]).astype(BF)
        dk_ref[0, :, rows] = (dot(grad_scores, q_ref[0, :, rows]) * softmax_scale).astype(BF)
        dqt_s[rows, :] = dot(keys_t[rows, :], grad_scores) * softmax_scale
    dq_ref[0] = dqt_s[...].T.astype(BF)


def attend_pull(qkv, weights, attended_t, grad_out):
    count, length, _ = qkv.shape
    pairs, wide = HEADS // 2, 2 * HD
    third = lambda k: pl.BlockSpec((1, length, wide), lambda i, p: (i, 0, k * pairs + p))
    return pl.pallas_call(
        attend_pull_kernel,
        grid=(count, pairs),
        in_specs=[
            third(0), third(1), third(2),
            pl.BlockSpec((1, 2, length, length), lambda i, p: (i, p, 0, 0)),
            pl.BlockSpec((1, wide, length), lambda i, p: (i, p, 0)),
            third(0),
        ],
        out_specs=[third(0)] * 3,
        out_shape=[jax.ShapeDtypeStruct((count, length, D), BF)] * 3,
        scratch_shapes=[pltpu.VMEM((wide, length), F32)],
        compiler_params=compiler_params(56, 2),
        cost_estimate=cost(count * 6e9, 2e7),
        name="attend_backward",
    )(qkv, qkv, qkv, weights, attended_t, grad_out)


def project_pull_kernel(
    here_ref, x_ref, dq_ref, dk_ref, dv_ref, dy_ref, own_ref, near_ref, far_ref, gproj_ref, vec_one_ref,
    gx_ref, keep_ref, send_ref, vec_out_ref,
    w_s, gvec_ref, acc,
):
    step = pl.program_id(0)

    @pl.when(step == 0)
    def _():
        place_rows(w_s, here_ref, own_ref, near_ref, far_ref)
        acc[...] = jnp.zeros_like(acc)
        gvec_ref[...] = vec_one_ref[...]

    gvec_ref[0:1, :] += colsum(dq_ref[0].astype(F32))
    gvec_ref[1:2, :] += colsum(dv_ref[0].astype(F32))
    total = dy_ref[0]
    for k, grad_ref_k in enumerate((dq_ref, dk_ref, dv_ref)):
        cols = slice(k * D, (k + 1) * D)
        grad = grad_ref_k[0]
        acc[:, cols] += contract_rows(x_ref[0], grad)
        total += against(grad, w_s[:, :, cols].reshape(D, D))
    gx_ref[0] = total

    @pl.when(step == pl.num_programs(0) - 1)
    def _():
        half = D // 2
        vec_low = gvec_ref[...].astype(BF)
        vec_out_ref[...] = vec_low
        send_ref[4 * half :, :] = vec_low

        def block(y, j):
            if j == 3:
                return gproj_ref[y]
            return acc[y * half : (y + 1) * half, j * D : (j + 1) * D].astype(BF)

        for core in range(2):

            @pl.when(here_ref[1] == core)
            def _():
                for y in range(2):
                    for j in range(2):
                        rows = slice((2 * y + j) * half, (2 * y + j + 1) * half)
                        keep_ref[y, j * half : (j + 1) * half, :] = block(y, 2 * core + j)
                        send_ref[rows, :] = block(y, 2 - 2 * core + j)


def project_pull(here, x, grads, grad_first, qkv_parts, grad_proj, vec_one):
    count, length, _ = x.shape
    item = pl.BlockSpec((1, length, D), lambda i: (i, 0, 0))
    return pl.pallas_call(
        project_pull_kernel,
        grid=(count,),
        in_specs=[SCALARS, item, item, item, item, item]
        + [fixed(p.shape) for p in qkv_parts]
        + [fixed((2, D // 2, D)), fixed((16, D))],
        out_specs=[item, fixed((2, D, D)), fixed((2 * D + 16, D)), fixed((16, D))],
        out_shape=[
            jax.ShapeDtypeStruct((count, length, D), F32),
            jax.ShapeDtypeStruct((2, D, D), BF),
            jax.ShapeDtypeStruct((2 * D + 16, D), BF),
            jax.ShapeDtypeStruct((16, D), BF),
        ],
        scratch_shapes=[
            pltpu.VMEM((2, D // 2, 3 * D), BF),
            pltpu.VMEM((16, D), F32),
            pltpu.VMEM((D, 3 * D), F32),
        ],
        compiler_params=compiler_params(36),
        cost_estimate=cost(count * 4e9, 1.5e7),
        name="project_backward",
    )(here, x, *grads, grad_first, *qkv_parts, grad_proj, vec_one)


def column_blocks(cols):
    return [slice(start, start + D) for start in range(0, cols, D)]


def normalize(cols, work, low):
    squares = sum(colsum(work[:, block] * work[:, block]) for block in column_blocks(cols))
    scale = 1.0 / (jnp.sqrt(jnp.sum(squares)) + 1e-07)
    for block in column_blocks(cols):
        made = work[:, block] * scale
        work[:, block] = made
        low[:, block] = made.astype(BF)


def iterate(cols, work, low):
    eye = lax.broadcasted_iota(jnp.int32, (D, D), 0) == lax.broadcasted_iota(jnp.int32, (D, D), 1)
    gram = against(low[:, :cols], low[:, :cols])
    own = jnp.where(eye, gram, 0.0)
    down = jnp.sum(own, 1, keepdims=True)
    across = jnp.sum(own, 0, keepdims=True)
    rest = jnp.where(eye, 0.0, gram)
    rest_low = rest.astype(BF)
    square = dot(rest_low, rest_low)
    poly = rest * (newton_b + newton_c * (down + across)) + newton_c * square
    poly = jnp.where(eye, 0.0, poly).astype(BF)
    square_own = jnp.sum(jnp.where(eye, square, 0.0), 1, keepdims=True)
    factor = newton_a + newton_b * down + newton_c * (down * down + square_own)
    for block in column_blocks(cols):
        made = factor * work[:, block] + dot(poly, low[:, block])
        work[:, block] = made
        low[:, block] = made.astype(BF)


def load_blocks(work, blocks):
    half = D // 2
    for k, (ref, j) in enumerate(blocks):
        for y in range(2):
            rows = slice(y * half, (y + 1) * half)
            work[rows, k * D : (k + 1) * D] = ref[y, j * half : (j + 1) * half, :].astype(F32)


def store_blocks(y, out_ref, low, count):
    half = D // 2
    rows = pl.ds(pl.multiple_of(y * half, half), half)
    for k in range(count):
        out_ref[k * half : (k + 1) * half, :] = low[rows, k * D : (k + 1) * D]


def large_kernel(here_ref, m_ref, out_ref, work, low):
    y, core = here_ref[0], here_ref[1]
    blocks = FF // D

    @pl.when(core == 0)
    def _():
        load_blocks(work, [(m_ref, j) for j in range(blocks)])

    @pl.when(core != 0)
    def _():
        for j in range(blocks):
            rows = slice((j % 2) * D, (j % 2 + 1) * D)
            work[:, j * D : (j + 1) * D] = m_ref[j // 2, rows, :].astype(F32).T

    normalize(FF, work, low)

    @pl.loop(0, NS_ITERS)
    def _(_):
        iterate(FF, work, low)

    @pl.when(core == 0)
    def _():
        store_blocks(y, out_ref, low, blocks)

    for k in range(2):

        @pl.when((core != 0) & (y == k))
        def _():
            for j in range(blocks // 2):
                cols = slice((k * blocks // 2 + j) * D, (k * blocks // 2 + j + 1) * D)
                out_ref[j * D : (j + 1) * D, :] = work[:, cols].T.astype(BF)


def orthogonal_large(here, moment):
    blocks = FF // D
    return pl.pallas_call(
        large_kernel,
        in_specs=[SCALARS, pl.BlockSpec(memory_space=pltpu.VMEM)],
        out_specs=pl.BlockSpec(memory_space=pltpu.VMEM),
        out_shape=jax.ShapeDtypeStruct((FF // 2, D), BF),
        scratch_shapes=[pltpu.VMEM((D, FF), F32), pltpu.VMEM((D, FF), BF)],
        compiler_params=pltpu.CompilerParams(vmem_limit_bytes=32 * MIB),
        cost_estimate=cost(NS_ITERS * (4.0 * blocks + 2.0) * D * D * D, 4e6),
        name="newton_schulz_large",
    )(here, moment)


def rate(rows, cols):
    return muon_rate * math.sqrt(max(rows, cols) / rows)


def small_kernel(
    here_ref, mine_ref, other_ref, large_m, large_m_other, large_x, large_x_other, up_w, down_w,
    out_ref, up_m_new, down_m_new, up_w_new, down_w_new, qkv_m_new, proj_m_new,
    work, low, m_s, m_other_s, x_s, x_other_s, up_w_s, down_w_s,
    up_m_s, down_m_s, qkv_m_s, proj_m_s, in_sems, out_sems,
):
    half = D // 2
    y, core = here_ref[0], here_ref[1]
    first = core == 0
    arrivals = [
        pltpu.make_async_copy(source, target, in_sems.at[k])
        for k, (source, target) in enumerate(
            [
                (large_m.at[y], m_s), (large_m_other, m_other_s), (large_x, x_s),
                (large_x_other, x_other_s), (up_w, up_w_s), (down_w, down_w_s),
            ]
        )
    ]
    results = [
        pltpu.make_async_copy(source, target, out_sems.at[k])
        for k, (source, target) in enumerate(
            [
                (up_m_s, up_m_new), (down_m_s, down_m_new), (up_w_s, up_w_new),
                (down_w_s, down_w_new), (qkv_m_s, qkv_m_new), (proj_m_s, proj_m_new),
            ]
        )
    ]
    for copy in arrivals:
        copy.start()

    @pl.when(first)
    def _():
        load_blocks(work, [(other_ref, 1)])
        normalize(D, work, low)

    @pl.when(core != 0)
    def _():
        load_blocks(work, [(other_ref, 0), (other_ref, 1), (mine_ref, 0)])
        normalize(3 * D, work, low)

    @pl.loop(0, NS_ITERS)
    def _(step):
        @pl.when(first)
        def _():
            iterate(D, work, low)

        @pl.when(core != 0)
        def _():
            iterate(3 * D, work, low)

        @pl.when(step == 1)
        def _():
            for copy in arrivals:
                copy.wait()
            for j in range(FF // D):
                rows, cols = slice(j * half, (j + 1) * half), slice(j * D, (j + 1) * D)
                m, m_other = m_s[rows, :].astype(F32), m_other_s[rows, :].astype(F32)
                x, x_other = x_s[rows, :].astype(F32), x_other_s[rows, :].astype(F32)
                up_m_s[:, cols] = jnp.where(first, m, m_other)
                down_m_s[rows, :] = jnp.where(first, m_other, m)
                up_w_s[:, cols] -= rate(D, FF) * jnp.where(first, x, x_other)
                down_w_s[rows, :] -= rate(FF, D) * jnp.where(first, x_other, x)
                part = slice(j % 2 * half, (j % 2 + 1) * half)
                mine, other = mine_ref[y, part, :].astype(F32), other_ref[y, part, :].astype(F32)
                own = jnp.where(first == (j < 2), mine, other)
                if j < 3:
                    qkv_m_s[:, cols] = own
                else:
                    proj_m_s[...] = own
            for copy in results:
                copy.start()

    @pl.when(first)
    def _():
        out_ref[...] = jnp.zeros_like(out_ref)
        store_blocks(y, out_ref, low, 1)

    @pl.when(core != 0)
    def _():
        store_blocks(y, out_ref, low, 3)

    for copy in results:
        copy.wait()


def orthogonal_small(here, mine, other, large_whole, m_other, x, x_other, up, down):
    half = D // 2
    spaces = lambda kind, count: [pl.BlockSpec(memory_space=kind)] * count
    large = pltpu.VMEM((FF // 2, D), BF)
    shapes = [up.shape, down.shape, up.shape, down.shape, (half, 3 * D), (half, D)]
    return pl.pallas_call(
        small_kernel,
        in_specs=[SCALARS] + spaces(pltpu.VMEM, 2) + spaces(pl.ANY, 6),
        out_specs=spaces(pltpu.VMEM, 1) + spaces(pl.ANY, 6),
        out_shape=[jax.ShapeDtypeStruct((3 * half, D), BF)]
        + [jax.ShapeDtypeStruct(shape, F32) for shape in shapes],
        scratch_shapes=[
            pltpu.VMEM((D, 3 * D), F32), pltpu.VMEM((D, 3 * D), BF),
            large, large, large, large, pltpu.VMEM(up.shape, F32), pltpu.VMEM(down.shape, F32),
            pltpu.VMEM(up.shape, F32), pltpu.VMEM(down.shape, F32),
            pltpu.VMEM((half, 3 * D), F32), pltpu.VMEM((half, D), F32),
            pltpu.SemaphoreType.DMA((6,)), pltpu.SemaphoreType.DMA((6,)),
        ],
        compiler_params=pltpu.CompilerParams(vmem_limit_bytes=44 * MIB),
        cost_estimate=cost(NS_ITERS * 14.0 * D * D * D, 4e6),
        name="newton_schulz_small",
    )(here, mine, other, large_whole, m_other, x, x_other, up, down)


def step_small_kernel(
    here_ref, x_ref, x_other_ref, qkv_ref, proj_ref, sum_ref, vec_ref, one_ref, two_ref,
    qkv_w_ref, proj_w_ref, vec_out, one_out, two_out,
):
    first = here_ref[1] == 0
    half = D // 2
    for j in range(3):
        rows, cols = slice(j * half, (j + 1) * half), slice(j * D, (j + 1) * D)
        x, x_other = x_ref[rows, :].astype(F32), x_other_ref[rows, :].astype(F32)
        qkv_w_ref[:, cols] = qkv_ref[:, cols] - rate(D, 3 * D) * jnp.where(first, x_other, x)
        if j == 0:
            proj_w_ref[...] = proj_ref[...] - rate(D, D) * jnp.where(first, x, x_other)
    whole = sum_ref[...].astype(F32)
    own = jnp.where(here_ref[0] == 0, whole[:6], whole[6:12])
    one = beta_first * one_ref[...] + (1.0 - beta_first) * own
    two = beta_second * two_ref[...] + (1.0 - beta_second) * own * own
    one_out[...] = one
    two_out[...] = two
    fix_first = 1.0 - beta_first**STEP
    fix_second = 1.0 - beta_second**STEP
    vec_out[...] = vec_ref[...] - adam_rate * (
        one / fix_first / (jnp.sqrt(two / fix_second) + adam_epsilon) + weight_decay * vec_ref[...]
    )


def step_small(here, x, x_other, qkv, proj, vec_sum, vectors, vec_first, vec_second):
    whole = pl.BlockSpec(memory_space=pltpu.VMEM)
    shapes = (qkv.shape, proj.shape) + (vectors.shape,) * 3
    return pl.pallas_call(
        step_small_kernel,
        in_specs=[SCALARS] + [whole] * 8,
        out_specs=[whole] * 5,
        out_shape=[jax.ShapeDtypeStruct(s, F32) for s in shapes],
        compiler_params=pltpu.CompilerParams(vmem_limit_bytes=20 * MIB),
        cost_estimate=cost(4e6, 6e6),
        name="step_small",
    )(here, x, x_other, qkv, proj, vec_sum, vectors, vec_first, vec_second)


def after(value, *others):
    for other in others:
        row = other.reshape(-1, other.shape[-1])[:1, :D].astype(F32) * 0.0
        value = (value.astype(F32) + row).astype(value.dtype)
    return value


class Place:
    def __init__(self):
        self.dp = lax.axis_index("dp")
        self.y = lax.axis_index("fsdp")
        self.bits = [1 << k for k in range(lax.axis_size("dp").bit_length() - 1)]

    def high(self, bit):
        return (self.y if bit == "y" else self.dp & bit) != 0

    def swap(self, value, bit):
        if bit == "y":
            return lax.ppermute(value, "fsdp", [(0, 1), (1, 0)])
        size = lax.axis_size("dp")
        return lax.ppermute(value, "dp", [(i, i ^ bit) for i in range(size)])

    def join(self, mine, theirs, bit, axis):
        return jnp.where(
            self.high(bit),
            jnp.concatenate([theirs, mine], axis),
            jnp.concatenate([mine, theirs], axis),
        )

    def halves(self, value, bit):
        axis = 0 if bit == "y" else 1
        middle = value.shape[axis] // 2
        low = lax.slice_in_dim(value, 0, middle, axis=axis)
        high = lax.slice_in_dim(value, middle, 2 * middle, axis=axis)
        flag = self.high(bit)
        return jnp.where(flag, high, low), jnp.where(flag, low, high)


class Chain:
    def __init__(self, place, grad, order, rider=None):
        self.place, self.value, self.order, self.rider = place, grad, list(order), rider
        self.offset = jnp.int32(0)

    def send(self, k):
        self.keep, out = self.place.halves(self.value, self.order[k])
        if self.rider is None:
            return out
        return jnp.concatenate([out.reshape(-1, D), self.rider], 0)

    def add(self, got, k):
        self.last = got
        if self.rider is not None:
            self.rider = (self.rider.astype(F32) + got[-16:].astype(F32)).astype(BF)
            got = got[:-16].reshape(self.keep.shape)
        self.value = (self.keep.astype(F32) + got.astype(F32)).astype(BF)
        if self.order[k] != "y":
            self.offset = self.offset + jnp.where(
                self.place.high(self.order[k]), self.value.shape[1], 0
            )

    def scatter(self, steps, *waits):
        for k in steps:
            self.add(after(self.place.swap(self.send(k), self.order[k]), *waits), k)

    def decay(self, rows_at):
        own = rows_at(self.offset, self.value.shape[1])
        self.value = (momentum_decay * own[None] + self.value.astype(F32)).astype(BF)

    def gather(self, steps=None, *waits):
        for k in reversed(range(len(self.order))) if steps is None else steps:
            bit = self.order[k]
            self.last = self.place.swap(self.value, bit)
            theirs = after(self.last, *waits)
            self.value = self.place.join(self.value, theirs, bit, 0 if bit == "y" else 1)
        return self.value


def blocked(matrix):
    rows, cols = matrix.shape
    return matrix.reshape(rows, cols // D, D).transpose(1, 0, 2).reshape(-1, D)


def block_rows(matrix, offset, count):
    rows, cols = matrix.shape
    block = jnp.minimum(offset // rows, cols // D - 1)
    return lax.dynamic_slice(matrix, (offset % rows, block * D), (count, D))


def on_device(
    inputs, cotangent, segment_ids,
    qkv_weight, proj_weight, up_weight, down_weight, vectors,
    qkv_moment, proj_moment, up_moment, down_moment, vec_first, vec_second,
):
    place = Place()
    core, across, rest = place.bits[0], place.bits[1], place.bits[2:]
    half = D // 2
    here = jnp.stack([place.y, place.dp % 2]).astype(jnp.int32)
    first_core = place.dp % 2 == 0

    def core_part(value):
        middle = value.shape[0] // 2
        return jnp.where(first_core, value[:middle], value[middle:])

    vec_low = vectors.astype(BF)
    vec_other = place.swap(vec_low, "y")
    vec = place.join(vec_low, vec_other, "y", 0).astype(F32)
    qkv_own = qkv_weight.astype(BF)
    qkv_near = place.swap(core_part(qkv_weight).astype(BF), "y")
    rest_own = jnp.concatenate([down_weight, blocked(up_weight), proj_weight], 0).astype(BF)
    qkv_far = place.swap(qkv_near, core)
    rest_part = after(core_part(rest_own), qkv_near, vec_other)
    qkv_parts = (qkv_own, qkv_near, qkv_far)
    rest_near = place.swap(rest_part, "y")
    qkv, attended, attended_t, weights = attend(here, inputs, qkv_parts, vec, segment_ids)
    rest_near = after(rest_near, attended)
    rest_parts = (rest_own, rest_near, place.swap(rest_near, core))

    layer_out, grad_first, grad_out, keep, send, grad_proj, vec_one = layer(
        here, inputs.reshape(-1, D), attended.reshape(-1, D), cotangent.reshape(-1, D), vec, rest_parts
    )
    got = place.swap(send, core)
    large = (keep.astype(F32) + got.astype(F32)).astype(BF)
    middle = large.shape[1] // 2
    chain_one = Chain(place, large[:, :middle], ["y", across])
    chain_two = Chain(place, large[:, middle:], [across, "y"])
    send_one, send_two = chain_one.send(0), chain_two.send(0)
    grad_out, send_one, send_two = lax.optimization_barrier((grad_out, send_one, send_two))
    chain_one.add(place.swap(send_one, "y"), 0)
    chain_two.add(place.swap(send_two, across), 0)

    grads = attend_pull(qkv, weights, attended_t, grad_out.reshape(inputs.shape))
    input_grad, keep, send, vec_sum = project_pull(
        here, inputs, grads, grad_first.reshape(inputs.shape), qkv_parts, grad_proj,
        after(vec_one, chain_one.last, chain_two.last),
    )
    chain_small = Chain(place, keep, [core, "y", across] + rest, vec_sum)
    chain_small.keep = keep

    chain_one.scatter([1])
    chain_two.scatter([1])
    apart = chain_one.value.shape[1]
    chain_both = Chain(place, jnp.concatenate([chain_one.value, chain_two.value], 1), rest)
    chain_both.value = after(chain_both.value, keep)
    chain_both.scatter(range(len(rest)))

    def large_rows(offset, count):
        offset = jnp.where(offset >= apart, middle - apart, 0) + chain_one.offset + offset
        return jnp.where(
            first_core, block_rows(up_moment, offset, count), block_rows(down_moment, offset, count)
        )

    chain_both.decay(large_rows)
    count = len(rest)
    chain_small.add(after(place.swap(send, core), chain_one.last, chain_two.last), 0)
    chain_small.scatter([1])
    both = chain_both.gather([count - 1])
    chain_both.value = after(chain_both.value, chain_small.last)
    chain_small.scatter([2])
    both = chain_both.gather(reversed(range(count - 1)))
    chain_small.scatter(range(3, 2 + count), chain_both.last)
    chain_one.value, chain_two.value = both[:, :apart], both[:, apart:]
    chain_one.gather([1])
    chain_two.gather([1])
    chain_small.scatter([2 + count], chain_one.last, chain_two.last)
    chain_small.decay(
        lambda offset, count: jnp.where(
            offset >= 3 * half,
            block_rows(proj_moment, offset % half, count),
            block_rows(qkv_moment, offset, count),
        )
    )
    chain_small.gather(reversed(range(3, 3 + count)))
    large_whole = jnp.concatenate([chain_one.gather([0]), chain_two.gather([0])], 1)
    chain_small.value = after(chain_small.value, chain_one.last, chain_two.last)
    chain_small.gather([2])
    large_whole = after(large_whole, chain_small.last)
    large_x = orthogonal_large(here, large_whole)
    large_other = place.swap(jnp.where(place.y != 0, large_whole[1], large_whole[0]), core)
    chain_small.gather([1], large_x)
    small_mine = chain_small.value
    small_other = place.swap(small_mine, core)
    (
        small_x, up_moment_new, down_moment_new, up_weight_new, down_weight_new,
        qkv_moment_new, proj_moment_new,
    ) = orthogonal_small(
        here, small_mine, small_other, large_whole, large_other, large_x,
        place.swap(after(large_x, large_other), core),
        up_weight, down_weight,
    )
    qkv_weight_new, proj_weight_new, vectors_new, vec_first_new, vec_second_new = step_small(
        here, small_x, place.swap(small_x, core), qkv_weight, proj_weight,
        chain_small.rider, vectors, vec_first, vec_second,
    )
    return (
        layer_out.reshape(inputs.shape),
        input_grad,
        qkv_moment_new,
        proj_moment_new,
        up_moment_new,
        down_moment_new,
        qkv_weight_new,
        proj_weight_new,
        up_weight_new,
        down_weight_new,
        vec_first_new,
        vec_second_new,
        vectors_new,
    )


def solution(mesh):
    tokens = P(("dp", "fsdp"), None, None)
    rows = P("fsdp", None)
    in_specs = (tokens, tokens, P(("dp", "fsdp"), None)) + (rows,) * 11
    out_specs = (tokens, tokens) + (rows,) * 11
    return jax.shard_map(
        on_device, mesh=mesh, in_specs=in_specs, out_specs=out_specs, check_vma=False
    )
```
